32 devices in a mesh: groups: 2 (over y), item: 4 (over z), dp: 2 (over core), tensor: 2 (over x).
Axes of the slice: x: 2, y: 2, z: 4, core: 2. Of those that a mesh axis runs over, the one named last changes fastest.
Arguments:
- events: bfloat16 [12288, 1024], P(('groups', 'item', 'dp')), parts along dimension 0, may hold values from -6 to 6
- lengths: int32 [16], P('groups'), parts along dimension 0, may hold values from 192 to 768, as said below
- packing: int32 [16], P('groups'), parts along dimension 0, may hold values from 0 to 7, each once
- positions: int32 [16, 64], P('groups'), parts along dimension 0, may hold values from 0 to 767, as said below
- logged: int32 [16, 64], P('groups'), parts along dimension 0, may hold values from 0 to 16383
- w_uvqk: bfloat16 [1024, 1024], P(None, 'tensor'), may hold values from -0.1875 to 0.1875
- w_out: bfloat16 [256, 1024], P('tensor'), may hold values from -0.375 to 0.375
- catalogue: bfloat16 [16384, 1024], P(('item', 'dp', 'tensor')), may hold values from -0.46875 to 0.46875
Outputs:
- scoring_state: bfloat16 [1024, 1024], P(('groups', 'item', 'dp'), 'tensor'), parts along dimension 0
- log_propensity: float32 [1024], P(('groups', 'item', 'dp')), parts along dimension 0
The draws below stay inside these ranges and needn't reach their ends.
There are 2 independent parts, one for each index of `groups`. The reference program is written for one: setup_inputs(seed, part) draws one part's arguments, and reference() takes and returns one part's arrays. A program takes and returns all parts, laid end to end along the dimension named above; an argument that names none is the same for every part. Nothing has to cross between parts.
Inputs may be any that keep to these rules, and one draw needn't show every extreme that they name: `lengths`: one history has exactly 768 valid events and one exactly 192. positions[h, k] < lengths[h]. `packing`: each history id appears once.
All inputs are finite; a program needn't handle non-finite values.
Results may differ from the reference program's by a relative error of at most 0.0048.
Values may be sent and summed in bfloat16 or wider, within the bound.
No kernel may reach another device: no remote copies, remote signals or barrier semaphores. Data moves between devices by JAX's collectives and lax.ppermute only.
A program may use at most 64 MiB of HBM per device.

```python
import math
import jax
import jax.numpy as jnp
import numpy as np
from jax import lax

D = 1024
DH = 128
SLOT = 768
IMP_DEV = 64
ITEM_DEV = 1024
HEADS = 2
NHIST = 8
ITEMS = 16384
N_TENSOR = 2


def lengths_of(key):
    drawn = jax.random.randint(jax.random.fold_in(key, 11), (NHIST,), SLOT // 4, SLOT + 1)
    longest = jax.random.randint(jax.random.fold_in(key, 12), (), 0, NHIST)
    hist_index = jnp.arange(NHIST)
    drawn = jnp.where(hist_index == longest, SLOT, drawn)
    drawn = jnp.where(hist_index == (longest + 1) % NHIST, SLOT // 4, drawn)
    return (drawn.astype(jnp.int32), longest)


def draw_lengths(key, part):
    return lengths_of(key)[0]


def draw_positions(key, part):
    hist_lengths, longest = lengths_of(key)
    event_spots = jax.random.randint(jax.random.fold_in(key, 13), (NHIST, IMP_DEV), 0, hist_lengths[:, None])
    row_index = jnp.arange(NHIST)[:, None]
    col_index = jnp.arange(IMP_DEV)[None, :]
    event_spots = jnp.where((row_index == longest) & (col_index == 0), SLOT - 1, event_spots)
    event_spots = jnp.where((row_index == longest) & (col_index == 1), 0, event_spots)
    return event_spots.astype(jnp.int32)


def draw_events(key, part):
    shape = (NHIST * SLOT, D)
    values = jnp.clip(jax.random.normal(jax.random.fold_in(key, 22), shape, jnp.float32), -6.0, 6.0)
    return values.astype(jnp.bfloat16)


def draw_catalogue(key, part):
    shape = (ITEMS, D)
    scale = 1.0 / D ** 0.5
    values = jnp.clip(jax.random.normal(jax.random.fold_in(key, 32), shape, jnp.float32) * 2.5, -15.0, 15.0) * scale
    return values.astype(jnp.bfloat16)


def set_ends(entries, stream_key, smallest, largest):
    place = [jax.random.randint(jax.random.fold_in(stream_key, axis), (), 0, length) for axis, length in enumerate(entries.shape)]
    widest = entries.shape.index(max(entries.shape))
    neighbour = place[:widest] + [(place[widest] + 1) % entries.shape[widest]] + place[widest + 1:]
    return entries.at[tuple(place)].set(smallest).at[tuple(neighbour)].set(largest)


def block_levels(rng, extent, shards, least, largest):
    def one(axis_at, shards_of):
        heights = jax.random.uniform(jax.random.fold_in(jax.random.fold_in(rng, 6), axis_at), (shards_of,), jnp.float32, least / len(shards), largest / len(shards))
        return jnp.repeat(jnp.exp(heights), extent[axis_at] // shards_of).reshape((-1,) + (1,) * (len(extent) - axis_at - 1))

    gain = one(*shards[0])
    for cut in shards[1:]:
        gain = gain * one(*cut)
    return gain


def rank_bounds(number_of, lean):
    portions = [(1 << 20) // math.isqrt(grade ** lean) + 1 for grade in range(1, number_of + 1)]
    spread = 1 + sum(portions) // (1 << 30)
    return np.cumsum(np.array([max(1, weight // spread) for weight in portions]))


def skewed_ids(key, extent, amount, skew):
    listing = rank_bounds(amount, skew)
    ticket = jax.random.randint(jax.random.fold_in(key, 1), extent, 0, int(listing[amount - 1]))
    grade = jnp.searchsorted(jnp.asarray(listing, jnp.int32), ticket, side="right")
    return jax.random.permutation(jax.random.fold_in(key, 2), amount)[grade].astype(jnp.int32)


def noise(key, shape, deviation, reach, split=(), held_as=jnp.bfloat16):
    gain = block_levels(key, shape, split, -0.22, 0.18) if split else 1.0
    values = jax.random.normal(key, shape, jnp.float32) * deviation * gain
    return jnp.minimum(jnp.maximum(values, -reach), reach).astype(held_as)


def setup_inputs(seed: int = 0, part: int = 0) -> dict:
    seeds = jax.random.split(jax.random.key(seed), 9)
    part_splits = jax.random.split(jax.random.fold_in(seeds[8], part), 9)
    return {
        "events": draw_events(jax.random.fold_in(jax.random.fold_in(seeds[8], part), 71), part),
        "lengths": draw_lengths(jax.random.fold_in(jax.random.fold_in(seeds[8], part), 71), part),
        "packing": jax.random.permutation(part_splits[2], NHIST).astype(jnp.int32),
        "positions": draw_positions(jax.random.fold_in(jax.random.fold_in(seeds[8], part), 71), part),
        "logged": set_ends(skewed_ids(part_splits[4], (NHIST, IMP_DEV), ITEMS, 2), jax.random.fold_in(part_splits[4], 3), 0, ITEMS - 1).astype(jnp.int32),
        "w_uvqk": noise(seeds[5], (D, HEADS * 4 * DH), D ** -0.5, 0.1875, ((1, 2),)),
        "w_out": noise(seeds[6], (HEADS * DH, D), (HEADS * DH) ** -0.5, 0.375, ((0, 2),)),
        "catalogue": draw_catalogue(jax.random.fold_in(seeds[8], 71), part),
    }


def score_slot(slot_events, hist_length, event_spots, w_uvqk, w_out):
    projected = jnp.dot(slot_events, w_uvqk, preferred_element_type=jnp.float32)
    projected = jax.nn.silu(projected).astype(jnp.bfloat16).reshape(SLOT, HEADS, 4, DH)
    chosen_proj = jnp.take(projected, event_spots, axis=0).astype(jnp.float32)
    keys_values = projected.astype(jnp.float32)
    scores = jnp.einsum('ied,med->iem', chosen_proj[:, :, 2], keys_values[:, :, 3]) / math.sqrt(DH)
    slot_range = jnp.arange(SLOT).astype(jnp.int32)
    is_valid = (slot_range[None, :] <= event_spots[:, None]) & (slot_range[None, :] < hist_length)
    weights = jnp.where(is_valid[:, None, :], jax.nn.silu(scores), 0.0).astype(jnp.bfloat16)
    attended = jnp.einsum('iem,med->ied', weights.astype(jnp.float32), keys_values[:, :, 1])
    inverse = lax.rsqrt(lax.optimization_barrier(jnp.mean(attended * attended, axis=-1, keepdims=True)) + 1e-06)
    gated_rows = (attended * inverse * chosen_proj[:, :, 0]).astype(jnp.bfloat16)
    gated_rows = gated_rows.reshape(IMP_DEV, HEADS * DH)
    mixed = jnp.dot(gated_rows, w_out, preferred_element_type=jnp.float32)
    mixed = mixed + jnp.take(slot_events, event_spots, axis=0).astype(jnp.float32)
    return mixed.astype(jnp.bfloat16)

def reference(events, lengths, packing, positions, logged, w_uvqk, w_out, catalogue):
    slot_lengths = jnp.take(lengths, packing)
    slot_spots = jnp.take(positions, packing, axis=0)
    slot_items = jnp.take(logged, packing, axis=0).reshape(NHIST * IMP_DEV)
    grouped = events.reshape(NHIST, SLOT, D)

    def one_slot(inputs):
        return score_slot(inputs[0], inputs[1], inputs[2], w_uvqk, w_out)
    states = lax.map(one_slot, (grouped, slot_lengths, slot_spots)).reshape(NHIST * IMP_DEV, D)
    block_size = ITEM_DEV * N_TENSOR
    block_count = ITEMS // block_size
    blocks = catalogue.reshape(block_count, block_size, D)
    bases = (jnp.arange(block_count) * block_size).astype(jnp.int32)
    state_values = states.astype(jnp.float32)

    def step(running, inputs):
        block, item_base = inputs
        logits = jnp.dot(state_values, block.astype(jnp.float32).T, precision=lax.Precision.HIGHEST)
        local_ids = slot_items - item_base
        inside = (local_ids >= 0) & (local_ids < block_size)
        clipped = jnp.clip(local_ids, 0, block_size - 1).astype(jnp.int32)
        picked = jnp.take_along_axis(logits, clipped[:, None], axis=1)[:, 0]
        new_totals = running[0] + lax.optimization_barrier(jnp.sum(jnp.exp(logits), axis=1))
        new_target = running[1] + jnp.where(inside, picked, 0.0)
        return ((new_totals, new_target), None)
    initial = (jnp.zeros((NHIST * IMP_DEV,), jnp.float32), jnp.zeros((NHIST * IMP_DEV,), jnp.float32))
    finals, unused = lax.scan(step, initial, (blocks, bases))
    return (states, finals[1] - jnp.log(finals[0]))
```

```python
import functools
import math

import jax
import jax.numpy as jnp
from jax import lax
from jax.experimental import pallas as pl
from jax.experimental.pallas import tpu as pltpu
from jax.sharding import PartitionSpec as P

DH = 128
SLOTS = ("item", "dp")
EVERY = ("item", "dp", "tensor")
NT = (((1,), (1,)), ((), ()))
VMEM_LIMIT = 32 * 1024 * 1024


def whole_spec(space=pltpu.VMEM):
    return pl.BlockSpec(memory_space=space)


def position_column(packing, positions, slot):
    row = positions[pl.ds(packing[slot], 1), :].astype(jnp.float32)
    count = row.shape[1]
    diagonal = lax.broadcasted_iota(jnp.int32, (count, count), 0) == lax.broadcasted_iota(
        jnp.int32, (count, count), 1
    )
    return jnp.sum(jnp.where(diagonal, row, 0.0), axis=1, keepdims=True).astype(jnp.int32)


def pick_kernel(place, packing, positions, events, chosen):
    rows = events.shape[0]
    spots = position_column(packing, positions, place[0])
    lanes = lax.broadcasted_iota(jnp.int32, (spots.shape[0], rows), 1)
    one_hot = jnp.where(lanes == spots, 1.0, 0.0).astype(jnp.bfloat16)
    chosen[...] = jnp.dot(one_hot, events[...], preferred_element_type=jnp.float32).astype(
        jnp.bfloat16
    )


def attend_kernel(place, packing, lengths, positions, events, chosen, w_uvqk, gated):
    rows = events.shape[0]
    slot = place[0]
    length = lengths[packing[slot]]
    spots = position_column(packing, positions, slot)
    lanes = lax.broadcasted_iota(jnp.int32, (spots.shape[0], rows), 1)
    valid = (lanes <= spots) & (lanes < length)
    for head in range(gated.shape[1] // DH):
        first = head * 4 * DH
        w_part = [w_uvqk[:, first + k * DH : first + (k + 1) * DH] for k in range(4)]
        w_gate_query = jnp.concatenate([w_part[0], w_part[2]], axis=1)
        w_value_key = jnp.concatenate([w_part[1], w_part[3]], axis=1)
        gate_query = jnp.dot(chosen[...], w_gate_query, preferred_element_type=jnp.float32)
        gate_query = jax.nn.silu(gate_query).astype(jnp.bfloat16)
        value_key = jnp.dot(events[...], w_value_key, preferred_element_type=jnp.float32)
        value_key = jax.nn.silu(value_key).astype(jnp.bfloat16)
        scores = lax.dot_general(
            gate_query[:, DH:], value_key[:, DH:], NT, preferred_element_type=jnp.float32
        ) / math.sqrt(DH)
        weights = jnp.where(valid, jax.nn.silu(scores), 0.0).astype(jnp.bfloat16)
        attended = jnp.dot(weights, value_key[:, :DH], preferred_element_type=jnp.float32)
        inverse = lax.rsqrt(jnp.mean(attended * attended, axis=-1, keepdims=True) + 1e-06)
        gated[:, head * DH : (head + 1) * DH] = (
            attended * inverse * gate_query[:, :DH].astype(jnp.float32)
        ).astype(jnp.bfloat16)


def score_kernel(slots, tensors, place, packing, logged, *refs):
    chosen, refs = refs[:slots], refs[slots:]
    gated, refs = refs[:slots], refs[slots:]
    w_out, refs = refs[:tensors], refs[tensors:]
    catalogue, state, sums, hidden, wanted = refs
    slot, tensor = place[0], place[1]
    imps = chosen[0].shape[0]
    items = catalogue.shape[0]
    local_width = w_out[0].shape[0]
    for r in range(slots):
        total = chosen[r][...].astype(jnp.float32)
        for t in range(tensors):
            total += jnp.dot(
                gated[r][:, t * local_width : (t + 1) * local_width],
                w_out[t][...],
                preferred_element_type=jnp.float32,
            )
        hidden[r * imps : (r + 1) * imps, :] = total.astype(jnp.bfloat16)
        wanted[0:1, r * imps : (r + 1) * imps] = logged[pl.ds(packing[slot ^ r], 1), :]
    share = state.shape[1]
    state[...] = hidden[0:imps, pl.ds(pl.multiple_of(tensor * share, share), share)]
    item_base = (slot * tensors + tensor) * items
    step_rows = min(256, slots * imps)
    step_items = min(256, items)
    for row in range(0, slots * imps, step_rows):
        ids = wanted[0:1, row : row + step_rows] - item_base
        total = jnp.zeros((8, step_rows), jnp.float32)
        target = jnp.zeros((8, step_rows), jnp.float32)
        for item in range(0, items, step_items):
            logits = lax.dot_general(
                catalogue[item : item + step_items, :],
                hidden[row : row + step_rows, :],
                NT,
                preferred_element_type=jnp.float32,
            )
            item_ids = item + lax.broadcasted_iota(jnp.int32, logits.shape, 0)
            found = jnp.where(item_ids == ids, logits, 0.0)
            total += jnp.sum(jnp.exp(logits).reshape(-1, 8, step_rows), axis=0)
            target += jnp.sum(found.reshape(-1, 8, step_rows), axis=0)
        total = jnp.sum(total, axis=0, keepdims=True)
        target = jnp.sum(target, axis=0, keepdims=True)
        for part in range(step_rows // imps):
            owner = slot ^ (row // imps + part)
            both = jnp.concatenate(
                [v[:, part * imps : (part + 1) * imps] for v in (total, target)], axis=1
            )
            for t in range(tensors):
                sums[owner * tensors + t] = both


def from_others(x, axes, count):
    return [x] + [
        lax.ppermute(x, axes, [(i, i ^ r) for i in range(count)]) for r in range(1, count)
    ]


def local(events, lengths, packing, positions, logged, w_uvqk, w_out, catalogue):
    rows, width = events.shape
    imps = positions.shape[1]
    items = catalogue.shape[0]
    local_width = w_out.shape[0]
    tensors = lax.axis_size("tensor")
    slots = lax.axis_size(SLOTS)
    params = pltpu.CompilerParams(vmem_limit_bytes=VMEM_LIMIT)
    place = jnp.stack([lax.axis_index(SLOTS), lax.axis_index("tensor")]).astype(jnp.int32)
    smem, vmem = whole_spec(pltpu.SMEM), whole_spec()

    chosen = pl.pallas_call(
        pick_kernel,
        out_shape=jax.ShapeDtypeStruct((imps, width), jnp.bfloat16),
        in_specs=[smem, smem, vmem, vmem],
        out_specs=vmem,
        compiler_params=params,
        cost_estimate=pl.CostEstimate(
            flops=2 * imps * rows * width, bytes_accessed=2 * rows * width, transcendentals=0
        ),
        name="pick",
    )(place, packing, positions, events)
    all_chosen = from_others(chosen, SLOTS, slots)
    all_w_out = from_others(w_out, "tensor", tensors)

    gated = pl.pallas_call(
        attend_kernel,
        out_shape=jax.ShapeDtypeStruct((imps, local_width), jnp.bfloat16),
        in_specs=[smem, smem, smem, vmem, vmem, vmem, vmem],
        out_specs=vmem,
        compiler_params=params,
        cost_estimate=pl.CostEstimate(
            flops=4 * rows * width * local_width,
            bytes_accessed=2 * rows * width + 8 * width * local_width,
            transcendentals=2 * rows * local_width,
        ),
        name="attend",
    )(place, packing, lengths, positions, events, chosen, w_uvqk)
    gated = jnp.concatenate(from_others(gated, "tensor", tensors), axis=1)
    all_gated = from_others(gated, SLOTS, slots)

    state, sums = pl.pallas_call(
        functools.partial(score_kernel, slots, tensors),
        out_shape=(
            jax.ShapeDtypeStruct((imps, width // tensors), jnp.bfloat16),
            jax.ShapeDtypeStruct((slots * tensors, 1, 2 * imps), jnp.float32),
        ),
        in_specs=[smem, smem, vmem] + [vmem] * (2 * slots + tensors + 1),
        out_specs=(vmem, vmem),
        scratch_shapes=[
            pltpu.VMEM((slots * imps, width), jnp.bfloat16),
            pltpu.VMEM((1, slots * imps), jnp.int32),
        ],
        compiler_params=params,
        cost_estimate=pl.CostEstimate(
            flops=2 * slots * imps * width * (items + local_width * tensors),
            bytes_accessed=2 * items * width,
            transcendentals=slots * imps * items,
        ),
        name="score",
    )(place, packing, logged, *all_chosen, *all_gated, *all_w_out, catalogue)
    sums = lax.all_to_all(sums, EVERY, split_axis=0, concat_axis=0, tiled=True)
    sums = jnp.sum(sums, axis=(0, 1))
    return (state, sums[imps:] - jnp.log(sums[:imps]))


def solution(mesh):
    placed = (
        P(("groups", "item", "dp"), None),
        P("groups"),
        P("groups"),
        P("groups", None),
        P("groups", None),
        P(None, "tensor"),
        P("tensor", None),
        P(("item", "dp", "tensor"), None),
    )
    return jax.shard_map(
        local,
        mesh=mesh,
        in_specs=placed,
        out_specs=(P(("groups", "item", "dp"), "tensor"), P(("groups", "item", "dp"))),
        check_vma=False,
    )
```

```python
import functools
import math

import jax
import jax.numpy as jnp
from jax import lax
from jax.experimental import pallas as pl
from jax.experimental.pallas import tpu as pltpu
from jax.sharding import PartitionSpec as P

DH = 128
SLOTS = ("item", "dp")
COLUMN = ("item", "tensor")
NT = (((1,), (1,)), ((), ()))
VMEM_LIMIT = 32 * 1024 * 1024
EVENT_PARTS = 4


def spec(space):
    return pl.BlockSpec(memory_space=space)


def pick_kernel(
    shards,
    place,
    packing,
    lengths,
    positions,
    logged,
    events,
    chosen,
    limits,
    wanted,
    packing_s,
    lengths_s,
    positions_v,
    logged_v,
    events_v,
    sems,
):
    rows = events.shape[0]
    items_axis, dps = shards
    imps = positions.shape[1]
    part_rows = rows // EVENT_PARTS
    copies = [
        pltpu.make_async_copy(source, target, sems.at[k])
        for k, (source, target) in enumerate(
            [
                (packing, packing_s),
                (lengths, lengths_s),
                (positions, positions_v),
                (logged, logged_v),
            ]
            + [
                (events.at[pl.ds(k * part_rows, part_rows)], events_v.at[pl.ds(k * part_rows, part_rows)])
                for k in range(EVENT_PARTS)
            ]
        )
    ]
    for copy in copies:
        copy.start()
    for copy in copies[:4]:
        copy.wait()
    item, dp = place[0], place[1]
    history = packing_s[item * dps + dp]
    row = positions_v[pl.ds(history, 1), :].astype(jnp.float32)
    diagonal = lax.broadcasted_iota(jnp.int32, (imps, imps), 0) == lax.broadcasted_iota(
        jnp.int32, (imps, imps), 1
    )
    spots = jnp.sum(jnp.where(diagonal, row, 0.0), axis=1, keepdims=True).astype(jnp.int32)
    limits[...] = jnp.broadcast_to(jnp.minimum(spots, lengths_s[history] - 1), limits.shape)
    for k in range(items_axis):
        wanted[0:1, k * imps : (k + 1) * imps] = logged_v[pl.ds(packing_s[k * dps + dp], 1), :]
    total = jnp.zeros((imps, events.shape[1]), jnp.float32)
    for k in range(EVENT_PARTS):
        copies[4 + k].wait()
        lanes = k * part_rows + lax.broadcasted_iota(jnp.int32, (imps, part_rows), 1)
        one_hot = jnp.where(lanes == spots, 1.0, 0.0).astype(jnp.bfloat16)
        total += jnp.dot(
            one_hot,
            events_v[k * part_rows : (k + 1) * part_rows, :],
            preferred_element_type=jnp.float32,
        )
    total = total.astype(jnp.bfloat16)
    for k in range(items_axis):
        chosen[k] = total


def attend_kernel(place, limits, events, chosen, w_uvqk, gated):
    rows = events.shape[0]
    own = chosen[place[0]]
    lanes = lax.broadcasted_iota(jnp.int32, (own.shape[0], rows), 1)
    valid = lanes <= limits[:, 0:1]
    for head in range(gated.shape[2] // DH):
        first = head * 4 * DH
        w_part = [w_uvqk[:, first + k * DH : first + (k + 1) * DH] for k in range(4)]
        w_gate_query = jnp.concatenate([w_part[0], w_part[2]], axis=1)
        w_value_key = jnp.concatenate([w_part[1], w_part[3]], axis=1)
        gate_query = jnp.dot(own, w_gate_query, preferred_element_type=jnp.float32)
        gate_query = jax.nn.silu(gate_query).astype(jnp.bfloat16)
        value_key = jnp.dot(events[...], w_value_key, preferred_element_type=jnp.float32)
        value_key = jax.nn.silu(value_key).astype(jnp.bfloat16)
        scores = lax.dot_general(
            gate_query[:, DH:], value_key[:, DH:], NT, preferred_element_type=jnp.float32
        ) / math.sqrt(DH)
        weights = jnp.where(valid, jax.nn.silu(scores), 0.0).astype(jnp.bfloat16)
        attended = jnp.dot(weights, value_key[:, :DH], preferred_element_type=jnp.float32)
        inverse = lax.rsqrt(jnp.mean(attended * attended, axis=-1, keepdims=True) + 1e-06)
        gated_rows = (attended * inverse * gate_query[:, :DH].astype(jnp.float32)).astype(
            jnp.bfloat16
        )
        for k in range(gated.shape[0]):
            gated[k, :, head * DH : (head + 1) * DH] = gated_rows


def score_kernel(sizes, place, wanted, chosen, gated, *refs):
    items_axis, dps, tensors = sizes
    w_out, refs = refs[:tensors], refs[tensors:]
    catalogue, refs = refs[:dps], refs[dps:]
    state, sums, hidden = refs
    item, dp, tensor = place[0], place[1], place[2]
    imps = chosen.shape[1]
    items = catalogue[0].shape[0]
    for k in range(items_axis):
        total = chosen[k].astype(jnp.float32)
        for t in range(tensors):
            total += jnp.dot(
                gated[k * tensors + (tensor ^ t)], w_out[t][...], preferred_element_type=jnp.float32
            )
        hidden[k * imps : (k + 1) * imps, :] = total.astype(jnp.bfloat16)
    share = state.shape[1]
    state[...] = hidden[
        pl.ds(pl.multiple_of(item * imps, imps), imps),
        pl.ds(pl.multiple_of(tensor * share, share), share),
    ]
    step_rows = min(256, items_axis * imps)
    step_items = min(256, items)
    for row in range(0, items_axis * imps, step_rows):
        total = jnp.zeros((8, step_rows), jnp.float32)
        target = jnp.zeros((8, step_rows), jnp.float32)
        for d in range(dps):
            item_base = ((item * dps + (dp ^ d)) * tensors + tensor) * items
            ids = wanted[0:1, row : row + step_rows] - item_base
            for first in range(0, items, step_items):
                logits = lax.dot_general(
                    catalogue[d][first : first + step_items, :],
                    hidden[row : row + step_rows, :],
                    NT,
                    preferred_element_type=jnp.float32,
                )
                item_ids = first + lax.broadcasted_iota(jnp.int32, logits.shape, 0)
                found = jnp.where(item_ids == ids, logits, 0.0)
                total += jnp.sum(jnp.exp(logits).reshape(-1, 8, step_rows), axis=0)
                target += jnp.sum(found.reshape(-1, 8, step_rows), axis=0)
        total = jnp.sum(total, axis=0, keepdims=True)
        target = jnp.sum(target, axis=0, keepdims=True)
        for part in range(step_rows // imps):
            owner = row // imps + part
            both = jnp.concatenate(
                [v[:, part * imps : (part + 1) * imps] for v in (total, target)], axis=1
            )
            for t in range(tensors):
                sums[owner * tensors + t] = both


def in_hbm(x):
    return pltpu.with_memory_space_constraint(x, pltpu.HBM)


def from_others(x, axes, count):
    return [x] + [
        lax.ppermute(x, axes, [(i, i ^ r) for i in range(count)]) for r in range(1, count)
    ]


def local(events, lengths, packing, positions, logged, w_uvqk, w_out, catalogue):
    rows, width = events.shape
    imps = positions.shape[1]
    hists = packing.shape[0]
    items = catalogue.shape[0]
    local_width = w_out.shape[0]
    items_axis, dps, tensors = (lax.axis_size(a) for a in ("item", "dp", "tensor"))
    receivers = items_axis * tensors
    params = pltpu.CompilerParams(vmem_limit_bytes=VMEM_LIMIT)
    place = jnp.stack([lax.axis_index(a) for a in ("item", "dp", "tensor")]).astype(jnp.int32)
    smem, vmem, hbm = spec(pltpu.SMEM), spec(pltpu.VMEM), spec(pltpu.HBM)

    all_w_out = from_others(w_out, "tensor", tensors)
    all_catalogue = from_others(catalogue, "dp", dps)
    chosen, limits, wanted = pl.pallas_call(
        functools.partial(pick_kernel, (items_axis, dps)),
        out_shape=(
            jax.ShapeDtypeStruct((items_axis, imps, width), jnp.bfloat16),
            jax.ShapeDtypeStruct((imps, 128), jnp.int32),
            jax.ShapeDtypeStruct((1, items_axis * imps), jnp.int32),
        ),
        in_specs=[smem] + [hbm] * 5,
        out_specs=(vmem, vmem, vmem),
        scratch_shapes=[
            pltpu.SMEM((hists,), jnp.int32),
            pltpu.SMEM((hists,), jnp.int32),
            pltpu.VMEM((hists, imps), jnp.int32),
            pltpu.VMEM((hists, imps), jnp.int32),
            pltpu.VMEM((rows, width), jnp.bfloat16),
            pltpu.SemaphoreType.DMA((4 + EVENT_PARTS,)),
        ],
        compiler_params=params,
        cost_estimate=pl.CostEstimate(
            flops=2 * imps * rows * width, bytes_accessed=2 * rows * width, transcendentals=0
        ),
        name="pick",
    )(place, *(in_hbm(x) for x in (packing, lengths, positions, logged, events)))
    all_chosen = lax.all_to_all(chosen, "item", split_axis=0, concat_axis=0, tiled=True)

    gated = pl.pallas_call(
        attend_kernel,
        out_shape=jax.ShapeDtypeStruct((receivers, imps, local_width), jnp.bfloat16),
        in_specs=[smem, vmem, vmem, vmem, vmem],
        out_specs=vmem,
        compiler_params=params,
        cost_estimate=pl.CostEstimate(
            flops=4 * rows * width * local_width,
            bytes_accessed=2 * rows * width + 8 * width * local_width,
            transcendentals=2 * rows * local_width,
        ),
        name="attend",
    )(place, limits, events, chosen, w_uvqk)
    all_gated = lax.all_to_all(gated, COLUMN, split_axis=0, concat_axis=0, tiled=True)

    state, sums = pl.pallas_call(
        functools.partial(score_kernel, (items_axis, dps, tensors)),
        out_shape=(
            jax.ShapeDtypeStruct((imps, width // tensors), jnp.bfloat16),
            jax.ShapeDtypeStruct((receivers, 1, 2 * imps), jnp.float32),
        ),
        in_specs=[smem] + [vmem] * (3 + tensors + dps),
        out_specs=(vmem, vmem),
        scratch_shapes=[pltpu.VMEM((items_axis * imps, width), jnp.bfloat16)],
        compiler_params=params,
        cost_estimate=pl.CostEstimate(
            flops=2 * items_axis * imps * width * (dps * items + local_width * tensors),
            bytes_accessed=2 * dps * items * width,
            transcendentals=items_axis * imps * dps * items,
        ),
        name="score",
    )(place, wanted, all_chosen, all_gated, *all_w_out, *all_catalogue)
    sums = lax.all_to_all(sums, COLUMN, split_axis=0, concat_axis=0, tiled=True)
    sums = jnp.sum(sums, axis=(0, 1))
    return (state, sums[imps:] - jnp.log(sums[:imps]))


def solution(mesh):
    placed = (
        P(("groups", "item", "dp"), None),
        P("groups"),
        P("groups"),
        P("groups", None),
        P("groups", None),
        P(None, "tensor"),
        P("tensor", None),
        P(("item", "dp", "tensor"), None),
    )
    return jax.shard_map(
        local,
        mesh=mesh,
        in_specs=placed,
        out_specs=(P(("groups", "item", "dp"), "tensor"), P(("groups", "item", "dp"))),
        check_vma=False,
    )
```

```python
import functools
import math

import jax
import jax.numpy as jnp
from jax import lax
from jax.experimental import pallas as pl
from jax.experimental.pallas import tpu as pltpu
from jax.sharding import PartitionSpec as P

DH = 128
SLOTS = ("item", "dp")
COLUMN = ("item", "tensor")
NT = (((1,), (1,)), ((), ()))
VMEM_LIMIT = 32 * 1024 * 1024
EVENT_PARTS = 4


def spec(space):
    return pl.BlockSpec(memory_space=space)


def pick_kernel(
    shards,
    place,
    packing,
    lengths,
    positions,
    logged,
    events,
    w_uvqk,
    chosen,
    limits,
    wanted,
    events_v,
    w_uvqk_v,
    packing_s,
    lengths_s,
    positions_v,
    logged_v,
    sems,
):
    rows = events.shape[0]
    items_axis, dps = shards
    imps = positions.shape[1]
    part_rows = rows // EVENT_PARTS
    parts = [pl.ds(k * part_rows, part_rows) for k in range(EVENT_PARTS)]
    copies = [
        pltpu.make_async_copy(source, target, sems.at[k])
        for k, (source, target) in enumerate(
            [
                (packing, packing_s),
                (positions, positions_v),
                (lengths, lengths_s),
                (logged, logged_v),
            ]
            + [(events.at[part], events_v.at[part]) for part in parts]
            + [(w_uvqk, w_uvqk_v)]
        )
    ]
    for copy in copies:
        copy.start()
    for copy in copies[:4]:
        copy.wait()
    item, dp = place[0], place[1]
    history = packing_s[item * dps + dp]
    row = positions_v[pl.ds(history, 1), :].astype(jnp.float32)
    diagonal = lax.broadcasted_iota(jnp.int32, (imps, imps), 0) == lax.broadcasted_iota(
        jnp.int32, (imps, imps), 1
    )
    spots = jnp.sum(jnp.where(diagonal, row, 0.0), axis=1, keepdims=True).astype(jnp.int32)
    limits[...] = jnp.broadcast_to(jnp.minimum(spots, lengths_s[history] - 1), limits.shape)
    for k in range(items_axis):
        other = packing_s[(item ^ k) * dps + dp]
        wanted[0:1, k * imps : (k + 1) * imps] = logged_v[pl.ds(other, 1), :]
    total = jnp.zeros((imps, events.shape[1]), jnp.float32)
    for k in range(EVENT_PARTS):
        copies[4 + k].wait()
        lanes = k * part_rows + lax.broadcasted_iota(jnp.int32, (imps, part_rows), 1)
        one_hot = jnp.where(lanes == spots, 1.0, 0.0).astype(jnp.bfloat16)
        total += jnp.dot(
            one_hot,
            events_v[k * part_rows : (k + 1) * part_rows, :],
            preferred_element_type=jnp.float32,
        )
    chosen[...] = total.astype(jnp.bfloat16)
    copies[-1].wait()


def attend_kernel(limits, events, chosen, w_uvqk, gated):
    rows = events.shape[0]
    own = chosen[...]
    lanes = lax.broadcasted_iota(jnp.int32, (own.shape[0], rows), 1)
    valid = lanes <= limits[:, 0:1]
    for head in range(gated.shape[2] // DH):
        first = head * 4 * DH
        w_part = [w_uvqk[:, first + k * DH : first + (k + 1) * DH] for k in range(4)]
        w_gate_query = jnp.concatenate([w_part[0], w_part[2]], axis=1)
        w_value_key = jnp.concatenate([w_part[1], w_part[3]], axis=1)
        gate_query = jnp.dot(own, w_gate_query, preferred_element_type=jnp.float32)
        gate_query = jax.nn.silu(gate_query).astype(jnp.bfloat16)
        value_key = jnp.dot(events[...], w_value_key, preferred_element_type=jnp.float32)
        value_key = jax.nn.silu(value_key).astype(jnp.bfloat16)
        scores = lax.dot_general(
            gate_query[:, DH:], value_key[:, DH:], NT, preferred_element_type=jnp.float32
        ) / math.sqrt(DH)
        weights = jnp.where(valid, jax.nn.silu(scores), 0.0).astype(jnp.bfloat16)
        attended = jnp.dot(weights, value_key[:, :DH], preferred_element_type=jnp.float32)
        inverse = lax.rsqrt(jnp.mean(attended * attended, axis=-1, keepdims=True) + 1e-06)
        gated_rows = (attended * inverse * gate_query[:, :DH].astype(jnp.float32)).astype(
            jnp.bfloat16
        )
        for k in range(gated.shape[0]):
            gated[k, :, head * DH : (head + 1) * DH] = gated_rows


def score_kernel(sizes, place, wanted, gated, *refs):
    items_axis, dps, tensors = sizes
    chosen, refs = refs[:items_axis], refs[items_axis:]
    w_out, refs = refs[:tensors], refs[tensors:]
    catalogue, refs = list(refs[:dps]), refs[dps:]
    state, sums, hidden, own_catalogue, sem = refs
    fetch = pltpu.make_async_copy(catalogue[0], own_catalogue, sem)
    fetch.start()
    catalogue[0] = own_catalogue
    item, dp, tensor = place[0], place[1], place[2]
    imps = chosen[0].shape[0]
    items = own_catalogue.shape[0]
    for k in range(items_axis):
        total = chosen[k][...].astype(jnp.float32)
        for t in range(tensors):
            total += jnp.dot(
                gated[(item ^ k) * tensors + (tensor ^ t)],
                w_out[t][...],
                preferred_element_type=jnp.float32,
            )
        hidden[k * imps : (k + 1) * imps, :] = total.astype(jnp.bfloat16)
    share = state.shape[1]
    state[...] = hidden[0:imps, pl.ds(pl.multiple_of(tensor * share, share), share)]
    step_rows = min(256, items_axis * imps)
    step_items = min(256, items)
    blocks = range(0, items_axis * imps, step_rows)
    totals = {row: jnp.zeros((8, step_rows), jnp.float32) for row in blocks}
    targets = dict(totals)
    for d in reversed(range(dps)):
        if d == 0:
            fetch.wait()
        item_base = ((item * dps + (dp ^ d)) * tensors + tensor) * items
        for row in blocks:
            ids = wanted[0:1, row : row + step_rows] - item_base
            for first in range(0, items, step_items):
                logits = lax.dot_general(
                    catalogue[d][first : first + step_items, :],
                    hidden[row : row + step_rows, :],
                    NT,
                    preferred_element_type=jnp.float32,
                )
                item_ids = first + lax.broadcasted_iota(jnp.int32, logits.shape, 0)
                found = jnp.where(item_ids == ids, logits, 0.0)
                totals[row] += jnp.sum(jnp.exp(logits).reshape(-1, 8, step_rows), axis=0)
                targets[row] += jnp.sum(found.reshape(-1, 8, step_rows), axis=0)
    for row in blocks:
        total = jnp.sum(totals[row], axis=0, keepdims=True)
        target = jnp.sum(targets[row], axis=0, keepdims=True)
        for part in range(step_rows // imps):
            owner = item ^ (row // imps + part)
            both = jnp.concatenate(
                [v[:, part * imps : (part + 1) * imps] for v in (total, target)], axis=1
            )
            for t in range(tensors):
                sums[owner * tensors + t] = both


def in_hbm(x):
    return pltpu.with_memory_space_constraint(x, pltpu.HBM)


def from_others(x, axes, count):
    return [x] + [
        lax.ppermute(x, axes, [(i, i ^ r) for i in range(count)]) for r in range(1, count)
    ]


def local(events, lengths, packing, positions, logged, w_uvqk, w_out, catalogue):
    rows, width = events.shape
    imps = positions.shape[1]
    hists = packing.shape[0]
    items = catalogue.shape[0]
    local_width = w_out.shape[0]
    items_axis, dps, tensors = (lax.axis_size(a) for a in ("item", "dp", "tensor"))
    receivers = items_axis * tensors
    params = pltpu.CompilerParams(vmem_limit_bytes=VMEM_LIMIT)
    place = jnp.stack([lax.axis_index(a) for a in ("item", "dp", "tensor")]).astype(jnp.int32)
    smem, vmem, hbm = spec(pltpu.SMEM), spec(pltpu.VMEM), spec(pltpu.HBM)

    all_w_out = from_others(w_out, "tensor", tensors)
    all_catalogue = from_others(catalogue, "dp", dps)
    chosen, limits, wanted, events, w_uvqk = pl.pallas_call(
        functools.partial(pick_kernel, (items_axis, dps)),
        out_shape=(
            jax.ShapeDtypeStruct((imps, width), jnp.bfloat16),
            jax.ShapeDtypeStruct((imps, 128), jnp.int32),
            jax.ShapeDtypeStruct((1, items_axis * imps), jnp.int32),
            jax.ShapeDtypeStruct(events.shape, events.dtype),
            jax.ShapeDtypeStruct(w_uvqk.shape, w_uvqk.dtype),
        ),
        in_specs=[smem] + [hbm] * 6,
        out_specs=(vmem,) * 5,
        scratch_shapes=[
            pltpu.SMEM((hists,), jnp.int32),
            pltpu.SMEM((hists,), jnp.int32),
            pltpu.VMEM((hists, imps), jnp.int32),
            pltpu.VMEM((hists, imps), jnp.int32),
            pltpu.SemaphoreType.DMA((5 + EVENT_PARTS,)),
        ],
        compiler_params=params,
        cost_estimate=pl.CostEstimate(
            flops=2 * imps * rows * width, bytes_accessed=2 * rows * width, transcendentals=0
        ),
        name="pick",
    )(place, *(in_hbm(x) for x in (packing, lengths, positions, logged, events, w_uvqk)))
    all_chosen = from_others(chosen, "item", items_axis)

    gated = pl.pallas_call(
        attend_kernel,
        out_shape=jax.ShapeDtypeStruct((receivers, imps, local_width), jnp.bfloat16),
        in_specs=[vmem] * 4,
        out_specs=vmem,
        compiler_params=params,
        cost_estimate=pl.CostEstimate(flops=0, bytes_accessed=0, transcendentals=0),
        name="attend",
    )(limits, events, chosen, w_uvqk)
    all_gated = lax.all_to_all(gated, COLUMN, split_axis=0, concat_axis=0, tiled=True)

    own_catalogue, *other_catalogues = all_catalogue
    state, sums = pl.pallas_call(
        functools.partial(score_kernel, (items_axis, dps, tensors)),
        out_shape=(
            jax.ShapeDtypeStruct((imps, width // tensors), jnp.bfloat16),
            jax.ShapeDtypeStruct((receivers, 1, 2 * imps), jnp.float32),
        ),
        in_specs=[smem] + [vmem] * (2 + items_axis + tensors) + [hbm] + [vmem] * (dps - 1),
        out_specs=(vmem, vmem),
        scratch_shapes=[
            pltpu.VMEM((items_axis * imps, width), jnp.bfloat16),
            pltpu.VMEM((items, width), jnp.bfloat16),
            pltpu.SemaphoreType.DMA,
        ],
        compiler_params=params,
        cost_estimate=pl.CostEstimate(
            flops=2 * items_axis * imps * width * (dps * items + local_width * tensors),
            bytes_accessed=2 * dps * items * width,
            transcendentals=items_axis * imps * dps * items,
        ),
        name="score",
    )(
        place,
        wanted,
        all_gated,
        *all_chosen,
        *all_w_out,
        in_hbm(own_catalogue),
        *other_catalogues,
    )
    sums = lax.all_to_all(sums, COLUMN, split_axis=0, concat_axis=0, tiled=True)
    sums = jnp.sum(sums, axis=(0, 1))
    return (state, sums[imps:] - jnp.log(sums[:imps]))


def solution(mesh):
    placed = (
        P(("groups", "item", "dp"), None),
        P("groups"),
        P("groups"),
        P("groups", None),
        P("groups", None),
        P(None, "tensor"),
        P("tensor", None),
        P(("item", "dp", "tensor"), None),
    )
    return jax.shard_map(
        local,
        mesh=mesh,
        in_specs=placed,
        out_specs=(P(("groups", "item", "dp"), "tensor"), P(("groups", "item", "dp"))),
        check_vma=False,
    )
```

```python
import functools
import math

import jax
import jax.numpy as jnp
from jax import lax
from jax.experimental import pallas as pl
from jax.experimental.pallas import tpu as pltpu
from jax.sharding import PartitionSpec as P

DH = 128
SLOTS = ("item", "dp")
COLUMN = ("item", "tensor")
NT = (((1,), (1,)), ((), ()))
VMEM_LIMIT = 16 * 1024 * 1024
EVENT_PARTS = 4


def spec(space):
    return pl.BlockSpec(memory_space=space)


def pick_kernel(
    shards,
    place,
    packing,
    lengths,
    positions,
    logged,
    events,
    w_uvqk,
    chosen,
    limits,
    wanted,
    events_v,
    w_uvqk_v,
    packing_s,
    lengths_s,
    positions_v,
    logged_v,
    sems,
):
    rows = events.shape[0]
    items_axis, dps = shards
    imps = positions.shape[1]
    part_rows = rows // EVENT_PARTS
    parts = [pl.ds(k * part_rows, part_rows) for k in range(EVENT_PARTS)]
    copies = [
        pltpu.make_async_copy(source, target, sems.at[k])
        for k, (source, target) in enumerate(
            [
                (packing, packing_s),
                (positions, positions_v),
                (lengths, lengths_s),
                (logged, logged_v),
            ]
            + [(events.at[part], events_v.at[part]) for part in parts]
            + [(w_uvqk, w_uvqk_v)]
        )
    ]
    for copy in copies:
        copy.start()
    for copy in copies[:4]:
        copy.wait()
    item, dp = place[0], place[1]
    history = packing_s[item * dps + dp]
    row = positions_v[pl.ds(history, 1), :].astype(jnp.float32)
    diagonal = lax.broadcasted_iota(jnp.int32, (imps, imps), 0) == lax.broadcasted_iota(
        jnp.int32, (imps, imps), 1
    )
    spots = jnp.sum(jnp.where(diagonal, row, 0.0), axis=1, keepdims=True).astype(jnp.int32)
    limits[...] = jnp.broadcast_to(jnp.minimum(spots, lengths_s[history] - 1), limits.shape)
    for k in range(items_axis):
        other = packing_s[(item ^ k) * dps + dp]
        wanted[0:1, k * imps : (k + 1) * imps] = logged_v[pl.ds(other, 1), :]
    total = jnp.zeros((imps, events.shape[1]), jnp.float32)
    for k in range(EVENT_PARTS):
        copies[4 + k].wait()
        lanes = k * part_rows + lax.broadcasted_iota(jnp.int32, (imps, part_rows), 1)
        one_hot = jnp.where(lanes == spots, 1.0, 0.0).astype(jnp.bfloat16)
        total += jnp.dot(
            one_hot,
            events_v[k * part_rows : (k + 1) * part_rows, :],
            preferred_element_type=jnp.float32,
        )
    chosen[...] = total.astype(jnp.bfloat16)
    copies[-1].wait()


def attend_kernel(limits, events, chosen, w_uvqk, gated):
    rows = events.shape[0]
    own = chosen[...]
    lanes = lax.broadcasted_iota(jnp.int32, (own.shape[0], rows), 1)
    valid = lanes <= limits[:, 0:1]
    for head in range(gated.shape[2] // DH):
        first = head * 4 * DH
        w_part = [w_uvqk[:, first + k * DH : first + (k + 1) * DH] for k in range(4)]
        w_gate_query = jnp.concatenate([w_part[0], w_part[2]], axis=1)
        w_value_key = jnp.concatenate([w_part[1], w_part[3]], axis=1)
        gate_query = jnp.dot(own, w_gate_query, preferred_element_type=jnp.float32)
        gate_query = jax.nn.silu(gate_query).astype(jnp.bfloat16)
        value_key = jnp.dot(events[...], w_value_key, preferred_element_type=jnp.float32)
        value_key = jax.nn.silu(value_key).astype(jnp.bfloat16)
        scores = lax.dot_general(
            gate_query[:, DH:], value_key[:, DH:], NT, preferred_element_type=jnp.float32
        ) / math.sqrt(DH)
        weights = jnp.where(valid, jax.nn.silu(scores), 0.0).astype(jnp.bfloat16)
        attended = jnp.dot(weights, value_key[:, :DH], preferred_element_type=jnp.float32)
        inverse = lax.rsqrt(jnp.mean(attended * attended, axis=-1, keepdims=True) + 1e-06)
        gated_rows = (attended * inverse * gate_query[:, :DH].astype(jnp.float32)).astype(
            jnp.bfloat16
        )
        for k in range(gated.shape[0]):
            gated[k, :, head * DH : (head + 1) * DH] = gated_rows


def score_kernel(sizes, place, wanted, gated, *refs):
    items_axis, dps, tensors = sizes
    chosen, refs = refs[:items_axis], refs[items_axis:]
    w_out, refs = refs[:tensors], refs[tensors:]
    catalogue, refs = list(refs[:dps]), refs[dps:]
    state, sums, hidden, own_catalogue, sem = refs
    fetch = pltpu.make_async_copy(catalogue[0], own_catalogue, sem)
    fetch.start()
    catalogue[0] = own_catalogue
    item, dp, tensor = place[0], place[1], place[2]
    imps = chosen[0].shape[0]
    items = own_catalogue.shape[0]
    for k in range(items_axis):
        total = chosen[k][...].astype(jnp.float32)
        for t in range(tensors):
            total += jnp.dot(
                gated[(item ^ k) * tensors + (tensor ^ t)],
                w_out[t][...],
                preferred_element_type=jnp.float32,
            )
        hidden[k * imps : (k + 1) * imps, :] = total.astype(jnp.bfloat16)
    share = state.shape[1]
    state[...] = hidden[0:imps, pl.ds(pl.multiple_of(tensor * share, share), share)]
    step_rows = min(256, items_axis * imps)
    step_items = min(1024, items)
    blocks = range(0, items_axis * imps, step_rows)
    totals = {row: jnp.zeros((8, step_rows), jnp.float32) for row in blocks}
    targets = dict(totals)
    for d in reversed(range(dps)):
        if d == 0:
            fetch.wait()
        item_base = ((item * dps + (dp ^ d)) * tensors + tensor) * items
        for row in blocks:
            ids = wanted[0:1, row : row + step_rows] - item_base
            for first in range(0, items, step_items):
                logits = lax.dot_general(
                    catalogue[d][first : first + step_items, :],
                    hidden[row : row + step_rows, :],
                    NT,
                    preferred_element_type=jnp.float32,
                )
                item_ids = first + lax.broadcasted_iota(jnp.int32, logits.shape, 0)
                found = jnp.where(item_ids == ids, logits, 0.0)
                totals[row] += jnp.sum(jnp.exp(logits).reshape(-1, 8, step_rows), axis=0)
                targets[row] += jnp.sum(found.reshape(-1, 8, step_rows), axis=0)
    for row in blocks:
        total = jnp.sum(totals[row], axis=0, keepdims=True)
        target = jnp.sum(targets[row], axis=0, keepdims=True)
        for part in range(step_rows // imps):
            owner = item ^ (row // imps + part)
            both = jnp.concatenate(
                [v[:, part * imps : (part + 1) * imps] for v in (total, target)], axis=1
            )
            for t in range(tensors):
                sums[owner * tensors + t] = both


def in_hbm(x):
    return pltpu.with_memory_space_constraint(x, pltpu.HBM)


def from_others(x, axes, count):
    return [x] + [
        lax.ppermute(x, axes, [(i, i ^ r) for i in range(count)]) for r in range(1, count)
    ]


def local(events, lengths, packing, positions, logged, w_uvqk, w_out, catalogue):
    rows, width = events.shape
    imps = positions.shape[1]
    hists = packing.shape[0]
    items = catalogue.shape[0]
    local_width = w_out.shape[0]
    items_axis, dps, tensors = (lax.axis_size(a) for a in ("item", "dp", "tensor"))
    receivers = items_axis * tensors
    params = pltpu.CompilerParams(vmem_limit_bytes=VMEM_LIMIT)
    place = jnp.stack([lax.axis_index(a) for a in ("item", "dp", "tensor")]).astype(jnp.int32)
    smem, vmem, hbm = spec(pltpu.SMEM), spec(pltpu.VMEM), spec(pltpu.HBM)

    all_w_out = from_others(w_out, "tensor", tensors)
    all_catalogue = from_others(catalogue, "dp", dps)
    chosen, limits, wanted, events, w_uvqk = pl.pallas_call(
        functools.partial(pick_kernel, (items_axis, dps)),
        out_shape=(
            jax.ShapeDtypeStruct((imps, width), jnp.bfloat16),
            jax.ShapeDtypeStruct((imps, 128), jnp.int32),
            jax.ShapeDtypeStruct((1, items_axis * imps), jnp.int32),
            jax.ShapeDtypeStruct(events.shape, events.dtype),
            jax.ShapeDtypeStruct(w_uvqk.shape, w_uvqk.dtype),
        ),
        in_specs=[smem] + [hbm] * 6,
        out_specs=(vmem,) * 5,
        scratch_shapes=[
            pltpu.SMEM((hists,), jnp.int32),
            pltpu.SMEM((hists,), jnp.int32),
            pltpu.VMEM((hists, imps), jnp.int32),
            pltpu.VMEM((hists, imps), jnp.int32),
            pltpu.SemaphoreType.DMA((5 + EVENT_PARTS,)),
        ],
        compiler_params=params,
        cost_estimate=pl.CostEstimate(
            flops=2 * imps * rows * width, bytes_accessed=2 * rows * width, transcendentals=0
        ),
        name="pick",
    )(place, *(in_hbm(x) for x in (packing, lengths, positions, logged, events, w_uvqk)))
    all_chosen = from_others(chosen, "item", items_axis)

    gated = pl.pallas_call(
        attend_kernel,
        out_shape=jax.ShapeDtypeStruct((receivers, imps, local_width), jnp.bfloat16),
        in_specs=[vmem] * 4,
        out_specs=vmem,
        compiler_params=params,
        cost_estimate=pl.CostEstimate(flops=0, bytes_accessed=0, transcendentals=0),
        name="attend",
    )(limits, events, chosen, w_uvqk)
    all_gated = lax.cond(
        lengths[0] > 0,
        lambda x: lax.all_to_all(x, COLUMN, split_axis=0, concat_axis=0, tiled=True),
        lambda x: x,
        gated,
    )

    own_catalogue, *other_catalogues = all_catalogue
    state, sums = pl.pallas_call(
        functools.partial(score_kernel, (items_axis, dps, tensors)),
        out_shape=(
            jax.ShapeDtypeStruct((imps, width // tensors), jnp.bfloat16),
            jax.ShapeDtypeStruct((receivers, 1, 2 * imps), jnp.float32),
        ),
        in_specs=[smem] + [vmem] * (2 + items_axis + tensors) + [hbm] + [vmem] * (dps - 1),
        out_specs=(vmem, vmem),
        scratch_shapes=[
            pltpu.VMEM((items_axis * imps, width), jnp.bfloat16),
            pltpu.VMEM((items, width), jnp.bfloat16),
            pltpu.SemaphoreType.DMA,
        ],
        compiler_params=params,
        cost_estimate=pl.CostEstimate(
            flops=2 * items_axis * imps * width * (dps * items + local_width * tensors),
            bytes_accessed=2 * dps * items * width,
            transcendentals=items_axis * imps * dps * items,
        ),
        name="score",
    )(
        place,
        wanted,
        all_gated,
        *all_chosen,
        *all_w_out,
        in_hbm(own_catalogue),
        *other_catalogues,
    )
    sums = lax.all_to_all(sums, COLUMN, split_axis=0, concat_axis=0, tiled=True)
    sums = jnp.sum(sums, axis=(0, 1))
    return (state, sums[imps:] - jnp.log(sums[:imps]))


def solution(mesh):
    placed = (
        P(("groups", "item", "dp"), None),
        P("groups"),
        P("groups"),
        P("groups", None),
        P("groups", None),
        P(None, "tensor"),
        P("tensor", None),
        P(("item", "dp", "tensor"), None),
    )
    return jax.shard_map(
        local,
        mesh=mesh,
        in_specs=placed,
        out_specs=(P(("groups", "item", "dp"), "tensor"), P(("groups", "item", "dp"))),
        check_vma=False,
    )
```

```python
import functools
import math

import jax
import jax.numpy as jnp
from jax import lax
from jax.experimental import pallas as pl
from jax.experimental.pallas import tpu as pltpu
from jax.sharding import PartitionSpec as P

DH = 128
SLOTS = ("item", "dp")
COLUMN = ("item", "tensor")
NT = (((1,), (1,)), ((), ()))
VMEM_LIMIT = 16 * 1024 * 1024
EVENT_PARTS = 3


def rounds(count):
    return [0] + sorted(range(1, count), key=lambda r: -(r & -2))


def spec(space):
    return pl.BlockSpec(memory_space=space)


def pick_kernel(
    shards,
    place,
    packing,
    lengths,
    positions,
    logged,
    events,
    w_uvqk,
    chosen,
    limits,
    wanted,
    events_v,
    w_uvqk_v,
    packing_s,
    lengths_s,
    positions_v,
    logged_v,
    sems,
):
    rows = events.shape[0]
    items_axis, dps = shards
    imps = positions.shape[1]
    part_rows = rows // EVENT_PARTS
    parts = [pl.ds(k * part_rows, part_rows) for k in range(EVENT_PARTS)]
    copies = [
        pltpu.make_async_copy(source, target, sems.at[k])
        for k, (source, target) in enumerate(
            [
                (packing, packing_s),
                (positions, positions_v),
                (lengths, lengths_s),
                (logged, logged_v),
            ]
            + [(events.at[part], events_v.at[part]) for part in parts]
            + [(w_uvqk, w_uvqk_v)]
        )
    ]
    for copy in copies:
        copy.start()
    for copy in copies[:4]:
        copy.wait()
    item, dp = place[0], place[1]
    history = packing_s[item * dps + dp]
    row = positions_v[pl.ds(history, 1), :].astype(jnp.float32)
    diagonal = lax.broadcasted_iota(jnp.int32, (imps, imps), 0) == lax.broadcasted_iota(
        jnp.int32, (imps, imps), 1
    )
    spots = jnp.sum(jnp.where(diagonal, row, 0.0), axis=1, keepdims=True).astype(jnp.int32)
    limits[...] = jnp.broadcast_to(jnp.minimum(spots, lengths_s[history] - 1), limits.shape)
    for k, r in enumerate(rounds(items_axis)):
        other = packing_s[(item ^ r) * dps + dp]
        wanted[0:1, k * imps : (k + 1) * imps] = logged_v[pl.ds(other, 1), :]
    total = jnp.zeros((imps, events.shape[1]), jnp.float32)
    for k in range(EVENT_PARTS):
        copies[4 + k].wait()
        lanes = k * part_rows + lax.broadcasted_iota(jnp.int32, (imps, part_rows), 1)
        one_hot = jnp.where(lanes == spots, 1.0, 0.0).astype(jnp.bfloat16)
        total += jnp.dot(
            one_hot,
            events_v[k * part_rows : (k + 1) * part_rows, :],
            preferred_element_type=jnp.float32,
        )
    chosen[...] = total.astype(jnp.bfloat16)
    copies[-1].wait()


def attend_kernel(
    limits, events, chosen, w_uvqk, w_out, catalogue, gated, w_out_v, catalogue_v, sems
):
    fetches = [
        pltpu.make_async_copy(w_out, w_out_v, sems.at[0]),
        pltpu.make_async_copy(catalogue, catalogue_v, sems.at[1]),
    ]
    for fetch in fetches:
        fetch.start()
    rows = events.shape[0]
    own = chosen[...]
    lanes = lax.broadcasted_iota(jnp.int32, (own.shape[0], rows), 1)
    valid = lanes <= limits[:, 0:1]
    for head in range(gated.shape[2] // DH):
        first = head * 4 * DH
        w_part = [w_uvqk[:, first + k * DH : first + (k + 1) * DH] for k in range(4)]
        w_gate_query = jnp.concatenate([w_part[0], w_part[2]], axis=1)
        w_value_key = jnp.concatenate([w_part[1], w_part[3]], axis=1)
        gate_query = jnp.dot(own, w_gate_query, preferred_element_type=jnp.float32)
        gate_query = jax.nn.silu(gate_query).astype(jnp.bfloat16)
        value_key = jnp.dot(events[...], w_value_key, preferred_element_type=jnp.float32)
        value_key = jax.nn.silu(value_key).astype(jnp.bfloat16)
        scores = lax.dot_general(
            gate_query[:, DH:], value_key[:, DH:], NT, preferred_element_type=jnp.float32
        ) / math.sqrt(DH)
        weights = jnp.where(valid, jax.nn.silu(scores), 0.0).astype(jnp.bfloat16)
        attended = jnp.dot(weights, value_key[:, :DH], preferred_element_type=jnp.float32)
        inverse = lax.rsqrt(jnp.mean(attended * attended, axis=-1, keepdims=True) + 1e-06)
        gated_rows = (attended * inverse * gate_query[:, :DH].astype(jnp.float32)).astype(
            jnp.bfloat16
        )
        for k in range(gated.shape[0]):
            gated[k, :, head * DH : (head + 1) * DH] = gated_rows
    for fetch in fetches:
        fetch.wait()


def score_kernel(sizes, place, wanted, gated, *refs):
    items_axis, dps, tensors = sizes
    chosen, refs = refs[:items_axis], refs[items_axis:]
    w_out, refs = refs[:tensors], refs[tensors:]
    catalogue, refs = refs[:dps], refs[dps:]
    state, sums, hidden, others, sems = refs
    fetches = [
        pltpu.make_async_copy(catalogue[d], others.at[d - 1], sems.at[d - 1]) for d in range(1, dps)
    ]
    for fetch in fetches:
        fetch.start()
    catalogue = [catalogue[0]] + [others.at[d - 1] for d in range(1, dps)]
    item, dp, tensor = place[0], place[1], place[2]
    imps = chosen[0].shape[0]
    items = catalogue[0].shape[0]
    slot_rounds, tensor_rounds = rounds(items_axis), rounds(tensors)
    for k in range(items_axis):
        total = chosen[k][...].astype(jnp.float32)
        for t in range(tensors):
            total += jnp.dot(
                gated[(item ^ slot_rounds[k]) * tensors + (tensor ^ tensor_rounds[t])],
                w_out[t][...],
                preferred_element_type=jnp.float32,
            )
        hidden[k * imps : (k + 1) * imps, :] = total.astype(jnp.bfloat16)
    share = state.shape[1]
    state[...] = hidden[0:imps, pl.ds(pl.multiple_of(tensor * share, share), share)]
    step_rows = min(256, items_axis * imps)
    step_items = min(512, items)
    blocks = range(0, items_axis * imps, step_rows)
    totals = {row: jnp.zeros((8, step_rows), jnp.float32) for row in blocks}
    targets = dict(totals)
    for d in range(dps):
        if d > 0:
            fetches[d - 1].wait()
        item_base = ((item * dps + (dp ^ rounds(dps)[d])) * tensors + tensor) * items
        for row in blocks:
            ids = wanted[0:1, row : row + step_rows] - item_base
            for first in range(0, items, step_items):
                logits = lax.dot_general(
                    catalogue[d][first : first + step_items, :],
                    hidden[row : row + step_rows, :],
                    NT,
                    preferred_element_type=jnp.float32,
                )
                item_ids = first + lax.broadcasted_iota(jnp.int32, logits.shape, 0)
                found = jnp.where(item_ids == ids, logits, 0.0)
                totals[row] += jnp.sum(jnp.exp(logits).reshape(-1, 8, step_rows), axis=0)
                targets[row] += jnp.sum(found.reshape(-1, 8, step_rows), axis=0)
    for row in blocks:
        total = jnp.sum(totals[row], axis=0, keepdims=True)
        target = jnp.sum(targets[row], axis=0, keepdims=True)
        for part in range(step_rows // imps):
            owner = item ^ slot_rounds[row // imps + part]
            both = jnp.concatenate(
                [v[:, part * imps : (part + 1) * imps] for v in (total, target)], axis=1
            )
            for t in range(tensors):
                sums[owner * tensors + t] = both


def in_hbm(x):
    return pltpu.with_memory_space_constraint(x, pltpu.HBM)


def from_others(x, axes, count):
    return [x] + [
        lax.ppermute(x, axes, [(i, i ^ r) for i in range(count)]) for r in rounds(count)[1:]
    ]


def local(events, lengths, packing, positions, logged, w_uvqk, w_out, catalogue):
    rows, width = events.shape
    imps = positions.shape[1]
    hists = packing.shape[0]
    items = catalogue.shape[0]
    local_width = w_out.shape[0]
    items_axis, dps, tensors = (lax.axis_size(a) for a in ("item", "dp", "tensor"))
    receivers = items_axis * tensors
    params = pltpu.CompilerParams(vmem_limit_bytes=VMEM_LIMIT)
    place = jnp.stack([lax.axis_index(a) for a in ("item", "dp", "tensor")]).astype(jnp.int32)
    smem, vmem, hbm = spec(pltpu.SMEM), spec(pltpu.VMEM), spec(pltpu.HBM)

    chosen, limits, wanted, events, w_uvqk = pl.pallas_call(
        functools.partial(pick_kernel, (items_axis, dps)),
        out_shape=(
            jax.ShapeDtypeStruct((imps, width), jnp.bfloat16),
            jax.ShapeDtypeStruct((imps, 128), jnp.int32),
            jax.ShapeDtypeStruct((1, items_axis * imps), jnp.int32),
            jax.ShapeDtypeStruct(events.shape, events.dtype),
            jax.ShapeDtypeStruct(w_uvqk.shape, w_uvqk.dtype),
        ),
        in_specs=[smem] + [hbm] * 6,
        out_specs=(vmem,) * 5,
        scratch_shapes=[
            pltpu.SMEM((hists,), jnp.int32),
            pltpu.SMEM((hists,), jnp.int32),
            pltpu.VMEM((hists, imps), jnp.int32),
            pltpu.VMEM((hists, imps), jnp.int32),
            pltpu.SemaphoreType.DMA((5 + EVENT_PARTS,)),
        ],
        compiler_params=params,
        cost_estimate=pl.CostEstimate(
            flops=2 * imps * rows * width, bytes_accessed=2 * rows * width, transcendentals=0
        ),
        name="pick",
    )(place, *(in_hbm(x) for x in (packing, lengths, positions, logged, events, w_uvqk)))
    all_chosen = from_others(chosen, "item", items_axis)

    gated, w_out, catalogue = pl.pallas_call(
        attend_kernel,
        out_shape=(
            jax.ShapeDtypeStruct((receivers, imps, local_width), jnp.bfloat16),
            jax.ShapeDtypeStruct(w_out.shape, w_out.dtype),
            jax.ShapeDtypeStruct(catalogue.shape, catalogue.dtype),
        ),
        in_specs=[vmem] * 4 + [hbm] * 2,
        out_specs=(vmem,) * 3,
        scratch_shapes=[pltpu.SemaphoreType.DMA((2,))],
        compiler_params=params,
        cost_estimate=pl.CostEstimate(flops=0, bytes_accessed=0, transcendentals=0),
        name="attend",
    )(limits, events, chosen, w_uvqk, in_hbm(w_out), in_hbm(catalogue))

    def exchange(gated, w_out, catalogue):
        return (
            lax.all_to_all(gated, COLUMN, split_axis=0, concat_axis=0, tiled=True),
            from_others(w_out, "tensor", tensors)[1:],
            from_others(catalogue, "dp", dps)[1:],
        )

    def keep(gated, w_out, catalogue):
        return gated, [w_out] * (tensors - 1), [catalogue] * (dps - 1)

    all_gated, other_w_out, other_catalogues = lax.cond(
        lengths[0] > 0, exchange, keep, gated, w_out, catalogue
    )

    state, sums = pl.pallas_call(
        functools.partial(score_kernel, (items_axis, dps, tensors)),
        out_shape=(
            jax.ShapeDtypeStruct((imps, width // tensors), jnp.bfloat16),
            jax.ShapeDtypeStruct((receivers, 1, 2 * imps), jnp.float32),
        ),
        in_specs=[smem] + [vmem] * (3 + items_axis + tensors) + [hbm] * (dps - 1),
        out_specs=(vmem, vmem),
        scratch_shapes=[
            pltpu.VMEM((items_axis * imps, width), jnp.bfloat16),
            pltpu.VMEM((dps - 1, items, width), jnp.bfloat16),
            pltpu.SemaphoreType.DMA((dps - 1,)),
        ],
        compiler_params=params,
        cost_estimate=pl.CostEstimate(
            flops=2 * items_axis * imps * width * (dps * items + local_width * tensors),
            bytes_accessed=2 * dps * items * width,
            transcendentals=items_axis * imps * dps * items,
        ),
        name="score",
    )(
        place,
        wanted,
        all_gated,
        *all_chosen,
        w_out,
        *other_w_out,
        catalogue,
        *(in_hbm(x) for x in other_catalogues),
    )
    sums = lax.all_to_all(sums, COLUMN, split_axis=0, concat_axis=0, tiled=True)
    sums = jnp.sum(sums, axis=(0, 1))
    return (state, sums[imps:] - jnp.log(sums[:imps]))


def solution(mesh):
    placed = (
        P(("groups", "item", "dp"), None),
        P("groups"),
        P("groups"),
        P("groups", None),
        P("groups", None),
        P(None, "tensor"),
        P("tensor", None),
        P(("item", "dp", "tensor"), None),
    )
    return jax.shard_map(
        local,
        mesh=mesh,
        in_specs=placed,
        out_specs=(P(("groups", "item", "dp"), "tensor"), P(("groups", "item", "dp"))),
        check_vma=False,
    )
```

```python
import functools
import math

import jax
import jax.numpy as jnp
from jax import lax
from jax.experimental import pallas as pl
from jax.experimental.pallas import tpu as pltpu
from jax.sharding import PartitionSpec as P

DH = 128
SLOTS = ("item", "dp")
COLUMN = ("item", "tensor")
NT = (((1,), (1,)), ((), ()))
VMEM_LIMIT = 32 * 1024 * 1024
EVENT_PARTS = 3


def rounds(count):
    return [0] + sorted(range(1, count), key=lambda r: -(r & -2))


def spec(space):
    return pl.BlockSpec(memory_space=space)


def pick_kernel(
    shards,
    place,
    packing,
    lengths,
    positions,
    logged,
    events,
    w_uvqk,
    chosen,
    limits,
    wanted,
    events_v,
    w_uvqk_v,
    packing_s,
    lengths_s,
    positions_v,
    logged_v,
    sems,
):
    rows = events.shape[0]
    items_axis, dps = shards
    imps = positions.shape[1]
    part_rows = rows // EVENT_PARTS
    parts = [pl.ds(k * part_rows, part_rows) for k in range(EVENT_PARTS)]
    copies = [
        pltpu.make_async_copy(source, target, sems.at[k])
        for k, (source, target) in enumerate(
            [
                (packing, packing_s),
                (positions, positions_v),
                (lengths, lengths_s),
                (logged, logged_v),
            ]
            + [(events.at[part], events_v.at[part]) for part in parts]
            + [(w_uvqk, w_uvqk_v)]
        )
    ]
    for copy in copies[4:-1] + copies[:4]:
        copy.start()
    for copy in copies[:4]:
        copy.wait()
    item, dp = place[0], place[1]
    history = packing_s[item * dps + dp]
    row = positions_v[pl.ds(history, 1), :].astype(jnp.float32)
    diagonal = lax.broadcasted_iota(jnp.int32, (imps, imps), 0) == lax.broadcasted_iota(
        jnp.int32, (imps, imps), 1
    )
    spots = jnp.sum(jnp.where(diagonal, row, 0.0), axis=1, keepdims=True).astype(jnp.int32)
    limits[...] = jnp.broadcast_to(jnp.minimum(spots, lengths_s[history] - 1), limits.shape)
    for k, r in enumerate(rounds(items_axis)):
        other = packing_s[(item ^ r) * dps + dp]
        wanted[0:1, k * imps : (k + 1) * imps] = logged_v[pl.ds(other, 1), :]
    total = jnp.zeros((imps, events.shape[1]), jnp.float32)
    for k in range(EVENT_PARTS):
        copies[4 + k].wait()
        if k == 0:
            copies[-1].start()
        lanes = k * part_rows + lax.broadcasted_iota(jnp.int32, (imps, part_rows), 1)
        one_hot = jnp.where(lanes == spots, 1.0, 0.0).astype(jnp.bfloat16)
        total += jnp.dot(
            one_hot,
            events_v[k * part_rows : (k + 1) * part_rows, :],
            preferred_element_type=jnp.float32,
        )
    chosen[...] = total.astype(jnp.bfloat16)
    copies[-1].wait()


def attend_kernel(
    limits, events, chosen, w_uvqk, w_out, gated, w_out_v, sem
):
    fetch = pltpu.make_async_copy(w_out, w_out_v, sem)
    fetch.start()
    rows = events.shape[0]
    own = chosen[...]
    lanes = lax.broadcasted_iota(jnp.int32, (own.shape[0], rows), 1)
    valid = lanes <= limits[:, 0:1]
    for head in range(gated.shape[2] // DH):
        first = head * 4 * DH
        w_part = [w_uvqk[:, first + k * DH : first + (k + 1) * DH] for k in range(4)]
        w_gate_query = jnp.concatenate([w_part[0], w_part[2]], axis=1)
        w_value_key = jnp.concatenate([w_part[1], w_part[3]], axis=1)
        gate_query = jnp.dot(own, w_gate_query, preferred_element_type=jnp.float32)
        gate_query = jax.nn.silu(gate_query).astype(jnp.bfloat16)
        value_key = jnp.dot(events[...], w_value_key, preferred_element_type=jnp.float32)
        value_key = jax.nn.silu(value_key).astype(jnp.bfloat16)
        scores = lax.dot_general(
            gate_query[:, DH:], value_key[:, DH:], NT, preferred_element_type=jnp.float32
        ) / math.sqrt(DH)
        weights = jnp.where(valid, jax.nn.silu(scores), 0.0).astype(jnp.bfloat16)
        attended = jnp.dot(weights, value_key[:, :DH], preferred_element_type=jnp.float32)
        inverse = lax.rsqrt(jnp.mean(attended * attended, axis=-1, keepdims=True) + 1e-06)
        gated_rows = (attended * inverse * gate_query[:, :DH].astype(jnp.float32)).astype(
            jnp.bfloat16
        )
        for k in range(gated.shape[0]):
            gated[k, :, head * DH : (head + 1) * DH] = gated_rows
    fetch.wait()


def score_kernel(sizes, place, wanted, gated, *refs):
    items_axis, dps, tensors = sizes
    chosen, refs = refs[:items_axis], refs[items_axis:]
    w_out, refs = refs[:tensors], refs[tensors:]
    catalogue, refs = list(refs[:dps]), refs[dps:]
    state_hbm, sums, hidden, w_out_v, catalogue_v, w_sems, sems, state_sem = refs
    item, dp, tensor = place[0], place[1], place[2]
    imps = chosen[0].shape[0]
    items = catalogue_v.shape[0]
    step_rows = min(256, items_axis * imps)
    step_items = min(256, items)
    steps = range(0, items, step_items)
    w_fetches = [
        pltpu.make_async_copy(w_out[t], w_out_v.at[t - 1], w_sems.at[t - 1])
        for t in range(1, tensors)
    ]
    parts = [pl.ds(first, step_items) for first in steps]
    fetches = [
        pltpu.make_async_copy(catalogue[0].at[part], catalogue_v.at[part], sems.at[n])
        for n, part in enumerate(parts)
    ]
    for fetch in w_fetches + fetches:
        fetch.start()
    catalogue[0] = catalogue_v

    slot_rounds, tensor_rounds = rounds(items_axis), rounds(tensors)
    totals = [c[...].astype(jnp.float32) for c in chosen]
    for t in range(tensors):
        if t > 0:
            w_fetches[t - 1].wait()
        w_part = w_out[0][...] if t == 0 else w_out_v[t - 1]
        for k in range(items_axis):
            sender = (item ^ slot_rounds[k]) * tensors + (tensor ^ tensor_rounds[t])
            totals[k] += jnp.dot(gated[sender], w_part, preferred_element_type=jnp.float32)
    for k in range(items_axis):
        hidden[k * imps : (k + 1) * imps, :] = totals[k].astype(jnp.bfloat16)
    share = state_hbm.shape[1]
    state_copy = pltpu.make_async_copy(
        hidden.at[pl.ds(0, imps), pl.ds(pl.multiple_of(tensor * share, share), share)],
        state_hbm,
        state_sem,
    )
    state_copy.start()

    blocks = range(0, items_axis * imps, step_rows)
    totals = {row: jnp.zeros((8, step_rows), jnp.float32) for row in blocks}
    targets = dict(totals)
    for d in range(dps):
        item_base = ((item * dps + (dp ^ rounds(dps)[d])) * tensors + tensor) * items
        ids = {row: wanted[0:1, row : row + step_rows] - item_base for row in blocks}
        for first in steps:
            if d == 0:
                fetches[first // step_items].wait()
            for row in blocks:
                logits = lax.dot_general(
                    catalogue[d][first : first + step_items, :],
                    hidden[row : row + step_rows, :],
                    NT,
                    preferred_element_type=jnp.float32,
                )
                item_ids = lax.broadcasted_iota(jnp.int32, logits.shape, 0)
                found = jnp.where(item_ids == ids[row] - first, logits, 0.0)
                totals[row] += jnp.sum(jnp.exp(logits).reshape(-1, 8, step_rows), axis=0)
                targets[row] += jnp.sum(found.reshape(-1, 8, step_rows), axis=0)
    for row in blocks:
        total = jnp.sum(totals[row], axis=0, keepdims=True)
        target = jnp.sum(targets[row], axis=0, keepdims=True)
        for part in range(step_rows // imps):
            owner = item ^ slot_rounds[row // imps + part]
            both = jnp.concatenate(
                [v[:, part * imps : (part + 1) * imps] for v in (total, target)], axis=1
            )
            for t in range(tensors):
                sums[owner * tensors + t] = both
    state_copy.wait()


def in_hbm(x):
    return pltpu.with_memory_space_constraint(x, pltpu.HBM)


def from_others(x, axes, count):
    return [x] + [
        lax.ppermute(x, axes, [(i, i ^ r) for i in range(count)]) for r in rounds(count)[1:]
    ]


def local(events, lengths, packing, positions, logged, w_uvqk, w_out, catalogue):
    rows, width = events.shape
    imps = positions.shape[1]
    hists = packing.shape[0]
    items = catalogue.shape[0]
    local_width = w_out.shape[0]
    items_axis, dps, tensors = (lax.axis_size(a) for a in ("item", "dp", "tensor"))
    receivers = items_axis * tensors
    params = pltpu.CompilerParams(vmem_limit_bytes=VMEM_LIMIT)
    place = jnp.stack([lax.axis_index(a) for a in ("item", "dp", "tensor")]).astype(jnp.int32)
    smem, vmem, hbm = spec(pltpu.SMEM), spec(pltpu.VMEM), spec(pltpu.HBM)

    other_catalogues = from_others(catalogue, "dp", dps)[1:]
    chosen, limits, wanted, events, w_uvqk = pl.pallas_call(
        functools.partial(pick_kernel, (items_axis, dps)),
        out_shape=(
            jax.ShapeDtypeStruct((imps, width), jnp.bfloat16),
            jax.ShapeDtypeStruct((imps, 128), jnp.int32),
            jax.ShapeDtypeStruct((1, items_axis * imps), jnp.int32),
            jax.ShapeDtypeStruct(events.shape, events.dtype),
            jax.ShapeDtypeStruct(w_uvqk.shape, w_uvqk.dtype),
        ),
        in_specs=[smem] + [hbm] * 6,
        out_specs=(vmem,) * 5,
        scratch_shapes=[
            pltpu.SMEM((hists,), jnp.int32),
            pltpu.SMEM((hists,), jnp.int32),
            pltpu.VMEM((hists, imps), jnp.int32),
            pltpu.VMEM((hists, imps), jnp.int32),
            pltpu.SemaphoreType.DMA((5 + EVENT_PARTS,)),
        ],
        compiler_params=params,
        cost_estimate=pl.CostEstimate(
            flops=2 * imps * rows * width, bytes_accessed=2 * rows * width, transcendentals=0
        ),
        name="pick",
    )(place, *(in_hbm(x) for x in (packing, lengths, positions, logged, events, w_uvqk)))
    all_chosen = from_others(chosen, "item", items_axis)

    gated, w_out = pl.pallas_call(
        attend_kernel,
        out_shape=(
            jax.ShapeDtypeStruct((receivers, imps, local_width), jnp.bfloat16),
            jax.ShapeDtypeStruct(w_out.shape, w_out.dtype),
        ),
        in_specs=[vmem] * 4 + [hbm],
        out_specs=(vmem,) * 2,
        scratch_shapes=[pltpu.SemaphoreType.DMA],
        compiler_params=params,
        cost_estimate=pl.CostEstimate(flops=0, bytes_accessed=0, transcendentals=0),
        name="attend",
    )(limits, events, chosen, w_uvqk, in_hbm(w_out))

    def exchange(gated, w_out):
        return (
            lax.all_to_all(gated, COLUMN, split_axis=0, concat_axis=0, tiled=True),
            from_others(w_out, "tensor", tensors)[1:],
        )

    def keep(gated, w_out):
        return gated, [w_out] * (tensors - 1)

    all_gated, other_w_out = lax.cond(lengths[0] > 0, exchange, keep, gated, w_out)

    state, sums = pl.pallas_call(
        functools.partial(score_kernel, (items_axis, dps, tensors)),
        out_shape=(
            jax.ShapeDtypeStruct((imps, width // tensors), jnp.bfloat16),
            jax.ShapeDtypeStruct((receivers, 1, 2 * imps), jnp.float32),
        ),
        in_specs=[smem] + [vmem] * (3 + items_axis) + [hbm] * tensors + [vmem] * (dps - 1),
        out_specs=(hbm, vmem),
        scratch_shapes=[
            pltpu.VMEM((items_axis * imps, width), jnp.bfloat16),
            pltpu.VMEM((max(tensors - 1, 1), local_width, width), jnp.bfloat16),
            pltpu.VMEM((items, width), jnp.bfloat16),
            pltpu.SemaphoreType.DMA((max(tensors - 1, 1),)),
            pltpu.SemaphoreType.DMA((items // min(256, items),)),
            pltpu.SemaphoreType.DMA,
        ],
        compiler_params=params,
        cost_estimate=pl.CostEstimate(
            flops=2 * items_axis * imps * width * (dps * items + local_width * tensors),
            bytes_accessed=2 * dps * items * width,
            transcendentals=items_axis * imps * dps * items,
        ),
        name="score",
    )(
        place,
        wanted,
        all_gated,
        *all_chosen,
        w_out,
        *(in_hbm(x) for x in (*other_w_out, catalogue)),
        *other_catalogues,
    )
    sums = lax.all_to_all(sums, COLUMN, split_axis=0, concat_axis=0, tiled=True)
    sums = jnp.sum(sums, axis=(0, 1))
    return (state, sums[imps:] - jnp.log(sums[:imps]))


def solution(mesh):
    placed = (
        P(("groups", "item", "dp"), None),
        P("groups"),
        P("groups"),
        P("groups", None),
        P("groups", None),
        P(None, "tensor"),
        P("tensor", None),
        P(("item", "dp", "tensor"), None),
    )
    return jax.shard_map(
        local,
        mesh=mesh,
        in_specs=placed,
        out_specs=(P(("groups", "item", "dp"), "tensor"), P(("groups", "item", "dp"))),
        check_vma=False,
    )
```

```python
import functools
import math

import jax
import jax.numpy as jnp
from jax import lax
from jax.experimental import pallas as pl
from jax.experimental.pallas import tpu as pltpu
from jax.sharding import PartitionSpec as P

DH = 128
SLOTS = ("item", "dp")
COLUMN = ("item", "tensor")
NT = (((1,), (1,)), ((), ()))
MIB = 1024 * 1024
EVENT_PARTS = 3


def rounds(count):
    return [0] + sorted(range(1, count), key=lambda r: (r & 3 == 3, -(r & -2)))


def spec(space):
    return pl.BlockSpec(memory_space=space)


def pick_kernel(
    shards,
    place,
    packing,
    lengths,
    positions,
    logged,
    events,
    w_uvqk,
    chosen,
    limits,
    wanted,
    events_v,
    w_uvqk_v,
    packing_s,
    lengths_s,
    positions_v,
    logged_v,
    sems,
):
    rows = events.shape[0]
    items_axis, dps = shards
    imps = positions.shape[1]
    part_rows = rows // EVENT_PARTS
    parts = [pl.ds(k * part_rows, part_rows) for k in range(EVENT_PARTS)]
    copies = [
        pltpu.make_async_copy(source, target, sems.at[k])
        for k, (source, target) in enumerate(
            [
                (packing, packing_s),
                (positions, positions_v),
                (lengths, lengths_s),
                (logged, logged_v),
            ]
            + [(events.at[part], events_v.at[part]) for part in parts]
            + [(w_uvqk, w_uvqk_v)]
        )
    ]
    for copy in copies:
        copy.start()
    for copy in copies[:4]:
        copy.wait()
    item, dp = place[0], place[1]
    history = packing_s[item * dps + dp]
    row = positions_v[pl.ds(history, 1), :].astype(jnp.float32)
    diagonal = lax.broadcasted_iota(jnp.int32, (imps, imps), 0) == lax.broadcasted_iota(
        jnp.int32, (imps, imps), 1
    )
    spots = jnp.sum(jnp.where(diagonal, row, 0.0), axis=1, keepdims=True).astype(jnp.int32)
    limits[...] = jnp.broadcast_to(jnp.minimum(spots, lengths_s[history] - 1), limits.shape)
    for k, r in enumerate(rounds(items_axis)):
        other = packing_s[(item ^ r) * dps + dp]
        wanted[0:1, k * imps : (k + 1) * imps] = logged_v[pl.ds(other, 1), :]
    total = jnp.zeros((imps, events.shape[1]), jnp.float32)
    for k in range(EVENT_PARTS):
        copies[4 + k].wait()
        lanes = k * part_rows + lax.broadcasted_iota(jnp.int32, (imps, part_rows), 1)
        one_hot = jnp.where(lanes == spots, 1.0, 0.0).astype(jnp.bfloat16)
        total += jnp.dot(
            one_hot,
            events_v[k * part_rows : (k + 1) * part_rows, :],
            preferred_element_type=jnp.float32,
        )
    chosen[...] = total.astype(jnp.bfloat16)
    copies[-1].wait()


def attend_kernel(
    limits, events, chosen, w_uvqk, w_out, gated, w_out_v, sem
):
    fetch = pltpu.make_async_copy(w_out, w_out_v, sem)
    fetch.start()
    rows = events.shape[0]
    own = chosen[...]
    lanes = lax.broadcasted_iota(jnp.int32, (own.shape[0], rows), 1)
    valid = lanes <= limits[:, 0:1]
    for head in range(gated.shape[2] // DH):
        first = head * 4 * DH
        w_part = [w_uvqk[:, first + k * DH : first + (k + 1) * DH] for k in range(4)]
        w_gate_query = jnp.concatenate([w_part[0], w_part[2]], axis=1)
        w_value_key = jnp.concatenate([w_part[1], w_part[3]], axis=1)
        gate_query = jnp.dot(own, w_gate_query, preferred_element_type=jnp.float32)
        gate_query = jax.nn.silu(gate_query).astype(jnp.bfloat16)
        value_key = jnp.dot(events[...], w_value_key, preferred_element_type=jnp.float32)
        value_key = jax.nn.silu(value_key).astype(jnp.bfloat16)
        scores = lax.dot_general(
            gate_query[:, DH:], value_key[:, DH:], NT, preferred_element_type=jnp.float32
        ) / math.sqrt(DH)
        weights = jnp.where(valid, jax.nn.silu(scores), 0.0).astype(jnp.bfloat16)
        attended = jnp.dot(weights, value_key[:, :DH], preferred_element_type=jnp.float32)
        inverse = lax.rsqrt(jnp.mean(attended * attended, axis=-1, keepdims=True) + 1e-06)
        gated_rows = (attended * inverse * gate_query[:, :DH].astype(jnp.float32)).astype(
            jnp.bfloat16
        )
        for k in range(gated.shape[0]):
            gated[k, :, head * DH : (head + 1) * DH] = gated_rows
    fetch.wait()


def score_kernel(sizes, place, wanted, gated, *refs):
    items_axis, dps, tensors = sizes
    chosen, refs = refs[:items_axis], refs[items_axis:]
    w_out, refs = refs[:tensors], refs[tensors:]
    catalogue, refs = list(refs[:dps]), refs[dps:]
    state_hbm, sums, hidden, others, sems, state_sem = refs
    fetches = [
        pltpu.make_async_copy(catalogue[d], others.at[d - 1], sems.at[d - 1]) for d in range(1, dps)
    ]
    for fetch in fetches:
        fetch.start()
    catalogue[1:] = [others.at[d - 1] for d in range(1, dps)]
    item, dp, tensor = place[0], place[1], place[2]
    imps = chosen[0].shape[0]
    items = catalogue[0].shape[0]
    step_rows = min(256, items_axis * imps)
    step_items = min(256, items)
    steps = range(0, items, step_items)
    slot_rounds, tensor_rounds = rounds(items_axis), rounds(tensors)
    totals = [c[...].astype(jnp.float32) for c in chosen]
    for t in range(tensors):
        for k in range(items_axis):
            sender = (item ^ slot_rounds[k]) * tensors + (tensor ^ tensor_rounds[t])
            totals[k] += jnp.dot(
                gated[sender], w_out[t][...], preferred_element_type=jnp.float32
            )
    for k in range(items_axis):
        hidden[k * imps : (k + 1) * imps, :] = totals[k].astype(jnp.bfloat16)
    share = state_hbm.shape[1]
    state_copy = pltpu.make_async_copy(
        hidden.at[pl.ds(0, imps), pl.ds(pl.multiple_of(tensor * share, share), share)],
        state_hbm,
        state_sem,
    )
    state_copy.start()

    blocks = range(0, items_axis * imps, step_rows)
    totals = {row: jnp.zeros((8, step_rows), jnp.float32) for row in blocks}
    targets = dict(totals)
    for d in range(dps):
        if d > 0:
            fetches[d - 1].wait()
        item_base = ((item * dps + (dp ^ rounds(dps)[d])) * tensors + tensor) * items
        ids = {row: wanted[0:1, row : row + step_rows] - item_base for row in blocks}
        for first in steps:
            for row in blocks:
                logits = lax.dot_general(
                    catalogue[d][first : first + step_items, :],
                    hidden[row : row + step_rows, :],
                    NT,
                    preferred_element_type=jnp.float32,
                )
                item_ids = lax.broadcasted_iota(jnp.int32, logits.shape, 0)
                found = jnp.where(item_ids == ids[row] - first, logits, 0.0)
                totals[row] += jnp.sum(jnp.exp(logits).reshape(-1, 8, step_rows), axis=0)
                targets[row] += jnp.sum(found.reshape(-1, 8, step_rows), axis=0)
    for row in blocks:
        total = jnp.sum(totals[row], axis=0, keepdims=True)
        target = jnp.sum(targets[row], axis=0, keepdims=True)
        for part in range(step_rows // imps):
            owner = item ^ slot_rounds[row // imps + part]
            both = jnp.concatenate(
                [v[:, part * imps : (part + 1) * imps] for v in (total, target)], axis=1
            )
            for t in range(tensors):
                sums[owner * tensors + t] = both
    state_copy.wait()


def in_hbm(x):
    return pltpu.with_memory_space_constraint(x, pltpu.HBM)


def send(x, axes, count, r):
    return lax.ppermute(x, axes, [(i, i ^ r) for i in range(count)])


def from_others(x, axes, count):
    pieces = {}
    for r in rounds(count)[1:]:
        if r & 3 == 3:
            held, pieces[r - 2] = lax.optimization_barrier((pieces[r - 1], pieces[r - 2]))
            pieces[r] = send(held, axes, count, 1)
        else:
            pieces[r] = send(x, axes, count, r)
    return list(pieces.values())


def local(events, lengths, packing, positions, logged, w_uvqk, w_out, catalogue):
    rows, width = events.shape
    imps = positions.shape[1]
    hists = packing.shape[0]
    items = catalogue.shape[0]
    local_width = w_out.shape[0]
    items_axis, dps, tensors = (lax.axis_size(a) for a in ("item", "dp", "tensor"))
    receivers = items_axis * tensors
    params = pltpu.CompilerParams(vmem_limit_bytes=(12 + 2 * items_axis) * MIB)
    place = jnp.stack([lax.axis_index(a) for a in ("item", "dp", "tensor")]).astype(jnp.int32)
    smem, vmem, hbm = spec(pltpu.SMEM), spec(pltpu.VMEM), spec(pltpu.HBM)

    other_catalogues = from_others(catalogue, "dp", dps)
    other_w_out = from_others(w_out, "tensor", tensors)
    chosen, limits, wanted, events, w_uvqk = pl.pallas_call(
        functools.partial(pick_kernel, (items_axis, dps)),
        out_shape=(
            jax.ShapeDtypeStruct((imps, width), jnp.bfloat16),
            jax.ShapeDtypeStruct((imps, 128), jnp.int32),
            jax.ShapeDtypeStruct((1, items_axis * imps), jnp.int32),
            jax.ShapeDtypeStruct(events.shape, events.dtype),
            jax.ShapeDtypeStruct(w_uvqk.shape, w_uvqk.dtype),
        ),
        in_specs=[smem] + [hbm] * 6,
        out_specs=(vmem,) * 5,
        scratch_shapes=[
            pltpu.SMEM((hists,), jnp.int32),
            pltpu.SMEM((hists,), jnp.int32),
            pltpu.VMEM((hists, imps), jnp.int32),
            pltpu.VMEM((hists, imps), jnp.int32),
            pltpu.SemaphoreType.DMA((5 + EVENT_PARTS,)),
        ],
        compiler_params=params,
        cost_estimate=pl.CostEstimate(
            flops=2 * imps * rows * width, bytes_accessed=2 * rows * width, transcendentals=0
        ),
        name="pick",
    )(place, *(in_hbm(x) for x in (packing, lengths, positions, logged, events, w_uvqk)))
    other_chosen = from_others(chosen, "item", items_axis)

    gated, own_w_out = pl.pallas_call(
        attend_kernel,
        out_shape=(
            jax.ShapeDtypeStruct((receivers, imps, local_width), jnp.bfloat16),
            jax.ShapeDtypeStruct(w_out.shape, w_out.dtype),
        ),
        in_specs=[vmem] * 4 + [hbm],
        out_specs=(vmem,) * 2,
        scratch_shapes=[pltpu.SemaphoreType.DMA],
        compiler_params=params,
        cost_estimate=pl.CostEstimate(flops=0, bytes_accessed=0, transcendentals=0),
        name="attend",
    )(limits, events, chosen, w_uvqk, in_hbm(w_out))

    all_gated = lax.all_to_all(gated, COLUMN, split_axis=0, concat_axis=0, tiled=True)

    state, sums = pl.pallas_call(
        functools.partial(score_kernel, (items_axis, dps, tensors)),
        out_shape=(
            jax.ShapeDtypeStruct((imps, width // tensors), jnp.bfloat16),
            jax.ShapeDtypeStruct((receivers, 1, 2 * imps), jnp.float32),
        ),
        in_specs=[smem] + [vmem] * (3 + items_axis + tensors) + [hbm] * (dps - 1),
        out_specs=(hbm, vmem),
        scratch_shapes=[
            pltpu.VMEM((items_axis * imps, width), jnp.bfloat16),
            pltpu.VMEM((dps - 1, items, width), jnp.bfloat16),
            pltpu.SemaphoreType.DMA((dps - 1,)),
            pltpu.SemaphoreType.DMA,
        ],
        compiler_params=params,
        cost_estimate=pl.CostEstimate(
            flops=2 * items_axis * imps * width * (dps * items + local_width * tensors),
            bytes_accessed=2 * dps * items * width,
            transcendentals=items_axis * imps * dps * items,
        ),
        name="score",
    )(
        place,
        wanted,
        all_gated,
        chosen,
        *other_chosen,
        own_w_out,
        *other_w_out,
        catalogue,
        *(in_hbm(x) for x in other_catalogues),
    )
    sums = lax.all_to_all(sums, COLUMN, split_axis=0, concat_axis=0, tiled=True)
    sums = jnp.sum(sums, axis=(0, 1))
    return (state, sums[imps:] - jnp.log(sums[:imps]))


def solution(mesh):
    placed = (
        P(("groups", "item", "dp"), None),
        P("groups"),
        P("groups"),
        P("groups", None),
        P("groups", None),
        P(None, "tensor"),
        P("tensor", None),
        P(("item", "dp", "tensor"), None),
    )
    return jax.shard_map(
        local,
        mesh=mesh,
        in_specs=placed,
        out_specs=(P(("groups", "item", "dp"), "tensor"), P(("groups", "item", "dp"))),
        check_vma=False,
    )
```

```python
import functools
import math

import jax
import jax.numpy as jnp
from jax import lax
from jax.experimental import pallas as pl
from jax.experimental.pallas import tpu as pltpu
from jax.sharding import PartitionSpec as P

DH = 128
SLOTS = ("item", "dp")
COLUMN = ("item", "tensor")
NT = (((1,), (1,)), ((), ()))
MIB = 1024 * 1024
EVENT_PARTS = 3


def rounds(count):
    return [0] + sorted(range(1, count), key=lambda r: (r & 3 == 3, -(r & -2)))


def spec(space):
    return pl.BlockSpec(memory_space=space)


def pick_kernel(
    shards,
    place,
    packing,
    lengths,
    positions,
    logged,
    events,
    w_uvqk,
    chosen,
    limits,
    wanted,
    events_v,
    w_uvqk_v,
    done,
    packing_s,
    lengths_s,
    positions_v,
    logged_v,
    sems,
):
    rows = events.shape[0]
    items_axis, dps = shards
    imps = positions.shape[1]
    part_rows = rows // EVENT_PARTS
    parts = [pl.ds(k * part_rows, part_rows) for k in range(EVENT_PARTS)]
    copies = [
        pltpu.make_async_copy(source, target, sems.at[k])
        for k, (source, target) in enumerate(
            [
                (packing, packing_s),
                (positions, positions_v),
                (lengths, lengths_s),
                (logged, logged_v),
            ]
            + [(events.at[part], events_v.at[part]) for part in parts]
            + [(w_uvqk, w_uvqk_v)]
        )
    ]
    for copy in copies:
        copy.start()
    for copy in copies[:4]:
        copy.wait()
    item, dp = place[0], place[1]
    history = packing_s[item * dps + dp]
    row = positions_v[pl.ds(history, 1), :].astype(jnp.float32)
    diagonal = lax.broadcasted_iota(jnp.int32, (imps, imps), 0) == lax.broadcasted_iota(
        jnp.int32, (imps, imps), 1
    )
    spots = jnp.sum(jnp.where(diagonal, row, 0.0), axis=1, keepdims=True).astype(jnp.int32)
    limits[...] = jnp.broadcast_to(jnp.minimum(spots, lengths_s[history] - 1), limits.shape)
    for k, r in enumerate(rounds(items_axis)):
        other = packing_s[(item ^ r) * dps + dp]
        wanted[0:1, k * imps : (k + 1) * imps] = logged_v[pl.ds(other, 1), :]
    total = jnp.zeros((imps, events.shape[1]), jnp.float32)
    for k in range(EVENT_PARTS):
        copies[4 + k].wait()
        lanes = k * part_rows + lax.broadcasted_iota(jnp.int32, (imps, part_rows), 1)
        one_hot = jnp.where(lanes == spots, 1.0, 0.0).astype(jnp.bfloat16)
        total += jnp.dot(
            one_hot,
            events_v[k * part_rows : (k + 1) * part_rows, :],
            preferred_element_type=jnp.float32,
        )
    chosen[...] = total.astype(jnp.bfloat16)
    copies[-1].wait()

    @pl.when(item * 2 < items_axis)
    def _():
        attention(limits, events_v, chosen, w_uvqk_v, done)


def attention(limits, events, own, w_uvqk, store):
    lanes = lax.broadcasted_iota(jnp.int32, (own.shape[0], events.shape[0]), 1)
    valid = lanes <= limits[:, 0:1]
    for head in range(w_uvqk.shape[1] // (4 * DH)):
        first = head * 4 * DH
        w_part = [w_uvqk[:, first + k * DH : first + (k + 1) * DH] for k in range(4)]
        w_gate_query = jnp.concatenate([w_part[0], w_part[2]], axis=1)
        w_value_key = jnp.concatenate([w_part[1], w_part[3]], axis=1)
        gate_query = jnp.dot(own[...], w_gate_query, preferred_element_type=jnp.float32)
        gate_query = jax.nn.silu(gate_query).astype(jnp.bfloat16)
        value_key = jnp.dot(events[...], w_value_key, preferred_element_type=jnp.float32)
        value_key = jax.nn.silu(value_key).astype(jnp.bfloat16)
        scores = lax.dot_general(
            gate_query[:, DH:], value_key[:, DH:], NT, preferred_element_type=jnp.float32
        ) / math.sqrt(DH)
        weights = jnp.where(valid, jax.nn.silu(scores), 0.0).astype(jnp.bfloat16)
        attended = jnp.dot(weights, value_key[:, :DH], preferred_element_type=jnp.float32)
        inverse = lax.rsqrt(jnp.mean(attended * attended, axis=-1, keepdims=True) + 1e-06)
        store[:, head * DH : (head + 1) * DH] = (
            attended * inverse * gate_query[:, :DH].astype(jnp.float32)
        ).astype(jnp.bfloat16)


def attend_kernel(
    items_axis, place, limits, events, chosen, w_uvqk, done, w_out, gated, w_out_v, rows, sem
):
    fetch = pltpu.make_async_copy(w_out, w_out_v, sem)
    fetch.start()
    early = place[0] * 2 < items_axis

    @pl.when(early)
    def _():
        rows[...] = done[...]

    @pl.when(jnp.logical_not(early))
    def _():
        attention(limits, events, chosen, w_uvqk, rows)

    for k in range(gated.shape[0]):
        gated[k] = rows[...]
    fetch.wait()


def score_kernel(sizes, place, wanted, gated, *refs):
    items_axis, dps, tensors = sizes
    chosen, refs = refs[:items_axis], refs[items_axis:]
    w_out, refs = refs[:tensors], refs[tensors:]
    catalogue, refs = list(refs[:dps]), refs[dps:]
    state_hbm, sums, hidden, gates, others, sems, state_sem = refs
    fetches = [
        pltpu.make_async_copy(catalogue[d], others.at[d - 1], sems.at[d - 1]) for d in range(1, dps)
    ]
    for fetch in fetches:
        fetch.start()
    catalogue[1:] = [others.at[d - 1] for d in range(1, dps)]
    item, dp, tensor = place[0], place[1], place[2]
    imps = chosen[0].shape[0]
    items = catalogue[0].shape[0]
    step_rows = min(256, items_axis * imps)
    step_items = min(256, items)
    steps = range(0, items, step_items)
    slot_rounds, tensor_rounds = rounds(items_axis), rounds(tensors)
    local_width = w_out[0].shape[0]
    for k in range(items_axis):
        for t in range(tensors):
            sender = (item ^ slot_rounds[k]) * tensors + (tensor ^ tensor_rounds[t])
            gates[k * imps : (k + 1) * imps, t * local_width : (t + 1) * local_width] = gated[sender]
    w_whole = jnp.concatenate([w[...] for w in w_out], axis=0)
    mixed = jnp.dot(gates[...], w_whole, preferred_element_type=jnp.float32)
    for k in range(items_axis):
        rows = slice(k * imps, (k + 1) * imps)
        hidden[rows, :] = (mixed[rows] + chosen[k][...].astype(jnp.float32)).astype(jnp.bfloat16)
    share = state_hbm.shape[1]
    state_copy = pltpu.make_async_copy(
        hidden.at[pl.ds(0, imps), pl.ds(pl.multiple_of(tensor * share, share), share)],
        state_hbm,
        state_sem,
    )
    state_copy.start()

    blocks = range(0, items_axis * imps, step_rows)
    totals = {row: jnp.zeros((8, step_rows), jnp.float32) for row in blocks}
    targets = dict(totals)
    for d in range(dps):
        if d > 0:
            fetches[d - 1].wait()
        item_base = ((item * dps + (dp ^ rounds(dps)[d])) * tensors + tensor) * items
        ids = {row: wanted[0:1, row : row + step_rows] - item_base for row in blocks}
        for first in steps:
            for row in blocks:
                logits = lax.dot_general(
                    catalogue[d][first : first + step_items, :],
                    hidden[row : row + step_rows, :],
                    NT,
                    preferred_element_type=jnp.float32,
                )
                item_ids = lax.broadcasted_iota(jnp.int32, logits.shape, 0)
                found = jnp.where(item_ids == ids[row] - first, logits, 0.0)
                totals[row] += jnp.sum(jnp.exp(logits).reshape(-1, 8, step_rows), axis=0)
                targets[row] += jnp.sum(found.reshape(-1, 8, step_rows), axis=0)
    for row in blocks:
        total = jnp.sum(totals[row], axis=0, keepdims=True)
        target = jnp.sum(targets[row], axis=0, keepdims=True)
        for part in range(step_rows // imps):
            owner = item ^ slot_rounds[row // imps + part]
            both = jnp.concatenate(
                [v[:, part * imps : (part + 1) * imps] for v in (total, target)], axis=1
            )
            for t in range(tensors):
                sums[owner * tensors + t] = both
    state_copy.wait()


def in_hbm(x):
    return pltpu.with_memory_space_constraint(x, pltpu.HBM)


def send(x, axes, count, r):
    return lax.ppermute(x, axes, [(i, i ^ r) for i in range(count)])


def from_others(x, axes, count):
    pieces = {}
    for r in rounds(count)[1:]:
        if r & 3 == 3:
            held, pieces[r - 2] = lax.optimization_barrier((pieces[r - 1], pieces[r - 2]))
            pieces[r] = send(held, axes, count, 1)
        else:
            pieces[r] = send(x, axes, count, r)
    return list(pieces.values())


def local(events, lengths, packing, positions, logged, w_uvqk, w_out, catalogue):
    rows, width = events.shape
    imps = positions.shape[1]
    hists = packing.shape[0]
    items = catalogue.shape[0]
    local_width = w_out.shape[0]
    items_axis, dps, tensors = (lax.axis_size(a) for a in ("item", "dp", "tensor"))
    receivers = items_axis * tensors
    params = pltpu.CompilerParams(vmem_limit_bytes=(12 + 2 * items_axis) * MIB)
    place = jnp.stack([lax.axis_index(a) for a in ("item", "dp", "tensor")]).astype(jnp.int32)
    smem, vmem, hbm = spec(pltpu.SMEM), spec(pltpu.VMEM), spec(pltpu.HBM)

    other_catalogues = from_others(catalogue, "dp", dps)
    other_w_out = from_others(w_out, "tensor", tensors)
    chosen, limits, wanted, events, w_uvqk, done = pl.pallas_call(
        functools.partial(pick_kernel, (items_axis, dps)),
        out_shape=(
            jax.ShapeDtypeStruct((imps, width), jnp.bfloat16),
            jax.ShapeDtypeStruct((imps, 128), jnp.int32),
            jax.ShapeDtypeStruct((1, items_axis * imps), jnp.int32),
            jax.ShapeDtypeStruct(events.shape, events.dtype),
            jax.ShapeDtypeStruct(w_uvqk.shape, w_uvqk.dtype),
            jax.ShapeDtypeStruct((imps, local_width), jnp.bfloat16),
        ),
        in_specs=[smem] + [hbm] * 6,
        out_specs=(vmem,) * 6,
        scratch_shapes=[
            pltpu.SMEM((hists,), jnp.int32),
            pltpu.SMEM((hists,), jnp.int32),
            pltpu.VMEM((hists, imps), jnp.int32),
            pltpu.VMEM((hists, imps), jnp.int32),
            pltpu.SemaphoreType.DMA((5 + EVENT_PARTS,)),
        ],
        compiler_params=params,
        cost_estimate=pl.CostEstimate(
            flops=2 * imps * rows * width, bytes_accessed=2 * rows * width, transcendentals=0
        ),
        name="pick",
    )(place, *(in_hbm(x) for x in (packing, lengths, positions, logged, events, w_uvqk)))
    other_chosen = from_others(chosen, "item", items_axis)

    gated, own_w_out = pl.pallas_call(
        functools.partial(attend_kernel, items_axis),
        out_shape=(
            jax.ShapeDtypeStruct((receivers, imps, local_width), jnp.bfloat16),
            jax.ShapeDtypeStruct(w_out.shape, w_out.dtype),
        ),
        in_specs=[smem] + [vmem] * 5 + [hbm],
        out_specs=(vmem,) * 2,
        scratch_shapes=[
            pltpu.VMEM((imps, local_width), jnp.bfloat16),
            pltpu.SemaphoreType.DMA,
        ],
        compiler_params=params,
        cost_estimate=pl.CostEstimate(flops=0, bytes_accessed=0, transcendentals=0),
        name="attend",
    )(place, limits, events, chosen, w_uvqk, done, in_hbm(w_out))

    all_gated = lax.all_to_all(gated, COLUMN, split_axis=0, concat_axis=0, tiled=True)

    state, sums = pl.pallas_call(
        functools.partial(score_kernel, (items_axis, dps, tensors)),
        out_shape=(
            jax.ShapeDtypeStruct((imps, width // tensors), jnp.bfloat16),
            jax.ShapeDtypeStruct((receivers, 1, 2 * imps), jnp.float32),
        ),
        in_specs=[smem] + [vmem] * (3 + items_axis + tensors) + [hbm] * (dps - 1),
        out_specs=(hbm, vmem),
        scratch_shapes=[
            pltpu.VMEM((items_axis * imps, width), jnp.bfloat16),
            pltpu.VMEM((items_axis * imps, local_width * tensors), jnp.bfloat16),
            pltpu.VMEM((dps - 1, items, width), jnp.bfloat16),
            pltpu.SemaphoreType.DMA((dps - 1,)),
            pltpu.SemaphoreType.DMA,
        ],
        compiler_params=params,
        cost_estimate=pl.CostEstimate(
            flops=2 * items_axis * imps * width * (dps * items + local_width * tensors),
            bytes_accessed=2 * dps * items * width,
            transcendentals=items_axis * imps * dps * items,
        ),
        name="score",
    )(
        place,
        wanted,
        all_gated,
        chosen,
        *other_chosen,
        own_w_out,
        *other_w_out,
        catalogue,
        *(in_hbm(x) for x in other_catalogues),
    )
    sums = lax.all_to_all(sums, COLUMN, split_axis=0, concat_axis=0, tiled=True)
    sums = jnp.sum(sums, axis=(0, 1))
    return (state, sums[imps:] - jnp.log(sums[:imps]))


def solution(mesh):
    placed = (
        P(("groups", "item", "dp"), None),
        P("groups"),
        P("groups"),
        P("groups", None),
        P("groups", None),
        P(None, "tensor"),
        P("tensor", None),
        P(("item", "dp", "tensor"), None),
    )
    return jax.shard_map(
        local,
        mesh=mesh,
        in_specs=placed,
        out_specs=(P(("groups", "item", "dp"), "tensor"), P(("groups", "item", "dp"))),
        check_vma=False,
    )
```

```python
import functools
import math

import jax
import jax.numpy as jnp
from jax import lax
from jax.experimental import pallas as pl
from jax.experimental.pallas import tpu as pltpu
from jax.sharding import PartitionSpec as P

DH = 128
SLOTS = ("item", "dp")
COLUMN = ("item", "tensor")
NT = (((1,), (1,)), ((), ()))
MIB = 1024 * 1024
EVENT_PARTS = 3


def rounds(count):
    return [0] + sorted(range(1, count), key=lambda r: (r & 3 == 3, -(r & -2)))


def spec(space):
    return pl.BlockSpec(memory_space=space)


def pick_kernel(
    shards,
    place,
    packing,
    lengths,
    positions,
    logged,
    events,
    w_uvqk,
    chosen,
    limits,
    wanted,
    events_v,
    w_uvqk_v,
    gated,
    gated_rows,
    packing_s,
    lengths_s,
    positions_v,
    logged_v,
    sems,
    gated_sems,
):
    rows = events.shape[0]
    items_axis, dps = shards
    imps = positions.shape[1]
    part_rows = rows // EVENT_PARTS
    parts = [pl.ds(k * part_rows, part_rows) for k in range(EVENT_PARTS)]
    copies = [
        pltpu.make_async_copy(source, target, sems.at[k])
        for k, (source, target) in enumerate(
            [
                (packing, packing_s),
                (positions, positions_v),
                (lengths, lengths_s),
                (logged, logged_v),
            ]
            + [(events.at[part], events_v.at[part]) for part in parts]
            + [(w_uvqk, w_uvqk_v)]
        )
    ]
    for copy in copies:
        copy.start()
    for copy in copies[:4]:
        copy.wait()
    item, dp = place[0], place[1]
    history = packing_s[item * dps + dp]
    row = positions_v[pl.ds(history, 1), :].astype(jnp.float32)
    diagonal = lax.broadcasted_iota(jnp.int32, (imps, imps), 0) == lax.broadcasted_iota(
        jnp.int32, (imps, imps), 1
    )
    spots = jnp.sum(jnp.where(diagonal, row, 0.0), axis=1, keepdims=True).astype(jnp.int32)
    limits[...] = jnp.broadcast_to(jnp.minimum(spots, lengths_s[history] - 1), limits.shape)
    for k, r in enumerate(rounds(items_axis)):
        other = packing_s[(item ^ r) * dps + dp]
        wanted[0:1, k * imps : (k + 1) * imps] = logged_v[pl.ds(other, 1), :]
    total = jnp.zeros((imps, events.shape[1]), jnp.float32)
    for k in range(EVENT_PARTS):
        copies[4 + k].wait()
        lanes = k * part_rows + lax.broadcasted_iota(jnp.int32, (imps, part_rows), 1)
        one_hot = jnp.where(lanes == spots, 1.0, 0.0).astype(jnp.bfloat16)
        total += jnp.dot(
            one_hot,
            events_v[k * part_rows : (k + 1) * part_rows, :],
            preferred_element_type=jnp.float32,
        )
    chosen[...] = total.astype(jnp.bfloat16)
    copies[-1].wait()

    @pl.when(is_early(item, items_axis))
    def _():
        attention(limits, events_v, chosen, w_uvqk_v, gated_rows)
        hand_out(gated_rows, gated, gated_sems)


def attention(limits, events, own, w_uvqk, store):
    lanes = lax.broadcasted_iota(jnp.int32, (own.shape[0], events.shape[0]), 1)
    valid = lanes <= limits[:, 0:1]
    for head in range(w_uvqk.shape[1] // (4 * DH)):
        first = head * 4 * DH
        w_part = [w_uvqk[:, first + k * DH : first + (k + 1) * DH] for k in range(4)]
        w_gate_query = jnp.concatenate([w_part[0], w_part[2]], axis=1)
        w_value_key = jnp.concatenate([w_part[1], w_part[3]], axis=1)
        gate_query = jnp.dot(own[...], w_gate_query, preferred_element_type=jnp.float32)
        gate_query = jax.nn.silu(gate_query).astype(jnp.bfloat16)
        value_key = jnp.dot(events[...], w_value_key, preferred_element_type=jnp.float32)
        value_key = jax.nn.silu(value_key).astype(jnp.bfloat16)
        scores = lax.dot_general(
            gate_query[:, DH:], value_key[:, DH:], NT, preferred_element_type=jnp.float32
        ) / math.sqrt(DH)
        weights = jnp.where(valid, jax.nn.silu(scores), 0.0).astype(jnp.bfloat16)
        attended = jnp.dot(weights, value_key[:, :DH], preferred_element_type=jnp.float32)
        inverse = lax.rsqrt(jnp.mean(attended * attended, axis=-1, keepdims=True) + 1e-06)
        store[:, head * DH : (head + 1) * DH] = (
            attended * inverse * gate_query[:, :DH].astype(jnp.float32)
        ).astype(jnp.bfloat16)


def is_early(item, items_axis):
    return item * 4 < items_axis


def hand_out(rows, gated, sems):
    copies = [pltpu.make_async_copy(rows, gated.at[k], sems.at[k]) for k in range(gated.shape[0])]
    for copy in copies:
        copy.start()
    for copy in copies:
        copy.wait()


def attend_kernel(
    items_axis, place, limits, events, chosen, w_uvqk, gated_in, gated, rows, sems
):
    del gated_in

    @pl.when(jnp.logical_not(is_early(place[0], items_axis)))
    def _():
        attention(limits, events, chosen, w_uvqk, rows)
        hand_out(rows, gated, sems)


def score_kernel(sizes, place, wanted, gated, *refs):
    items_axis, dps, tensors = sizes
    chosen, refs = refs[:items_axis], refs[items_axis:]
    w_out, refs = refs[:tensors], refs[tensors:]
    catalogue, refs = list(refs[:dps]), refs[dps:]
    state_hbm, sums, hidden, gates, others, sems, state_sem = refs
    fetches = [
        pltpu.make_async_copy(catalogue[d], others.at[d - 1], sems.at[d - 1]) for d in range(1, dps)
    ]
    for fetch in fetches:
        fetch.start()
    catalogue[1:] = [others.at[d - 1] for d in range(1, dps)]
    item, dp, tensor = place[0], place[1], place[2]
    imps = chosen[0].shape[0]
    items = catalogue[0].shape[0]
    step_rows = min(256, items_axis * imps)
    step_items = min(256, items)
    steps = range(0, items, step_items)
    slot_rounds, tensor_rounds = rounds(items_axis), rounds(tensors)
    local_width = w_out[0].shape[0]
    for k in range(items_axis):
        for t in range(tensors):
            sender = (item ^ slot_rounds[k]) * tensors + (tensor ^ tensor_rounds[t])
            gates[k * imps : (k + 1) * imps, t * local_width : (t + 1) * local_width] = gated[sender]
    w_whole = jnp.concatenate([w[...] for w in w_out], axis=0)
    mixed = jnp.dot(gates[...], w_whole, preferred_element_type=jnp.float32)
    for k in range(items_axis):
        rows = slice(k * imps, (k + 1) * imps)
        hidden[rows, :] = (mixed[rows] + chosen[k][...].astype(jnp.float32)).astype(jnp.bfloat16)
    share = state_hbm.shape[1]
    state_copy = pltpu.make_async_copy(
        hidden.at[pl.ds(0, imps), pl.ds(pl.multiple_of(tensor * share, share), share)],
        state_hbm,
        state_sem,
    )
    state_copy.start()

    blocks = range(0, items_axis * imps, step_rows)
    totals = {row: jnp.zeros((8, step_rows), jnp.float32) for row in blocks}
    targets = dict(totals)
    for d in range(dps):
        if d > 0:
            fetches[d - 1].wait()
        item_base = ((item * dps + (dp ^ rounds(dps)[d])) * tensors + tensor) * items
        ids = {row: wanted[0:1, row : row + step_rows] - item_base for row in blocks}
        for first in steps:
            for row in blocks:
                logits = lax.dot_general(
                    catalogue[d][first : first + step_items, :],
                    hidden[row : row + step_rows, :],
                    NT,
                    preferred_element_type=jnp.float32,
                )
                item_ids = lax.broadcasted_iota(jnp.int32, logits.shape, 0)
                found = jnp.where(item_ids == ids[row] - first, logits, 0.0)
                totals[row] += jnp.sum(jnp.exp(logits).reshape(-1, 8, step_rows), axis=0)
                targets[row] += jnp.sum(found.reshape(-1, 8, step_rows), axis=0)
    for row in blocks:
        total = jnp.sum(totals[row], axis=0, keepdims=True)
        target = jnp.sum(targets[row], axis=0, keepdims=True)
        for part in range(step_rows // imps):
            owner = item ^ slot_rounds[row // imps + part]
            both = jnp.concatenate(
                [v[:, part * imps : (part + 1) * imps] for v in (total, target)], axis=1
            )
            for t in range(tensors):
                sums[owner * tensors + t] = both
    state_copy.wait()


def in_hbm(x):
    return pltpu.with_memory_space_constraint(x, pltpu.HBM)


def send(x, axes, count, r):
    return lax.ppermute(x, axes, [(i, i ^ r) for i in range(count)])


def from_others(x, axes, count):
    pieces = {}
    for r in rounds(count)[1:]:
        if r & 3 == 3:
            held, pieces[r - 2] = lax.optimization_barrier((pieces[r - 1], pieces[r - 2]))
            pieces[r] = send(held, axes, count, 1)
        else:
            pieces[r] = send(x, axes, count, r)
    return list(pieces.values())


def local(events, lengths, packing, positions, logged, w_uvqk, w_out, catalogue):
    rows, width = events.shape
    imps = positions.shape[1]
    hists = packing.shape[0]
    items = catalogue.shape[0]
    local_width = w_out.shape[0]
    items_axis, dps, tensors = (lax.axis_size(a) for a in ("item", "dp", "tensor"))
    receivers = items_axis * tensors
    params = pltpu.CompilerParams(vmem_limit_bytes=(12 + 2 * items_axis) * MIB)
    place = jnp.stack([lax.axis_index(a) for a in ("item", "dp", "tensor")]).astype(jnp.int32)
    smem, vmem, hbm = spec(pltpu.SMEM), spec(pltpu.VMEM), spec(pltpu.HBM)

    other_catalogues = from_others(catalogue, "dp", dps)
    other_w_out = from_others(w_out, "tensor", tensors)
    chosen, limits, wanted, events, w_uvqk, gated = pl.pallas_call(
        functools.partial(pick_kernel, (items_axis, dps)),
        out_shape=(
            jax.ShapeDtypeStruct((imps, width), jnp.bfloat16),
            jax.ShapeDtypeStruct((imps, 128), jnp.int32),
            jax.ShapeDtypeStruct((1, items_axis * imps), jnp.int32),
            jax.ShapeDtypeStruct(events.shape, events.dtype),
            jax.ShapeDtypeStruct(w_uvqk.shape, w_uvqk.dtype),
            pltpu.HBM((receivers, imps, local_width), jnp.bfloat16),
        ),
        in_specs=[smem] + [hbm] * 6,
        out_specs=(vmem,) * 5 + (hbm,),
        scratch_shapes=[
            pltpu.VMEM((imps, local_width), jnp.bfloat16),
            pltpu.SMEM((hists,), jnp.int32),
            pltpu.SMEM((hists,), jnp.int32),
            pltpu.VMEM((hists, imps), jnp.int32),
            pltpu.VMEM((hists, imps), jnp.int32),
            pltpu.SemaphoreType.DMA((5 + EVENT_PARTS,)),
            pltpu.SemaphoreType.DMA((receivers,)),
        ],
        compiler_params=params,
        cost_estimate=pl.CostEstimate(
            flops=2 * imps * rows * width, bytes_accessed=2 * rows * width, transcendentals=0
        ),
        name="pick",
    )(place, *(in_hbm(x) for x in (packing, lengths, positions, logged, events, w_uvqk)))
    other_chosen = from_others(chosen, "item", items_axis)

    gated = pl.pallas_call(
        functools.partial(attend_kernel, items_axis),
        out_shape=jax.ShapeDtypeStruct(gated.shape, gated.dtype),
        in_specs=[smem] + [vmem] * 4 + [hbm],
        out_specs=hbm,
        scratch_shapes=[
            pltpu.VMEM((imps, local_width), jnp.bfloat16),
            pltpu.SemaphoreType.DMA((receivers,)),
        ],
        input_output_aliases={5: 0},
        compiler_params=params,
        cost_estimate=pl.CostEstimate(flops=0, bytes_accessed=0, transcendentals=0),
        name="attend",
    )(place, limits, events, chosen, w_uvqk, in_hbm(gated))
    all_gated = lax.all_to_all(gated, COLUMN, split_axis=0, concat_axis=0, tiled=True)

    state, sums = pl.pallas_call(
        functools.partial(score_kernel, (items_axis, dps, tensors)),
        out_shape=(
            jax.ShapeDtypeStruct((imps, width // tensors), jnp.bfloat16),
            jax.ShapeDtypeStruct((receivers, 1, 2 * imps), jnp.float32),
        ),
        in_specs=[smem] + [vmem] * (3 + items_axis + tensors) + [hbm] * (dps - 1),
        out_specs=(hbm, vmem),
        scratch_shapes=[
            pltpu.VMEM((items_axis * imps, width), jnp.bfloat16),
            pltpu.VMEM((items_axis * imps, local_width * tensors), jnp.bfloat16),
            pltpu.VMEM((dps - 1, items, width), jnp.bfloat16),
            pltpu.SemaphoreType.DMA((dps - 1,)),
            pltpu.SemaphoreType.DMA,
        ],
        compiler_params=params,
        cost_estimate=pl.CostEstimate(
            flops=2 * items_axis * imps * width * (dps * items + local_width * tensors),
            bytes_accessed=2 * dps * items * width,
            transcendentals=items_axis * imps * dps * items,
        ),
        name="score",
    )(
        place,
        wanted,
        all_gated,
        chosen,
        *other_chosen,
        w_out,
        *other_w_out,
        catalogue,
        *(in_hbm(x) for x in other_catalogues),
    )
    sums = lax.all_to_all(sums, COLUMN, split_axis=0, concat_axis=0, tiled=True)
    sums = jnp.sum(sums, axis=(0, 1))
    return (state, sums[imps:] - jnp.log(sums[:imps]))


def solution(mesh):
    placed = (
        P(("groups", "item", "dp"), None),
        P("groups"),
        P("groups"),
        P("groups", None),
        P("groups", None),
        P(None, "tensor"),
        P("tensor", None),
        P(("item", "dp", "tensor"), None),
    )
    return jax.shard_map(
        local,
        mesh=mesh,
        in_specs=placed,
        out_specs=(P(("groups", "item", "dp"), "tensor"), P(("groups", "item", "dp"))),
        check_vma=False,
    )
```

```python
import functools
import math

import jax
import jax.numpy as jnp
from jax import lax
from jax.experimental import pallas as pl
from jax.experimental.pallas import tpu as pltpu
from jax.sharding import PartitionSpec as P

DH = 128
SLOTS = ("item", "dp")
COLUMN = ("item", "tensor")
NT = (((1,), (1,)), ((), ()))
MIB = 1024 * 1024
EVENT_PARTS = 3


def rounds(count):
    return [0] + sorted(range(1, count), key=lambda r: (r & 3 == 3, -(r & -2)))


def spec(space):
    return pl.BlockSpec(memory_space=space)


def pick_kernel(
    shards,
    packing,
    lengths,
    positions,
    logged,
    events,
    w_uvqk,
    chosen,
    limits,
    wanted,
    events_v,
    w_uvqk_v,
    gated,
    gated_rows,
    packing_s,
    lengths_s,
    positions_v,
    logged_v,
    sems,
    gated_sems,
):
    rows = events.shape[0]
    items_axis, dps = shards
    imps = positions.shape[1]
    part_rows = rows // EVENT_PARTS
    parts = [pl.ds(k * part_rows, part_rows) for k in range(EVENT_PARTS)]
    copies = [
        pltpu.make_async_copy(source, target, sems.at[k])
        for k, (source, target) in enumerate(
            [
                (packing, packing_s),
                (positions, positions_v),
                (lengths, lengths_s),
                (logged, logged_v),
            ]
            + [(events.at[part], events_v.at[part]) for part in parts]
            + [(w_uvqk, w_uvqk_v)]
        )
    ]
    for copy in copies:
        copy.start()
    for copy in copies[:4]:
        copy.wait()
    item, dp = lax.axis_index("item"), lax.axis_index("dp")
    history = packing_s[item * dps + dp]
    row = positions_v[pl.ds(history, 1), :].astype(jnp.float32)
    diagonal = lax.broadcasted_iota(jnp.int32, (imps, imps), 0) == lax.broadcasted_iota(
        jnp.int32, (imps, imps), 1
    )
    spots = jnp.sum(jnp.where(diagonal, row, 0.0), axis=1, keepdims=True).astype(jnp.int32)
    limits[...] = jnp.broadcast_to(jnp.minimum(spots, lengths_s[history] - 1), limits.shape)
    for k, r in enumerate(rounds(items_axis)):
        other = packing_s[(item ^ r) * dps + dp]
        wanted[0:1, k * imps : (k + 1) * imps] = logged_v[pl.ds(other, 1), :]
    total = jnp.zeros((imps, events.shape[1]), jnp.float32)
    for k in range(EVENT_PARTS):
        copies[4 + k].wait()
        lanes = k * part_rows + lax.broadcasted_iota(jnp.int32, (imps, part_rows), 1)
        one_hot = jnp.where(lanes == spots, 1.0, 0.0).astype(jnp.bfloat16)
        total += jnp.dot(
            one_hot,
            events_v[k * part_rows : (k + 1) * part_rows, :],
            preferred_element_type=jnp.float32,
        )
    chosen[...] = total.astype(jnp.bfloat16)
    copies[-1].wait()

    @pl.when(is_early(item, items_axis))
    def _():
        attention(limits, events_v, chosen, w_uvqk_v, gated_rows)
        hand_out(gated_rows, gated, gated_sems)


def attention(limits, events, own, w_uvqk, store):
    lanes = lax.broadcasted_iota(jnp.int32, (own.shape[0], events.shape[0]), 1)
    valid = lanes <= limits[:, 0:1]
    for head in range(w_uvqk.shape[1] // (4 * DH)):
        first = head * 4 * DH
        w_part = [w_uvqk[:, first + k * DH : first + (k + 1) * DH] for k in range(4)]
        w_gate_query = jnp.concatenate([w_part[0], w_part[2]], axis=1)
        w_value_key = jnp.concatenate([w_part[1], w_part[3]], axis=1)
        gate_query = jnp.dot(own[...], w_gate_query, preferred_element_type=jnp.float32)
        gate_query = jax.nn.silu(gate_query).astype(jnp.bfloat16)
        value_key = jnp.dot(events[...], w_value_key, preferred_element_type=jnp.float32)
        value_key = jax.nn.silu(value_key).astype(jnp.bfloat16)
        scores = lax.dot_general(
            gate_query[:, DH:], value_key[:, DH:], NT, preferred_element_type=jnp.float32
        ) / math.sqrt(DH)
        weights = jnp.where(valid, jax.nn.silu(scores), 0.0).astype(jnp.bfloat16)
        attended = jnp.dot(weights, value_key[:, :DH], preferred_element_type=jnp.float32)
        inverse = lax.rsqrt(jnp.mean(attended * attended, axis=-1, keepdims=True) + 1e-06)
        store[:, head * DH : (head + 1) * DH] = (
            attended * inverse * gate_query[:, :DH].astype(jnp.float32)
        ).astype(jnp.bfloat16)


def is_early(item, items_axis):
    return item * 4 < items_axis


def hand_out(rows, gated, sems):
    copies = [pltpu.make_async_copy(rows, gated.at[k], sems.at[k]) for k in range(gated.shape[0])]
    for copy in copies:
        copy.start()
    for copy in copies:
        copy.wait()


def attend_kernel(
    items_axis, limits, events, chosen, w_uvqk, gated_in, gated, rows, sems
):
    del gated_in

    @pl.when(jnp.logical_not(is_early(lax.axis_index("item"), items_axis)))
    def _():
        attention(limits, events, chosen, w_uvqk, rows)
        hand_out(rows, gated, sems)


def score_kernel(sizes, wanted, gated, *refs):
    items_axis, dps, tensors = sizes
    chosen, refs = refs[:items_axis], refs[items_axis:]
    w_out, refs = refs[:tensors], refs[tensors:]
    catalogue, refs = list(refs[:dps]), refs[dps:]
    state_hbm, sums, hidden, gates, others, sems, state_sem = refs
    fetches = [
        pltpu.make_async_copy(catalogue[d], others.at[d - 1], sems.at[d - 1]) for d in range(1, dps)
    ]
    for fetch in fetches:
        fetch.start()
    catalogue[1:] = [others.at[d - 1] for d in range(1, dps)]
    item, dp, tensor = (lax.axis_index(a) for a in ("item", "dp", "tensor"))
    imps = chosen[0].shape[0]
    items = catalogue[0].shape[0]
    step_rows = min(256, items_axis * imps)
    step_items = min(256, items)
    steps = range(0, items, step_items)
    slot_rounds, tensor_rounds = rounds(items_axis), rounds(tensors)
    local_width = w_out[0].shape[0]
    for k in range(items_axis):
        for t in range(tensors):
            sender = (item ^ slot_rounds[k]) * tensors + (tensor ^ tensor_rounds[t])
            gates[k * imps : (k + 1) * imps, t * local_width : (t + 1) * local_width] = gated[sender]
    w_whole = jnp.concatenate([w[...] for w in w_out], axis=0)
    mixed = jnp.dot(gates[...], w_whole, preferred_element_type=jnp.float32)
    for k in range(items_axis):
        rows = slice(k * imps, (k + 1) * imps)
        hidden[rows, :] = (mixed[rows] + chosen[k][...].astype(jnp.float32)).astype(jnp.bfloat16)
    share = state_hbm.shape[1]
    state_copy = pltpu.make_async_copy(
        hidden.at[pl.ds(0, imps), pl.ds(pl.multiple_of(tensor * share, share), share)],
        state_hbm,
        state_sem,
    )
    state_copy.start()

    blocks = range(0, items_axis * imps, step_rows)
    totals = {row: jnp.zeros((8, step_rows), jnp.float32) for row in blocks}
    targets = dict(totals)
    for d in range(dps):
        if d > 0:
            fetches[d - 1].wait()
        item_base = ((item * dps + (dp ^ rounds(dps)[d])) * tensors + tensor) * items
        ids = {row: wanted[0:1, row : row + step_rows] - item_base for row in blocks}
        for first in steps:
            for row in blocks:
                logits = lax.dot_general(
                    catalogue[d][first : first + step_items, :],
                    hidden[row : row + step_rows, :],
                    NT,
                    preferred_element_type=jnp.float32,
                )
                item_ids = lax.broadcasted_iota(jnp.int32, logits.shape, 0)
                found = jnp.where(item_ids == ids[row] - first, logits, 0.0)
                totals[row] += jnp.sum(jnp.exp(logits).reshape(-1, 8, step_rows), axis=0)
                targets[row] += jnp.sum(found.reshape(-1, 8, step_rows), axis=0)
    for row in blocks:
        total = jnp.sum(totals[row], axis=0, keepdims=True)
        target = jnp.sum(targets[row], axis=0, keepdims=True)
        for part in range(step_rows // imps):
            owner = item ^ slot_rounds[row // imps + part]
            both = jnp.concatenate(
                [v[:, part * imps : (part + 1) * imps] for v in (total, target)], axis=1
            )
            for t in range(tensors):
                sums[owner * tensors + t] = both
    state_copy.wait()


def in_hbm(x):
    return pltpu.with_memory_space_constraint(x, pltpu.HBM)


def send(x, axes, count, r):
    return lax.ppermute(x, axes, [(i, i ^ r) for i in range(count)])


def from_others(x, axes, count, beside=()):
    pieces = {}
    for r in rounds(count)[1:]:
        if r & 3 == 3:
            held, pieces[r - 2], beside = lax.optimization_barrier(
                (pieces[r - 1], pieces[r - 2], beside)
            )
            pieces[r] = send(held, axes, count, 1)
        else:
            pieces[r] = send(x, axes, count, r)
    return list(pieces.values()), beside


def local(events, lengths, packing, positions, logged, w_uvqk, w_out, catalogue):
    rows, width = events.shape
    imps = positions.shape[1]
    hists = packing.shape[0]
    items = catalogue.shape[0]
    local_width = w_out.shape[0]
    items_axis, dps, tensors = (lax.axis_size(a) for a in ("item", "dp", "tensor"))
    receivers = items_axis * tensors
    params = pltpu.CompilerParams(vmem_limit_bytes=(12 + 2 * items_axis) * MIB)
    vmem, hbm = spec(pltpu.VMEM), spec(pltpu.HBM)

    other_catalogues, _ = from_others(catalogue, "dp", dps)
    other_w_out, _ = from_others(w_out, "tensor", tensors)
    chosen, limits, wanted, events, w_uvqk, gated = pl.pallas_call(
        functools.partial(pick_kernel, (items_axis, dps)),
        out_shape=(
            jax.ShapeDtypeStruct((imps, width), jnp.bfloat16),
            jax.ShapeDtypeStruct((imps, 128), jnp.int32),
            jax.ShapeDtypeStruct((1, items_axis * imps), jnp.int32),
            jax.ShapeDtypeStruct(events.shape, events.dtype),
            jax.ShapeDtypeStruct(w_uvqk.shape, w_uvqk.dtype),
            pltpu.HBM((receivers, imps, local_width), jnp.bfloat16),
        ),
        in_specs=[hbm] * 6,
        out_specs=(vmem,) * 5 + (hbm,),
        scratch_shapes=[
            pltpu.VMEM((imps, local_width), jnp.bfloat16),
            pltpu.SMEM((hists,), jnp.int32),
            pltpu.SMEM((hists,), jnp.int32),
            pltpu.VMEM((hists, imps), jnp.int32),
            pltpu.VMEM((hists, imps), jnp.int32),
            pltpu.SemaphoreType.DMA((5 + EVENT_PARTS,)),
            pltpu.SemaphoreType.DMA((receivers,)),
        ],
        compiler_params=params,
        cost_estimate=pl.CostEstimate(
            flops=2 * imps * rows * width, bytes_accessed=2 * rows * width, transcendentals=0
        ),
        name="pick",
    )(*(in_hbm(x) for x in (packing, lengths, positions, logged, events, w_uvqk)))
    other_chosen, other_w_out = from_others(chosen, "item", items_axis, other_w_out)

    gated = pl.pallas_call(
        functools.partial(attend_kernel, items_axis),
        out_shape=jax.ShapeDtypeStruct(gated.shape, gated.dtype),
        in_specs=[vmem] * 4 + [hbm],
        out_specs=hbm,
        scratch_shapes=[
            pltpu.VMEM((imps, local_width), jnp.bfloat16),
            pltpu.SemaphoreType.DMA((receivers,)),
        ],
        input_output_aliases={4: 0},
        compiler_params=params,
        cost_estimate=pl.CostEstimate(flops=0, bytes_accessed=0, transcendentals=0),
        name="attend",
    )(limits, events, chosen, w_uvqk, in_hbm(gated))
    all_gated = lax.all_to_all(gated, COLUMN, split_axis=0, concat_axis=0, tiled=True)

    state, sums = pl.pallas_call(
        functools.partial(score_kernel, (items_axis, dps, tensors)),
        out_shape=(
            jax.ShapeDtypeStruct((imps, width // tensors), jnp.bfloat16),
            jax.ShapeDtypeStruct((receivers, 1, 2 * imps), jnp.float32),
        ),
        in_specs=[vmem] * (3 + items_axis + tensors) + [hbm] * (dps - 1),
        out_specs=(hbm, vmem),
        scratch_shapes=[
            pltpu.VMEM((items_axis * imps, width), jnp.bfloat16),
            pltpu.VMEM((items_axis * imps, local_width * tensors), jnp.bfloat16),
            pltpu.VMEM((dps - 1, items, width), jnp.bfloat16),
            pltpu.SemaphoreType.DMA((dps - 1,)),
            pltpu.SemaphoreType.DMA,
        ],
        compiler_params=params,
        cost_estimate=pl.CostEstimate(
            flops=2 * items_axis * imps * width * (dps * items + local_width * tensors),
            bytes_accessed=2 * dps * items * width,
            transcendentals=items_axis * imps * dps * items,
        ),
        name="score",
    )(
        wanted,
        all_gated,
        chosen,
        *other_chosen,
        w_out,
        *other_w_out,
        catalogue,
        *(in_hbm(x) for x in other_catalogues),
    )
    sums = lax.all_to_all(sums, COLUMN, split_axis=0, concat_axis=0, tiled=True)
    sums = jnp.sum(sums, axis=(0, 1))
    return (state, sums[imps:] - jnp.log(sums[:imps]))


def solution(mesh):
    placed = (
        P(("groups", "item", "dp"), None),
        P("groups"),
        P("groups"),
        P("groups", None),
        P("groups", None),
        P(None, "tensor"),
        P("tensor", None),
        P(("item", "dp", "tensor"), None),
    )
    return jax.shard_map(
        local,
        mesh=mesh,
        in_specs=placed,
        out_specs=(P(("groups", "item", "dp"), "tensor"), P(("groups", "item", "dp"))),
        check_vma=False,
    )
```

```python
import functools
import math

import jax
import jax.numpy as jnp
from jax import lax
from jax.experimental import pallas as pl
from jax.experimental.pallas import tpu as pltpu
from jax.sharding import PartitionSpec as P

DH = 128
SLOTS = ("item", "dp")
COLUMN = ("tensor", "item")
NT = (((1,), (1,)), ((), ()))
MIB = 1024 * 1024
EVENT_PARTS = 3


def rounds(count):
    return [0] + sorted(range(1, count), key=lambda r: (r & 3 == 3, -(r & -2)))


def spec(space):
    return pl.BlockSpec(memory_space=space)


def pick_kernel(
    shards,
    packing,
    lengths,
    positions,
    logged,
    events,
    w_uvqk,
    chosen,
    limits,
    wanted,
    events_v,
    w_uvqk_v,
    done,
    packing_s,
    lengths_s,
    positions_v,
    logged_v,
    sems,
):
    rows = events.shape[0]
    items_axis, dps = shards
    imps = positions.shape[1]
    part_rows = rows // EVENT_PARTS
    parts = [pl.ds(k * part_rows, part_rows) for k in range(EVENT_PARTS)]
    copies = [
        pltpu.make_async_copy(source, target, sems.at[k])
        for k, (source, target) in enumerate(
            [
                (packing, packing_s),
                (positions, positions_v),
                (lengths, lengths_s),
                (logged, logged_v),
            ]
            + [(events.at[part], events_v.at[part]) for part in parts]
            + [(w_uvqk, w_uvqk_v)]
        )
    ]
    for copy in copies:
        copy.start()
    for copy in copies[:4]:
        copy.wait()
    item, dp = lax.axis_index("item"), lax.axis_index("dp")
    history = packing_s[item * dps + dp]
    row = positions_v[pl.ds(history, 1), :].astype(jnp.float32)
    diagonal = lax.broadcasted_iota(jnp.int32, (imps, imps), 0) == lax.broadcasted_iota(
        jnp.int32, (imps, imps), 1
    )
    spots = jnp.sum(jnp.where(diagonal, row, 0.0), axis=1, keepdims=True).astype(jnp.int32)
    limits[...] = jnp.broadcast_to(jnp.minimum(spots, lengths_s[history] - 1), limits.shape)
    for k, r in enumerate(rounds(items_axis)):
        other = packing_s[(item ^ r) * dps + dp]
        wanted[0:1, k * imps : (k + 1) * imps] = logged_v[pl.ds(other, 1), :]
    total = jnp.zeros((imps, events.shape[1]), jnp.float32)
    for k in range(EVENT_PARTS):
        copies[4 + k].wait()
        lanes = k * part_rows + lax.broadcasted_iota(jnp.int32, (imps, part_rows), 1)
        one_hot = jnp.where(lanes == spots, 1.0, 0.0).astype(jnp.bfloat16)
        total += jnp.dot(
            one_hot,
            events_v[k * part_rows : (k + 1) * part_rows, :],
            preferred_element_type=jnp.float32,
        )
    chosen[...] = total.astype(jnp.bfloat16)
    copies[-1].wait()

    @pl.when(is_early(item, items_axis))
    def _():
        attention(limits, events_v, chosen, w_uvqk_v, done)


def attention(limits, events, own, w_uvqk, store):
    lanes = lax.broadcasted_iota(jnp.int32, (own.shape[0], events.shape[0]), 1)
    valid = lanes <= limits[:, 0:1]
    for head in range(w_uvqk.shape[1] // (4 * DH)):
        first = head * 4 * DH
        w_part = [w_uvqk[:, first + k * DH : first + (k + 1) * DH] for k in range(4)]
        w_gate_query = jnp.concatenate([w_part[0], w_part[2]], axis=1)
        w_value_key = jnp.concatenate([w_part[1], w_part[3]], axis=1)
        gate_query = jnp.dot(own[...], w_gate_query, preferred_element_type=jnp.float32)
        gate_query = jax.nn.silu(gate_query).astype(jnp.bfloat16)
        value_key = jnp.dot(events[...], w_value_key, preferred_element_type=jnp.float32)
        value_key = jax.nn.silu(value_key).astype(jnp.bfloat16)
        scores = lax.dot_general(
            gate_query[:, DH:], value_key[:, DH:], NT, preferred_element_type=jnp.float32
        ) / math.sqrt(DH)
        weights = jnp.where(valid, jax.nn.silu(scores), 0.0).astype(jnp.bfloat16)
        attended = jnp.dot(weights, value_key[:, :DH], preferred_element_type=jnp.float32)
        inverse = lax.rsqrt(jnp.mean(attended * attended, axis=-1, keepdims=True) + 1e-06)
        store[:, head * DH : (head + 1) * DH] = (
            attended * inverse * gate_query[:, :DH].astype(jnp.float32)
        ).astype(jnp.bfloat16)


def is_early(item, items_axis):
    return item * 4 < items_axis


def attend_kernel(items_axis, limits, events, chosen, w_uvqk, done, gated, rows, sems):
    early = is_early(lax.axis_index("item"), items_axis)

    @pl.when(early)
    def _():
        rows[...] = done[...]

    @pl.when(jnp.logical_not(early))
    def _():
        attention(limits, events, chosen, w_uvqk, rows)

    copies = [pltpu.make_async_copy(rows, gated.at[k], sems.at[k]) for k in range(gated.shape[0])]
    for copy in copies:
        copy.start()
    for copy in copies:
        copy.wait()


def score_kernel(sizes, wanted, gated, *refs):
    items_axis, dps, tensors = sizes
    chosen, refs = refs[:items_axis], refs[items_axis:]
    w_out, refs = refs[:tensors], refs[tensors:]
    catalogue, refs = list(refs[:dps]), refs[dps:]
    state_hbm, sums, hidden, gates, others, sems, state_sem = refs
    fetches = [
        pltpu.make_async_copy(catalogue[d], others.at[d - 1], sems.at[d - 1]) for d in range(1, dps)
    ]
    for fetch in fetches:
        fetch.start()
    catalogue[1:] = [others.at[d - 1] for d in range(1, dps)]
    item, dp, tensor = (lax.axis_index(a) for a in ("item", "dp", "tensor"))
    imps = chosen[0].shape[0]
    items = catalogue[0].shape[0]
    step_rows = min(256, items_axis * imps)
    step_items = min(512, items)
    steps = range(0, items, step_items)
    slot_rounds, tensor_rounds = rounds(items_axis), rounds(tensors)
    local_width = w_out[0].shape[0]
    for k in range(items_axis):
        for t in range(tensors):
            sender = (tensor ^ tensor_rounds[t]) * items_axis + (item ^ slot_rounds[k])
            gates[k * imps : (k + 1) * imps, t * local_width : (t + 1) * local_width] = gated[sender]
    w_whole = jnp.concatenate([w[...] for w in w_out], axis=0)
    mixed = jnp.dot(gates[...], w_whole, preferred_element_type=jnp.float32)
    for k in range(items_axis):
        rows = slice(k * imps, (k + 1) * imps)
        hidden[rows, :] = (mixed[rows] + chosen[k][...].astype(jnp.float32)).astype(jnp.bfloat16)
    share = state_hbm.shape[1]
    state_copy = pltpu.make_async_copy(
        hidden.at[pl.ds(0, imps), pl.ds(pl.multiple_of(tensor * share, share), share)],
        state_hbm,
        state_sem,
    )
    state_copy.start()

    blocks = range(0, items_axis * imps, step_rows)
    totals = {row: jnp.zeros((8, step_rows), jnp.float32) for row in blocks}
    targets = dict(totals)
    for d in range(dps):
        if d > 0:
            fetches[d - 1].wait()
        item_base = ((item * dps + (dp ^ rounds(dps)[d])) * tensors + tensor) * items
        ids = {row: wanted[0:1, row : row + step_rows] - item_base for row in blocks}
        for first in steps:
            for row in blocks:
                logits = lax.dot_general(
                    catalogue[d][first : first + step_items, :],
                    hidden[row : row + step_rows, :],
                    NT,
                    preferred_element_type=jnp.float32,
                )
                item_ids = lax.broadcasted_iota(jnp.int32, logits.shape, 0)
                found = jnp.where(item_ids == ids[row] - first, logits, 0.0)
                totals[row] += jnp.sum(jnp.exp(logits).reshape(-1, 8, step_rows), axis=0)
                targets[row] += jnp.sum(found.reshape(-1, 8, step_rows), axis=0)
    for row in blocks:
        total = jnp.sum(totals[row], axis=0, keepdims=True)
        target = jnp.sum(targets[row], axis=0, keepdims=True)
        for part in range(step_rows // imps):
            owner = item ^ slot_rounds[row // imps + part]
            both = jnp.concatenate(
                [v[:, part * imps : (part + 1) * imps] for v in (total, target)], axis=1
            )
            for t in range(tensors):
                sums[t * items_axis + owner] = both
    state_copy.wait()


def in_hbm(x):
    return pltpu.with_memory_space_constraint(x, pltpu.HBM)


def send(x, axes, count, r):
    return lax.ppermute(x, axes, [(i, i ^ r) for i in range(count)])


def from_others(x, axes, count, beside=()):
    pieces = {}
    for r in rounds(count)[1:]:
        if r & 3 == 3:
            held, pieces[r - 2], beside = lax.optimization_barrier(
                (pieces[r - 1], pieces[r - 2], beside)
            )
            pieces[r] = send(held, axes, count, 1)
        else:
            pieces[r] = send(x, axes, count, r)
    return list(pieces.values()), beside


def local(events, lengths, packing, positions, logged, w_uvqk, w_out, catalogue):
    rows, width = events.shape
    imps = positions.shape[1]
    hists = packing.shape[0]
    items = catalogue.shape[0]
    local_width = w_out.shape[0]
    items_axis, dps, tensors = (lax.axis_size(a) for a in ("item", "dp", "tensor"))
    receivers = items_axis * tensors
    params = pltpu.CompilerParams(vmem_limit_bytes=(12 + 2 * items_axis) * MIB)
    vmem, hbm = spec(pltpu.VMEM), spec(pltpu.HBM)

    other_catalogues, _ = from_others(catalogue, "dp", dps)
    other_w_out, _ = from_others(w_out, "tensor", tensors)
    chosen, limits, wanted, events, w_uvqk, done = pl.pallas_call(
        functools.partial(pick_kernel, (items_axis, dps)),
        out_shape=(
            jax.ShapeDtypeStruct((imps, width), jnp.bfloat16),
            jax.ShapeDtypeStruct((imps, 128), jnp.int32),
            jax.ShapeDtypeStruct((1, items_axis * imps), jnp.int32),
            jax.ShapeDtypeStruct(events.shape, events.dtype),
            jax.ShapeDtypeStruct(w_uvqk.shape, w_uvqk.dtype),
            jax.ShapeDtypeStruct((imps, local_width), jnp.bfloat16),
        ),
        in_specs=[hbm] * 6,
        out_specs=(vmem,) * 6,
        scratch_shapes=[
            pltpu.SMEM((hists,), jnp.int32),
            pltpu.SMEM((hists,), jnp.int32),
            pltpu.VMEM((hists, imps), jnp.int32),
            pltpu.VMEM((hists, imps), jnp.int32),
            pltpu.SemaphoreType.DMA((5 + EVENT_PARTS,)),
        ],
        compiler_params=params,
        cost_estimate=pl.CostEstimate(
            flops=2 * imps * rows * width, bytes_accessed=2 * rows * width, transcendentals=0
        ),
        name="pick",
    )(*(in_hbm(x) for x in (packing, lengths, positions, logged, events, w_uvqk)))
    other_chosen, other_w_out = from_others(chosen, "item", items_axis, other_w_out)

    gated = pl.pallas_call(
        functools.partial(attend_kernel, items_axis),
        out_shape=pltpu.HBM((receivers, imps, local_width), jnp.bfloat16),
        in_specs=[vmem] * 5,
        out_specs=hbm,
        scratch_shapes=[
            pltpu.VMEM((imps, local_width), jnp.bfloat16),
            pltpu.SemaphoreType.DMA((receivers,)),
        ],
        compiler_params=params,
        cost_estimate=pl.CostEstimate(flops=0, bytes_accessed=0, transcendentals=0),
        name="attend",
    )(limits, events, chosen, w_uvqk, done)
    all_gated = lax.all_to_all(gated, COLUMN, split_axis=0, concat_axis=0, tiled=True)

    state, sums = pl.pallas_call(
        functools.partial(score_kernel, (items_axis, dps, tensors)),
        out_shape=(
            jax.ShapeDtypeStruct((imps, width // tensors), jnp.bfloat16),
            jax.ShapeDtypeStruct((receivers, 1, 2 * imps), jnp.float32),
        ),
        in_specs=[vmem] * (3 + items_axis + tensors) + [hbm] * (dps - 1),
        out_specs=(hbm, vmem),
        scratch_shapes=[
            pltpu.VMEM((items_axis * imps, width), jnp.bfloat16),
            pltpu.VMEM((items_axis * imps, local_width * tensors), jnp.bfloat16),
            pltpu.VMEM((dps - 1, items, width), jnp.bfloat16),
            pltpu.SemaphoreType.DMA((dps - 1,)),
            pltpu.SemaphoreType.DMA,
        ],
        compiler_params=params,
        cost_estimate=pl.CostEstimate(
            flops=2 * items_axis * imps * width * (dps * items + local_width * tensors),
            bytes_accessed=2 * dps * items * width,
            transcendentals=items_axis * imps * dps * items,
        ),
        name="score",
    )(
        wanted,
        all_gated,
        chosen,
        *other_chosen,
        w_out,
        *other_w_out,
        catalogue,
        *(in_hbm(x) for x in other_catalogues),
    )
    sums = lax.all_to_all(sums, COLUMN, split_axis=0, concat_axis=0, tiled=True)
    sums = jnp.sum(sums, axis=(0, 1))
    return (state, sums[imps:] - jnp.log(sums[:imps]))


def solution(mesh):
    placed = (
        P(("groups", "item", "dp"), None),
        P("groups"),
        P("groups"),
        P("groups", None),
        P("groups", None),
        P(None, "tensor"),
        P("tensor", None),
        P(("item", "dp", "tensor"), None),
    )
    return jax.shard_map(
        local,
        mesh=mesh,
        in_specs=placed,
        out_specs=(P(("groups", "item", "dp"), "tensor"), P(("groups", "item", "dp"))),
        check_vma=False,
    )
```

```python
import functools
import math

import jax
import jax.numpy as jnp
from jax import lax
from jax.experimental import pallas as pl
from jax.experimental.pallas import tpu as pltpu
from jax.sharding import PartitionSpec as P

DH = 128
SLOTS = ("item", "dp")
COLUMN = ("tensor", "item")
NT = (((1,), (1,)), ((), ()))
MIB = 1024 * 1024
EVENT_PARTS = 3


def rounds(count):
    return [0] + sorted(range(1, count), key=lambda r: (r & 3 == 3, -(r & -2)))


def spec(space):
    return pl.BlockSpec(memory_space=space)


def pick_kernel(
    shards,
    packing,
    lengths,
    positions,
    logged,
    events,
    w_uvqk,
    chosen,
    limits,
    wanted,
    events_v,
    w_uvqk_v,
    done,
    packing_s,
    lengths_s,
    positions_v,
    logged_v,
    sems,
):
    rows = events.shape[0]
    items_axis, dps = shards
    imps = positions.shape[1]
    part_rows = rows // EVENT_PARTS
    parts = [pl.ds(k * part_rows, part_rows) for k in range(EVENT_PARTS)]
    copies = [
        pltpu.make_async_copy(source, target, sems.at[k])
        for k, (source, target) in enumerate(
            [
                (packing, packing_s),
                (positions, positions_v),
                (lengths, lengths_s),
                (logged, logged_v),
            ]
            + [(events.at[part], events_v.at[part]) for part in parts]
            + [(w_uvqk, w_uvqk_v)]
        )
    ]
    for copy in copies:
        copy.start()
    for copy in copies[:4]:
        copy.wait()
    item, dp = lax.axis_index("item"), lax.axis_index("dp")
    history = packing_s[item * dps + dp]
    row = positions_v[pl.ds(history, 1), :].astype(jnp.float32)
    diagonal = lax.broadcasted_iota(jnp.int32, (imps, imps), 0) == lax.broadcasted_iota(
        jnp.int32, (imps, imps), 1
    )
    spots = jnp.sum(jnp.where(diagonal, row, 0.0), axis=1, keepdims=True).astype(jnp.int32)
    limits[...] = jnp.broadcast_to(jnp.minimum(spots, lengths_s[history] - 1), limits.shape)
    for k, r in enumerate(rounds(items_axis)):
        other = packing_s[(item ^ r) * dps + dp]
        wanted[0:1, k * imps : (k + 1) * imps] = logged_v[pl.ds(other, 1), :]
    total = jnp.zeros((imps, events.shape[1]), jnp.float32)
    for k in range(EVENT_PARTS):
        copies[4 + k].wait()
        lanes = k * part_rows + lax.broadcasted_iota(jnp.int32, (imps, part_rows), 1)
        one_hot = jnp.where(lanes == spots, 1.0, 0.0).astype(jnp.bfloat16)
        total += jnp.dot(
            one_hot,
            events_v[k * part_rows : (k + 1) * part_rows, :],
            preferred_element_type=jnp.float32,
        )
    chosen[...] = total.astype(jnp.bfloat16)
    copies[-1].wait()

    @pl.when(is_early(item, items_axis))
    def _():
        attention(limits, events_v, chosen, w_uvqk_v, done)


def attention(limits, events, own, w_uvqk, store):
    lanes = lax.broadcasted_iota(jnp.int32, (own.shape[0], events.shape[0]), 1)
    valid = lanes <= limits[:, 0:1]
    for head in range(w_uvqk.shape[1] // (4 * DH)):
        first = head * 4 * DH
        w_part = [w_uvqk[:, first + k * DH : first + (k + 1) * DH] for k in range(4)]
        w_gate_query = jnp.concatenate([w_part[0], w_part[2]], axis=1)
        w_value_key = jnp.concatenate([w_part[1], w_part[3]], axis=1)
        gate_query = jnp.dot(own[...], w_gate_query, preferred_element_type=jnp.float32)
        gate_query = jax.nn.silu(gate_query).astype(jnp.bfloat16)
        value_key = jnp.dot(events[...], w_value_key, preferred_element_type=jnp.float32)
        value_key = jax.nn.silu(value_key).astype(jnp.bfloat16)
        scores = lax.dot_general(
            gate_query[:, DH:], value_key[:, DH:], NT, preferred_element_type=jnp.float32
        ) / math.sqrt(DH)
        weights = jnp.where(valid, jax.nn.silu(scores), 0.0).astype(jnp.bfloat16)
        attended = jnp.dot(weights, value_key[:, :DH], preferred_element_type=jnp.float32)
        inverse = lax.rsqrt(jnp.mean(attended * attended, axis=-1, keepdims=True) + 1e-06)
        store[:, head * DH : (head + 1) * DH] = (
            attended * inverse * gate_query[:, :DH].astype(jnp.float32)
        ).astype(jnp.bfloat16)


def is_early(item, items_axis):
    return item * 4 < items_axis


def attend_kernel(items_axis, limits, events, chosen, w_uvqk, done, gated, rows, sems):
    early = is_early(lax.axis_index("item"), items_axis)

    @pl.when(early)
    def _():
        rows[...] = done[...]

    @pl.when(jnp.logical_not(early))
    def _():
        attention(limits, events, chosen, w_uvqk, rows)

    copies = [pltpu.make_async_copy(rows, gated.at[k], sems.at[k]) for k in range(gated.shape[0])]
    for copy in copies:
        copy.start()
    for copy in copies:
        copy.wait()


def score_kernel(sizes, wanted, gated, *refs):
    items_axis, dps, tensors = sizes
    chosen, refs = refs[:items_axis], refs[items_axis:]
    w_out, refs = refs[:tensors], refs[tensors:]
    catalogue, refs = list(refs[:dps]), refs[dps:]
    state_hbm, sums, hidden, gates, others, sems, state_sem = refs
    fetches = [
        pltpu.make_async_copy(catalogue[d], others.at[d - 1], sems.at[d - 1]) for d in range(1, dps)
    ]
    for fetch in fetches:
        fetch.start()
    catalogue[1:] = [others.at[d - 1] for d in range(1, dps)]
    item, dp, tensor = (lax.axis_index(a) for a in ("item", "dp", "tensor"))
    imps = chosen[0].shape[0]
    items = catalogue[0].shape[0]
    step_rows = min(256, items_axis * imps)
    step_items = min(128, items)
    steps = range(0, items, step_items)
    slot_rounds, tensor_rounds = rounds(items_axis), rounds(tensors)
    local_width = w_out[0].shape[0]
    for k in range(items_axis):
        for t in range(tensors):
            sender = (tensor ^ tensor_rounds[t]) * items_axis + (item ^ slot_rounds[k])
            gates[k * imps : (k + 1) * imps, t * local_width : (t + 1) * local_width] = gated[sender]
    w_whole = jnp.concatenate([w[...] for w in w_out], axis=0)
    mixed = jnp.dot(gates[...], w_whole, preferred_element_type=jnp.float32)
    for k in range(items_axis):
        rows = slice(k * imps, (k + 1) * imps)
        hidden[rows, :] = (mixed[rows] + chosen[k][...].astype(jnp.float32)).astype(jnp.bfloat16)
    share = state_hbm.shape[1]
    state_copy = pltpu.make_async_copy(
        hidden.at[pl.ds(0, imps), pl.ds(pl.multiple_of(tensor * share, share), share)],
        state_hbm,
        state_sem,
    )
    state_copy.start()

    blocks = range(0, items_axis * imps, step_rows)
    totals = {row: jnp.zeros((8, step_rows), jnp.float32) for row in blocks}
    targets = dict(totals)
    for d in range(dps):
        if d > 0:
            fetches[d - 1].wait()
        item_base = ((item * dps + (dp ^ rounds(dps)[d])) * tensors + tensor) * items
        ids = {row: wanted[0:1, row : row + step_rows] - item_base for row in blocks}
        for first in steps:
            for row in blocks:
                logits = lax.dot_general(
                    catalogue[d][first : first + step_items, :],
                    hidden[row : row + step_rows, :],
                    NT,
                    preferred_element_type=jnp.float32,
                )
                item_ids = lax.broadcasted_iota(jnp.int32, logits.shape, 0)
                found = jnp.where(item_ids == ids[row] - first, logits, 0.0)
                totals[row] += jnp.sum(jnp.exp(logits).reshape(-1, 8, step_rows), axis=0)
                targets[row] += jnp.sum(found.reshape(-1, 8, step_rows), axis=0)
    for row in blocks:
        total = jnp.sum(totals[row], axis=0, keepdims=True)
        target = jnp.sum(targets[row], axis=0, keepdims=True)
        for part in range(step_rows // imps):
            owner = item ^ slot_rounds[row // imps + part]
            both = jnp.concatenate(
                [v[:, part * imps : (part + 1) * imps] for v in (total, target)], axis=1
            )
            for t in range(tensors):
                sums[t * items_axis + owner] = both
    state_copy.wait()


def in_hbm(x):
    return pltpu.with_memory_space_constraint(x, pltpu.HBM)


def send(x, axes, count, r):
    return lax.ppermute(x, axes, [(i, i ^ r) for i in range(count)])


def from_others(x, axes, count):
    pieces = {}
    for r in rounds(count)[1:]:
        if r & 3 == 3:
            held, pieces[r - 2] = lax.optimization_barrier((pieces[r - 1], pieces[r - 2]))
            pieces[r] = send(held, axes, count, 1)
        else:
            pieces[r] = send(x, axes, count, r)
    return list(pieces.values())


def local(events, lengths, packing, positions, logged, w_uvqk, w_out, catalogue):
    rows, width = events.shape
    imps = positions.shape[1]
    hists = packing.shape[0]
    items = catalogue.shape[0]
    local_width = w_out.shape[0]
    items_axis, dps, tensors = (lax.axis_size(a) for a in ("item", "dp", "tensor"))
    receivers = items_axis * tensors
    params = pltpu.CompilerParams(vmem_limit_bytes=(12 + 2 * items_axis) * MIB)
    vmem, hbm = spec(pltpu.VMEM), spec(pltpu.HBM)

    other_catalogues = from_others(catalogue, "dp", dps)
    other_w_out = from_others(w_out, "tensor", tensors)
    chosen, limits, wanted, events, w_uvqk, done = pl.pallas_call(
        functools.partial(pick_kernel, (items_axis, dps)),
        out_shape=(
            jax.ShapeDtypeStruct((imps, width), jnp.bfloat16),
            jax.ShapeDtypeStruct((imps, 128), jnp.int32),
            jax.ShapeDtypeStruct((1, items_axis * imps), jnp.int32),
            jax.ShapeDtypeStruct(events.shape, events.dtype),
            jax.ShapeDtypeStruct(w_uvqk.shape, w_uvqk.dtype),
            jax.ShapeDtypeStruct((imps, local_width), jnp.bfloat16),
        ),
        in_specs=[hbm] * 6,
        out_specs=(vmem,) * 6,
        scratch_shapes=[
            pltpu.SMEM((hists,), jnp.int32),
            pltpu.SMEM((hists,), jnp.int32),
            pltpu.VMEM((hists, imps), jnp.int32),
            pltpu.VMEM((hists, imps), jnp.int32),
            pltpu.SemaphoreType.DMA((5 + EVENT_PARTS,)),
        ],
        compiler_params=params,
        cost_estimate=pl.CostEstimate(
            flops=2 * imps * rows * width, bytes_accessed=2 * rows * width, transcendentals=0
        ),
        name="pick",
    )(*(in_hbm(x) for x in (packing, lengths, positions, logged, events, w_uvqk)))
    other_chosen = from_others(chosen, "item", items_axis)

    gated = pl.pallas_call(
        functools.partial(attend_kernel, items_axis),
        out_shape=pltpu.HBM((receivers, imps, local_width), jnp.bfloat16),
        in_specs=[vmem] * 5,
        out_specs=hbm,
        scratch_shapes=[
            pltpu.VMEM((imps, local_width), jnp.bfloat16),
            pltpu.SemaphoreType.DMA((receivers,)),
        ],
        compiler_params=params,
        cost_estimate=pl.CostEstimate(flops=0, bytes_accessed=0, transcendentals=0),
        name="attend",
    )(limits, events, chosen, w_uvqk, done)
    all_gated = lax.all_to_all(gated, COLUMN, split_axis=0, concat_axis=0, tiled=True)

    state, sums = pl.pallas_call(
        functools.partial(score_kernel, (items_axis, dps, tensors)),
        out_shape=(
            jax.ShapeDtypeStruct((imps, width // tensors), jnp.bfloat16),
            jax.ShapeDtypeStruct((receivers, 1, 2 * imps), jnp.float32),
        ),
        in_specs=[vmem] * (3 + items_axis + tensors) + [hbm] * (dps - 1),
        out_specs=(hbm, vmem),
        scratch_shapes=[
            pltpu.VMEM((items_axis * imps, width), jnp.bfloat16),
            pltpu.VMEM((items_axis * imps, local_width * tensors), jnp.bfloat16),
            pltpu.VMEM((dps - 1, items, width), jnp.bfloat16),
            pltpu.SemaphoreType.DMA((dps - 1,)),
            pltpu.SemaphoreType.DMA,
        ],
        compiler_params=params,
        cost_estimate=pl.CostEstimate(
            flops=2 * items_axis * imps * width * (dps * items + local_width * tensors),
            bytes_accessed=2 * dps * items * width,
            transcendentals=items_axis * imps * dps * items,
        ),
        name="score",
    )(
        wanted,
        all_gated,
        chosen,
        *other_chosen,
        w_out,
        *other_w_out,
        catalogue,
        *(in_hbm(x) for x in other_catalogues),
    )
    sums = lax.all_to_all(sums, COLUMN, split_axis=0, concat_axis=0, tiled=True)
    sums = jnp.sum(sums, axis=(0, 1))
    return (state, sums[imps:] - jnp.log(sums[:imps]))


def solution(mesh):
    placed = (
        P(("groups", "item", "dp"), None),
        P("groups"),
        P("groups"),
        P("groups", None),
        P("groups", None),
        P(None, "tensor"),
        P("tensor", None),
        P(("item", "dp", "tensor"), None),
    )
    return jax.shard_map(
        local,
        mesh=mesh,
        in_specs=placed,
        out_specs=(P(("groups", "item", "dp"), "tensor"), P(("groups", "item", "dp"))),
        check_vma=False,
    )
```

```python
import functools
import math

import jax
import jax.numpy as jnp
from jax import lax
from jax.experimental import pallas as pl
from jax.experimental.pallas import tpu as pltpu
from jax.sharding import PartitionSpec as P

DH = 128
SLOTS = ("item", "dp")
COLUMN = ("tensor", "item")
NT = (((1,), (1,)), ((), ()))
MIB = 1024 * 1024
EVENT_PARTS = 3


def rounds(count):
    return [0] + sorted(range(1, count), key=lambda r: (r & 3 == 3, -(r & -2)))


def spec(space):
    return pl.BlockSpec(memory_space=space)


def pick_kernel(
    shards,
    packing,
    lengths,
    positions,
    logged,
    events,
    w_uvqk,
    chosen,
    limits,
    wanted,
    events_v,
    done,
    w_uvqk_v,
    packing_s,
    lengths_s,
    positions_v,
    logged_v,
    sems,
):
    rows = events.shape[0]
    items_axis, dps = shards
    imps = positions.shape[1]
    part_rows = rows // EVENT_PARTS
    parts = [pl.ds(k * part_rows, part_rows) for k in range(EVENT_PARTS)]
    copies = [
        pltpu.make_async_copy(source, target, sems.at[k])
        for k, (source, target) in enumerate(
            [
                (packing, packing_s),
                (positions, positions_v),
                (lengths, lengths_s),
                (logged, logged_v),
            ]
            + [(events.at[part], events_v.at[part]) for part in parts]
            + [(w_uvqk, w_uvqk_v)]
        )
    ]
    for copy in copies[:-1]:
        copy.start()
    item, dp = lax.axis_index("item"), lax.axis_index("dp")
    early = is_early(item, items_axis)
    pl.when(early)(copies[-1].start)
    for copy in copies[:4]:
        copy.wait()
    history = packing_s[item * dps + dp]
    row = positions_v[pl.ds(history, 1), :].astype(jnp.float32)
    diagonal = lax.broadcasted_iota(jnp.int32, (imps, imps), 0) == lax.broadcasted_iota(
        jnp.int32, (imps, imps), 1
    )
    spots = jnp.sum(jnp.where(diagonal, row, 0.0), axis=1, keepdims=True).astype(jnp.int32)
    limits[...] = jnp.broadcast_to(jnp.minimum(spots, lengths_s[history] - 1), limits.shape)
    for k, r in enumerate(rounds(items_axis)):
        other = packing_s[(item ^ r) * dps + dp]
        wanted[0:1, k * imps : (k + 1) * imps] = logged_v[pl.ds(other, 1), :]
    total = jnp.zeros((imps, events.shape[1]), jnp.float32)
    for k in range(EVENT_PARTS):
        copies[4 + k].wait()
        lanes = k * part_rows + lax.broadcasted_iota(jnp.int32, (imps, part_rows), 1)
        one_hot = jnp.where(lanes == spots, 1.0, 0.0).astype(jnp.bfloat16)
        total += jnp.dot(
            one_hot,
            events_v[k * part_rows : (k + 1) * part_rows, :],
            preferred_element_type=jnp.float32,
        )
    chosen[...] = total.astype(jnp.bfloat16)

    @pl.when(early)
    def _():
        copies[-1].wait()
        attention(limits, events_v, chosen, w_uvqk_v, done)


def attention(limits, events, own, w_uvqk, store):
    lanes = lax.broadcasted_iota(jnp.int32, (own.shape[0], events.shape[0]), 1)
    valid = lanes <= limits[:, 0:1]
    for head in range(w_uvqk.shape[1] // (4 * DH)):
        first = head * 4 * DH
        w_part = [w_uvqk[:, first + k * DH : first + (k + 1) * DH] for k in range(4)]
        w_gate_query = jnp.concatenate([w_part[0], w_part[2]], axis=1)
        w_value_key = jnp.concatenate([w_part[1], w_part[3]], axis=1)
        gate_query = jnp.dot(own[...], w_gate_query, preferred_element_type=jnp.float32)
        gate_query = jax.nn.silu(gate_query).astype(jnp.bfloat16)
        value_key = jnp.dot(events[...], w_value_key, preferred_element_type=jnp.float32)
        value_key = jax.nn.silu(value_key).astype(jnp.bfloat16)
        scores = lax.dot_general(
            gate_query[:, DH:], value_key[:, DH:], NT, preferred_element_type=jnp.float32
        ) / math.sqrt(DH)
        weights = jnp.where(valid, jax.nn.silu(scores), 0.0).astype(jnp.bfloat16)
        attended = jnp.dot(weights, value_key[:, :DH], preferred_element_type=jnp.float32)
        inverse = lax.rsqrt(jnp.mean(attended * attended, axis=-1, keepdims=True) + 1e-06)
        store[:, head * DH : (head + 1) * DH] = (
            attended * inverse * gate_query[:, :DH].astype(jnp.float32)
        ).astype(jnp.bfloat16)


def is_early(item, items_axis):
    return item * 4 < items_axis


def attend_kernel(items_axis, limits, events, chosen, w_uvqk, done, gated, rows, sems):
    early = is_early(lax.axis_index("item"), items_axis)

    @pl.when(early)
    def _():
        rows[...] = done[...]

    @pl.when(jnp.logical_not(early))
    def _():
        attention(limits, events, chosen, w_uvqk, rows)

    copies = [pltpu.make_async_copy(rows, gated.at[k], sems.at[k]) for k in range(gated.shape[0])]
    for copy in copies:
        copy.start()
    for copy in copies:
        copy.wait()


def score_kernel(sizes, wanted, gated, *refs):
    items_axis, dps, tensors = sizes
    chosen, refs = refs[:items_axis], refs[items_axis:]
    w_out, refs = refs[:tensors], refs[tensors:]
    catalogue, refs = list(refs[:dps]), refs[dps:]
    state_hbm, sums, hidden, gates, others, sems, state_sem = refs
    fetches = [
        pltpu.make_async_copy(catalogue[d], others.at[d - 1], sems.at[d - 1]) for d in range(1, dps)
    ]
    for fetch in fetches:
        fetch.start()
    catalogue[1:] = [others.at[d - 1] for d in range(1, dps)]
    item, dp, tensor = (lax.axis_index(a) for a in ("item", "dp", "tensor"))
    imps = chosen[0].shape[0]
    items = catalogue[0].shape[0]
    step_rows = min(256, items_axis * imps)
    step_items = min(256, items)
    steps = range(0, items, step_items)
    slot_rounds, tensor_rounds = rounds(items_axis), rounds(tensors)
    local_width = w_out[0].shape[0]
    for k in range(items_axis):
        for t in range(tensors):
            sender = (tensor ^ tensor_rounds[t]) * items_axis + (item ^ slot_rounds[k])
            gates[k * imps : (k + 1) * imps, t * local_width : (t + 1) * local_width] = gated[sender]
    w_whole = jnp.concatenate([w[...] for w in w_out], axis=0)
    mixed = jnp.dot(gates[...], w_whole, preferred_element_type=jnp.float32)
    for k in range(items_axis):
        rows = slice(k * imps, (k + 1) * imps)
        hidden[rows, :] = (mixed[rows] + chosen[k][...].astype(jnp.float32)).astype(jnp.bfloat16)
    share = state_hbm.shape[1]
    state_copy = pltpu.make_async_copy(
        hidden.at[pl.ds(0, imps), pl.ds(pl.multiple_of(tensor * share, share), share)],
        state_hbm,
        state_sem,
    )
    state_copy.start()

    blocks = range(0, items_axis * imps, step_rows)
    totals = {row: jnp.zeros((8, step_rows), jnp.float32) for row in blocks}
    targets = dict(totals)
    for d in range(dps):
        if d > 0:
            fetches[d - 1].wait()
        item_base = ((item * dps + (dp ^ rounds(dps)[d])) * tensors + tensor) * items
        ids = {row: wanted[0:1, row : row + step_rows] - item_base for row in blocks}
        for first in steps:
            for row in blocks:
                logits = lax.dot_general(
                    catalogue[d][first : first + step_items, :],
                    hidden[row : row + step_rows, :],
                    NT,
                    preferred_element_type=jnp.float32,
                )
                item_ids = lax.broadcasted_iota(jnp.int32, logits.shape, 0)
                found = jnp.where(item_ids == ids[row] - first, logits, 0.0)
                totals[row] += jnp.sum(jnp.exp(logits).reshape(-1, 8, step_rows), axis=0)
                targets[row] += jnp.sum(found.reshape(-1, 8, step_rows), axis=0)
    for row in blocks:
        total = jnp.sum(totals[row], axis=0, keepdims=True)
        target = jnp.sum(targets[row], axis=0, keepdims=True)
        for part in range(step_rows // imps):
            owner = item ^ slot_rounds[row // imps + part]
            both = jnp.concatenate(
                [v[:, part * imps : (part + 1) * imps] for v in (total, target)], axis=1
            )
            for t in range(tensors):
                sums[t * items_axis + owner] = both
    state_copy.wait()


def in_hbm(x):
    return pltpu.with_memory_space_constraint(x, pltpu.HBM)


def send(x, axes, count, r):
    return lax.ppermute(x, axes, [(i, i ^ r) for i in range(count)])


def from_others(x, axes, count):
    pieces = {}
    for r in rounds(count)[1:]:
        if r & 3 == 3:
            held, pieces[r - 2] = lax.optimization_barrier((pieces[r - 1], pieces[r - 2]))
            pieces[r] = send(held, axes, count, 1)
        else:
            pieces[r] = send(x, axes, count, r)
    return list(pieces.values())


def local(events, lengths, packing, positions, logged, w_uvqk, w_out, catalogue):
    rows, width = events.shape
    imps = positions.shape[1]
    hists = packing.shape[0]
    items = catalogue.shape[0]
    local_width = w_out.shape[0]
    items_axis, dps, tensors = (lax.axis_size(a) for a in ("item", "dp", "tensor"))
    receivers = items_axis * tensors
    params = pltpu.CompilerParams(vmem_limit_bytes=(12 + 2 * items_axis) * MIB)
    vmem, hbm = spec(pltpu.VMEM), spec(pltpu.HBM)

    other_catalogues = from_others(catalogue, "dp", dps)
    other_w_out = from_others(w_out, "tensor", tensors)
    chosen, limits, wanted, events, done = pl.pallas_call(
        functools.partial(pick_kernel, (items_axis, dps)),
        out_shape=(
            jax.ShapeDtypeStruct((imps, width), jnp.bfloat16),
            jax.ShapeDtypeStruct((imps, 128), jnp.int32),
            jax.ShapeDtypeStruct((1, items_axis * imps), jnp.int32),
            jax.ShapeDtypeStruct(events.shape, events.dtype),
            jax.ShapeDtypeStruct((imps, local_width), jnp.bfloat16),
        ),
        in_specs=[hbm] * 6,
        out_specs=(vmem,) * 5,
        scratch_shapes=[
            pltpu.VMEM(w_uvqk.shape, w_uvqk.dtype),
            pltpu.SMEM((hists,), jnp.int32),
            pltpu.SMEM((hists,), jnp.int32),
            pltpu.VMEM((hists, imps), jnp.int32),
            pltpu.VMEM((hists, imps), jnp.int32),
            pltpu.SemaphoreType.DMA((5 + EVENT_PARTS,)),
        ],
        compiler_params=params,
        cost_estimate=pl.CostEstimate(
            flops=2 * imps * rows * width, bytes_accessed=2 * rows * width, transcendentals=0
        ),
        name="pick",
    )(*(in_hbm(x) for x in (packing, lengths, positions, logged, events, w_uvqk)))
    other_chosen = from_others(chosen, "item", items_axis)

    gated = pl.pallas_call(
        functools.partial(attend_kernel, items_axis),
        out_shape=pltpu.HBM((receivers, imps, local_width), jnp.bfloat16),
        in_specs=[vmem] * 5,
        out_specs=hbm,
        scratch_shapes=[
            pltpu.VMEM((imps, local_width), jnp.bfloat16),
            pltpu.SemaphoreType.DMA((receivers,)),
        ],
        compiler_params=params,
        cost_estimate=pl.CostEstimate(flops=0, bytes_accessed=0, transcendentals=0),
        name="attend",
    )(limits, events, chosen, w_uvqk, done)
    all_gated = lax.all_to_all(gated, COLUMN, split_axis=0, concat_axis=0, tiled=True)

    state, sums = pl.pallas_call(
        functools.partial(score_kernel, (items_axis, dps, tensors)),
        out_shape=(
            jax.ShapeDtypeStruct((imps, width // tensors), jnp.bfloat16),
            jax.ShapeDtypeStruct((receivers, 1, 2 * imps), jnp.float32),
        ),
        in_specs=[vmem] * (3 + items_axis + tensors) + [hbm] * (dps - 1),
        out_specs=(hbm, vmem),
        scratch_shapes=[
            pltpu.VMEM((items_axis * imps, width), jnp.bfloat16),
            pltpu.VMEM((items_axis * imps, local_width * tensors), jnp.bfloat16),
            pltpu.VMEM((dps - 1, items, width), jnp.bfloat16),
            pltpu.SemaphoreType.DMA((dps - 1,)),
            pltpu.SemaphoreType.DMA,
        ],
        compiler_params=params,
        cost_estimate=pl.CostEstimate(
            flops=2 * items_axis * imps * width * (dps * items + local_width * tensors),
            bytes_accessed=2 * dps * items * width,
            transcendentals=items_axis * imps * dps * items,
        ),
        name="score",
    )(
        wanted,
        all_gated,
        chosen,
        *other_chosen,
        w_out,
        *other_w_out,
        catalogue,
        *(in_hbm(x) for x in other_catalogues),
    )
    sums = lax.all_to_all(sums, COLUMN, split_axis=0, concat_axis=0, tiled=True)
    sums = jnp.sum(sums, axis=(0, 1))
    return (state, sums[imps:] - jnp.log(sums[:imps]))


def solution(mesh):
    placed = (
        P(("groups", "item", "dp"), None),
        P("groups"),
        P("groups"),
        P("groups", None),
        P("groups", None),
        P(None, "tensor"),
        P("tensor", None),
        P(("item", "dp", "tensor"), None),
    )
    return jax.shard_map(
        local,
        mesh=mesh,
        in_specs=placed,
        out_specs=(P(("groups", "item", "dp"), "tensor"), P(("groups", "item", "dp"))),
        check_vma=False,
    )
```

```python
import functools
import math

import jax
import jax.numpy as jnp
from jax import lax
from jax.experimental import pallas as pl
from jax.experimental.pallas import tpu as pltpu
from jax.sharding import PartitionSpec as P

DH = 128
SLOTS = ("item", "dp")
COLUMN = ("tensor", "item")
NT = (((1,), (1,)), ((), ()))
MIB = 1024 * 1024
EVENT_PARTS = 3


def rounds(count):
    return [0] + sorted(range(1, count), key=lambda r: (r & 3 == 3, -(r & -2)))


def spec(space):
    return pl.BlockSpec(memory_space=space)


def pick_kernel(
    shards,
    packing,
    lengths,
    positions,
    logged,
    events,
    w_uvqk,
    chosen,
    limits,
    wanted,
    events_v,
    done,
    w_uvqk_v,
    packing_s,
    lengths_s,
    positions_v,
    logged_v,
    sems,
):
    rows = events.shape[0]
    items_axis, dps = shards
    imps = positions.shape[1]
    part_rows = rows // EVENT_PARTS
    parts = [pl.ds(k * part_rows, part_rows) for k in range(EVENT_PARTS)]
    copies = [
        pltpu.make_async_copy(source, target, sems.at[k])
        for k, (source, target) in enumerate(
            [
                (packing, packing_s),
                (positions, positions_v),
                (lengths, lengths_s),
                (logged, logged_v),
            ]
            + [(events.at[part], events_v.at[part]) for part in parts]
            + [(w_uvqk, w_uvqk_v)]
        )
    ]
    for copy in copies[:-1]:
        copy.start()
    item, dp = lax.axis_index("item"), lax.axis_index("dp")
    early = is_early(item, items_axis)
    pl.when(early)(copies[-1].start)
    for copy in copies[:4]:
        copy.wait()
    history = packing_s[item * dps + dp]
    row = positions_v[pl.ds(history, 1), :].astype(jnp.float32)
    diagonal = lax.broadcasted_iota(jnp.int32, (imps, imps), 0) == lax.broadcasted_iota(
        jnp.int32, (imps, imps), 1
    )
    spots = jnp.sum(jnp.where(diagonal, row, 0.0), axis=1, keepdims=True).astype(jnp.int32)
    limits[...] = jnp.broadcast_to(jnp.minimum(spots, lengths_s[history] - 1), limits.shape)
    for k, r in enumerate(rounds(items_axis)):
        other = packing_s[(item ^ r) * dps + dp]
        wanted[0:1, k * imps : (k + 1) * imps] = logged_v[pl.ds(other, 1), :]
    total = jnp.zeros((imps, events.shape[1]), jnp.float32)
    for k in range(EVENT_PARTS):
        copies[4 + k].wait()
        lanes = k * part_rows + lax.broadcasted_iota(jnp.int32, (imps, part_rows), 1)
        one_hot = jnp.where(lanes == spots, 1.0, 0.0).astype(jnp.bfloat16)
        total += jnp.dot(
            one_hot,
            events_v[k * part_rows : (k + 1) * part_rows, :],
            preferred_element_type=jnp.float32,
        )
    chosen[...] = total.astype(jnp.bfloat16)

    @pl.when(early)
    def _():
        copies[-1].wait()
        attention(limits, events_v, chosen, w_uvqk_v, done)


def attention(limits, events, own, w_uvqk, store):
    lanes = lax.broadcasted_iota(jnp.int32, (own.shape[0], events.shape[0]), 1)
    valid = lanes <= limits[:, 0:1]
    for head in range(w_uvqk.shape[1] // (4 * DH)):
        first = head * 4 * DH
        w_part = [w_uvqk[:, first + k * DH : first + (k + 1) * DH] for k in range(4)]
        w_gate_query = jnp.concatenate([w_part[0], w_part[2]], axis=1)
        w_value_key = jnp.concatenate([w_part[1], w_part[3]], axis=1)
        gate_query = jnp.dot(own[...], w_gate_query, preferred_element_type=jnp.float32)
        gate_query = jax.nn.silu(gate_query).astype(jnp.bfloat16)
        value_key = jnp.dot(events[...], w_value_key, preferred_element_type=jnp.float32)
        value_key = jax.nn.silu(value_key).astype(jnp.bfloat16)
        scores = lax.dot_general(
            gate_query[:, DH:], value_key[:, DH:], NT, preferred_element_type=jnp.float32
        ) / math.sqrt(DH)
        weights = jnp.where(valid, jax.nn.silu(scores), 0.0).astype(jnp.bfloat16)
        attended = jnp.dot(weights, value_key[:, :DH], preferred_element_type=jnp.float32)
        inverse = lax.rsqrt(jnp.mean(attended * attended, axis=-1, keepdims=True) + 1e-06)
        store[:, head * DH : (head + 1) * DH] = (
            attended * inverse * gate_query[:, :DH].astype(jnp.float32)
        ).astype(jnp.bfloat16)


def is_early(item, items_axis):
    return item * 4 < items_axis


def attend_kernel(items_axis, limits, events, chosen, w_uvqk, done, gated, rows, sems):
    early = is_early(lax.axis_index("item"), items_axis)

    @pl.when(early)
    def _():
        rows[...] = done[...]

    @pl.when(jnp.logical_not(early))
    def _():
        attention(limits, events, chosen, w_uvqk, rows)

    copies = [pltpu.make_async_copy(rows, gated.at[k], sems.at[k]) for k in range(gated.shape[0])]
    for copy in copies:
        copy.start()
    for copy in copies:
        copy.wait()


def score_kernel(sizes, wanted, gated, *refs):
    items_axis, dps, tensors = sizes
    chosen, refs = refs[:items_axis], refs[items_axis:]
    w_out, refs = refs[:tensors], refs[tensors:]
    catalogue, refs = list(refs[:dps]), refs[dps:]
    state_hbm, sums, hidden, gates, others, sems, state_sem = refs
    fetches = [
        pltpu.make_async_copy(catalogue[d], others.at[d - 1], sems.at[d - 1]) for d in range(1, dps)
    ]
    for fetch in fetches:
        fetch.start()
    catalogue[1:] = [others.at[d - 1] for d in range(1, dps)]
    item, dp, tensor = (lax.axis_index(a) for a in ("item", "dp", "tensor"))
    imps = chosen[0].shape[0]
    items = catalogue[0].shape[0]
    step_rows = min(256, items_axis * imps)
    step_items = min(256, items)
    steps = range(0, items, step_items)
    slot_rounds, tensor_rounds = rounds(items_axis), rounds(tensors)
    local_width = w_out[0].shape[0]
    for k in range(items_axis):
        for t in range(tensors):
            sender = rank(item ^ slot_rounds[k], tensor ^ tensor_rounds[t], items_axis)
            gates[k * imps : (k + 1) * imps, t * local_width : (t + 1) * local_width] = gated[sender]
    w_whole = jnp.concatenate([w[...] for w in w_out], axis=0)
    mixed = jnp.dot(gates[...], w_whole, preferred_element_type=jnp.float32)
    for k in range(items_axis):
        rows = slice(k * imps, (k + 1) * imps)
        hidden[rows, :] = (mixed[rows] + chosen[k][...].astype(jnp.float32)).astype(jnp.bfloat16)
    share = state_hbm.shape[1]
    state_copy = pltpu.make_async_copy(
        hidden.at[pl.ds(0, imps), pl.ds(pl.multiple_of(tensor * share, share), share)],
        state_hbm,
        state_sem,
    )
    state_copy.start()

    blocks = range(0, items_axis * imps, step_rows)
    totals = {row: jnp.zeros((8, step_rows), jnp.float32) for row in blocks}
    targets = dict(totals)
    for d in range(dps):
        if d > 0:
            fetches[d - 1].wait()
        item_base = ((item * dps + (dp ^ rounds(dps)[d])) * tensors + tensor) * items
        ids = {row: wanted[0:1, row : row + step_rows] - item_base for row in blocks}
        for first in steps:
            for row in blocks:
                logits = lax.dot_general(
                    catalogue[d][first : first + step_items, :],
                    hidden[row : row + step_rows, :],
                    NT,
                    preferred_element_type=jnp.float32,
                )
                item_ids = lax.broadcasted_iota(jnp.int32, logits.shape, 0)
                found = jnp.where(item_ids == ids[row] - first, logits, 0.0)
                totals[row] += jnp.sum(jnp.exp(logits).reshape(-1, 8, step_rows), axis=0)
                targets[row] += jnp.sum(found.reshape(-1, 8, step_rows), axis=0)
    for row in blocks:
        total = jnp.sum(totals[row], axis=0, keepdims=True)
        target = jnp.sum(targets[row], axis=0, keepdims=True)
        for part in range(step_rows // imps):
            owner = item ^ slot_rounds[row // imps + part]
            both = jnp.concatenate(
                [v[:, part * imps : (part + 1) * imps] for v in (total, target)], axis=1
            )
            for t in range(tensors):
                sums[rank(owner, t, items_axis)] = both
    state_copy.wait()


def in_hbm(x):
    return pltpu.with_memory_space_constraint(x, pltpu.HBM)


def rank(item, tensor, items_axis):
    return tensor * items_axis + (item + items_axis - 1) % items_axis


def exchange(x, items_axis, tensors):
    group = [0] * (items_axis * tensors)
    for tensor in range(tensors):
        for item in range(items_axis):
            group[rank(item, tensor, items_axis)] = tensor * items_axis + item
    return lax.all_to_all(
        x, COLUMN, split_axis=0, concat_axis=0, tiled=True, axis_index_groups=[group]
    )


def send(x, axes, count, r):
    return lax.ppermute(x, axes, [(i, i ^ r) for i in range(count)])


def from_others(x, axes, count):
    pieces = {}
    for r in rounds(count)[1:]:
        if r & 3 == 3:
            held, pieces[r - 2] = lax.optimization_barrier((pieces[r - 1], pieces[r - 2]))
            pieces[r] = send(held, axes, count, 1)
        else:
            pieces[r] = send(x, axes, count, r)
    return list(pieces.values())


def local(events, lengths, packing, positions, logged, w_uvqk, w_out, catalogue):
    rows, width = events.shape
    imps = positions.shape[1]
    hists = packing.shape[0]
    items = catalogue.shape[0]
    local_width = w_out.shape[0]
    items_axis, dps, tensors = (lax.axis_size(a) for a in ("item", "dp", "tensor"))
    receivers = items_axis * tensors
    params = pltpu.CompilerParams(vmem_limit_bytes=(12 + 2 * items_axis) * MIB)
    vmem, hbm = spec(pltpu.VMEM), spec(pltpu.HBM)

    other_catalogues = from_others(catalogue, "dp", dps)
    other_w_out = from_others(w_out, "tensor", tensors)
    chosen, limits, wanted, events, done = pl.pallas_call(
        functools.partial(pick_kernel, (items_axis, dps)),
        out_shape=(
            jax.ShapeDtypeStruct((imps, width), jnp.bfloat16),
            jax.ShapeDtypeStruct((imps, 128), jnp.int32),
            jax.ShapeDtypeStruct((1, items_axis * imps), jnp.int32),
            jax.ShapeDtypeStruct(events.shape, events.dtype),
            jax.ShapeDtypeStruct((imps, local_width), jnp.bfloat16),
        ),
        in_specs=[hbm] * 6,
        out_specs=(vmem,) * 5,
        scratch_shapes=[
            pltpu.VMEM(w_uvqk.shape, w_uvqk.dtype),
            pltpu.SMEM((hists,), jnp.int32),
            pltpu.SMEM((hists,), jnp.int32),
            pltpu.VMEM((hists, imps), jnp.int32),
            pltpu.VMEM((hists, imps), jnp.int32),
            pltpu.SemaphoreType.DMA((5 + EVENT_PARTS,)),
        ],
        compiler_params=params,
        cost_estimate=pl.CostEstimate(
            flops=2 * imps * rows * width, bytes_accessed=2 * rows * width, transcendentals=0
        ),
        name="pick",
    )(*(in_hbm(x) for x in (packing, lengths, positions, logged, events, w_uvqk)))
    other_chosen = from_others(chosen, "item", items_axis)

    gated = pl.pallas_call(
        functools.partial(attend_kernel, items_axis),
        out_shape=pltpu.HBM((receivers, imps, local_width), jnp.bfloat16),
        in_specs=[vmem] * 5,
        out_specs=hbm,
        scratch_shapes=[
            pltpu.VMEM((imps, local_width), jnp.bfloat16),
            pltpu.SemaphoreType.DMA((receivers,)),
        ],
        compiler_params=params,
        cost_estimate=pl.CostEstimate(flops=0, bytes_accessed=0, transcendentals=0),
        name="attend",
    )(limits, events, chosen, w_uvqk, done)
    all_gated = exchange(gated, items_axis, tensors)

    state, sums = pl.pallas_call(
        functools.partial(score_kernel, (items_axis, dps, tensors)),
        out_shape=(
            jax.ShapeDtypeStruct((imps, width // tensors), jnp.bfloat16),
            jax.ShapeDtypeStruct((receivers, 1, 2 * imps), jnp.float32),
        ),
        in_specs=[vmem] * (3 + items_axis + tensors) + [hbm] * (dps - 1),
        out_specs=(hbm, vmem),
        scratch_shapes=[
            pltpu.VMEM((items_axis * imps, width), jnp.bfloat16),
            pltpu.VMEM((items_axis * imps, local_width * tensors), jnp.bfloat16),
            pltpu.VMEM((dps - 1, items, width), jnp.bfloat16),
            pltpu.SemaphoreType.DMA((dps - 1,)),
            pltpu.SemaphoreType.DMA,
        ],
        compiler_params=params,
        cost_estimate=pl.CostEstimate(
            flops=2 * items_axis * imps * width * (dps * items + local_width * tensors),
            bytes_accessed=2 * dps * items * width,
            transcendentals=items_axis * imps * dps * items,
        ),
        name="score",
    )(
        wanted,
        all_gated,
        chosen,
        *other_chosen,
        w_out,
        *other_w_out,
        catalogue,
        *(in_hbm(x) for x in other_catalogues),
    )
    sums = exchange(sums, items_axis, tensors)
    sums = jnp.sum(sums, axis=(0, 1))
    return (state, sums[imps:] - jnp.log(sums[:imps]))


def solution(mesh):
    placed = (
        P(("groups", "item", "dp"), None),
        P("groups"),
        P("groups"),
        P("groups", None),
        P("groups", None),
        P(None, "tensor"),
        P("tensor", None),
        P(("item", "dp", "tensor"), None),
    )
    return jax.shard_map(
        local,
        mesh=mesh,
        in_specs=placed,
        out_specs=(P(("groups", "item", "dp"), "tensor"), P(("groups", "item", "dp"))),
        check_vma=False,
    )
```

```python
import functools
import math

import jax
import jax.numpy as jnp
from jax import lax
from jax.experimental import pallas as pl
from jax.experimental.pallas import tpu as pltpu
from jax.sharding import PartitionSpec as P

DH = 128
SLOTS = ("item", "dp")
COLUMN = ("tensor", "item")
NT = (((1,), (1,)), ((), ()))
MIB = 1024 * 1024
EVENT_PARTS = 3


def rounds(count):
    return [0] + sorted(range(1, count), key=lambda r: (r & 3 == 3, -(r & -2)))


def spec(space):
    return pl.BlockSpec(memory_space=space)


def pick_kernel(
    shards,
    packing,
    lengths,
    positions,
    logged,
    events,
    w_uvqk,
    chosen,
    limits,
    wanted,
    events_v,
    done,
    w_uvqk_v,
    packing_s,
    lengths_s,
    positions_v,
    logged_v,
    sems,
):
    rows = events.shape[0]
    items_axis, dps = shards
    imps = positions.shape[1]
    part_rows = rows // EVENT_PARTS
    parts = [pl.ds(k * part_rows, part_rows) for k in range(EVENT_PARTS)]
    copies = [
        pltpu.make_async_copy(source, target, sems.at[k])
        for k, (source, target) in enumerate(
            [
                (packing, packing_s),
                (positions, positions_v),
                (lengths, lengths_s),
                (logged, logged_v),
            ]
            + [(events.at[part], events_v.at[part]) for part in parts]
            + [(w_uvqk, w_uvqk_v)]
        )
    ]
    for copy in copies[:-1]:
        copy.start()
    item, dp = lax.axis_index("item"), lax.axis_index("dp")
    early = is_early(item, items_axis)
    pl.when(early)(copies[-1].start)
    for copy in copies[:4]:
        copy.wait()
    history = packing_s[item * dps + dp]
    row = positions_v[pl.ds(history, 1), :].astype(jnp.float32)
    diagonal = lax.broadcasted_iota(jnp.int32, (imps, imps), 0) == lax.broadcasted_iota(
        jnp.int32, (imps, imps), 1
    )
    spots = jnp.sum(jnp.where(diagonal, row, 0.0), axis=1, keepdims=True).astype(jnp.int32)
    limits[...] = jnp.broadcast_to(jnp.minimum(spots, lengths_s[history] - 1), limits.shape)
    for k, r in enumerate(rounds(items_axis)):
        other = packing_s[(item ^ r) * dps + dp]
        wanted[0:1, k * imps : (k + 1) * imps] = logged_v[pl.ds(other, 1), :]
    total = jnp.zeros((imps, events.shape[1]), jnp.float32)
    for k in range(EVENT_PARTS):
        copies[4 + k].wait()
        lanes = k * part_rows + lax.broadcasted_iota(jnp.int32, (imps, part_rows), 1)
        one_hot = jnp.where(lanes == spots, 1.0, 0.0).astype(jnp.bfloat16)
        total += jnp.dot(
            one_hot,
            events_v[k * part_rows : (k + 1) * part_rows, :],
            preferred_element_type=jnp.float32,
        )
    chosen[...] = total.astype(jnp.bfloat16)

    @pl.when(early)
    def _():
        copies[-1].wait()
        attention(limits, events_v, chosen, w_uvqk_v, done)


def attention(limits, events, own, w_uvqk, store):
    lanes = lax.broadcasted_iota(jnp.int32, (own.shape[0], events.shape[0]), 1)
    valid = lanes <= limits[:, 0:1]
    for head in range(w_uvqk.shape[1] // (4 * DH)):
        first = head * 4 * DH
        w_part = [w_uvqk[:, first + k * DH : first + (k + 1) * DH] for k in range(4)]
        w_gate_query = jnp.concatenate([w_part[0], w_part[2]], axis=1)
        w_value_key = jnp.concatenate([w_part[1], w_part[3]], axis=1)
        gate_query = jnp.dot(own[...], w_gate_query, preferred_element_type=jnp.float32)
        gate_query = jax.nn.silu(gate_query).astype(jnp.bfloat16)
        value_key = jnp.dot(events[...], w_value_key, preferred_element_type=jnp.float32)
        value_key = jax.nn.silu(value_key).astype(jnp.bfloat16)
        scores = lax.dot_general(
            gate_query[:, DH:], value_key[:, DH:], NT, preferred_element_type=jnp.float32
        ) / math.sqrt(DH)
        weights = jnp.where(valid, jax.nn.silu(scores), 0.0).astype(jnp.bfloat16)
        attended = jnp.dot(weights, value_key[:, :DH], preferred_element_type=jnp.float32)
        inverse = lax.rsqrt(jnp.mean(attended * attended, axis=-1, keepdims=True) + 1e-06)
        store[:, head * DH : (head + 1) * DH] = (
            attended * inverse * gate_query[:, :DH].astype(jnp.float32)
        ).astype(jnp.bfloat16)


def is_early(item, items_axis):
    return item * 4 < items_axis


def attend_kernel(items_axis, limits, events, chosen, w_uvqk, done, gated, rows, sems):
    early = is_early(lax.axis_index("item"), items_axis)

    @pl.when(early)
    def _():
        rows[...] = done[...]

    @pl.when(jnp.logical_not(early))
    def _():
        attention(limits, events, chosen, w_uvqk, rows)

    copies = [pltpu.make_async_copy(rows, gated.at[k], sems.at[k]) for k in range(gated.shape[0])]
    for copy in copies:
        copy.start()
    for copy in copies:
        copy.wait()


def score_kernel(sizes, wanted, gated, *refs):
    items_axis, dps, tensors = sizes
    chosen, refs = refs[:items_axis], refs[items_axis:]
    w_out, refs = refs[:tensors], refs[tensors:]
    catalogue, refs = list(refs[:dps]), refs[dps:]
    state_hbm, sums, hidden, gates, others, sems, state_sem = refs
    fetches = [
        pltpu.make_async_copy(catalogue[d], others.at[d - 1], sems.at[d - 1]) for d in range(1, dps)
    ]
    for fetch in fetches:
        fetch.start()
    catalogue[1:] = [others.at[d - 1] for d in range(1, dps)]
    item, dp, tensor = (lax.axis_index(a) for a in ("item", "dp", "tensor"))
    imps = chosen[0].shape[0]
    items = catalogue[0].shape[0]
    step_rows = min(256, items_axis * imps)
    step_items = min(256, items)
    steps = range(0, items, step_items)
    slot_rounds, tensor_rounds = rounds(items_axis), rounds(tensors)
    local_width = w_out[0].shape[0]
    for k in range(items_axis):
        for t in range(tensors):
            other, head = item ^ slot_rounds[k], tensor ^ tensor_rounds[t]
            sender = rank(other, head, items_axis, items_axis // 2)
            gates[k * imps : (k + 1) * imps, t * local_width : (t + 1) * local_width] = gated[sender]
    w_whole = jnp.concatenate([w[...] for w in w_out], axis=0)
    mixed = jnp.dot(gates[...], w_whole, preferred_element_type=jnp.float32)
    for k in range(items_axis):
        rows = slice(k * imps, (k + 1) * imps)
        hidden[rows, :] = (mixed[rows] + chosen[k][...].astype(jnp.float32)).astype(jnp.bfloat16)
    share = state_hbm.shape[1]
    state_copy = pltpu.make_async_copy(
        hidden.at[pl.ds(0, imps), pl.ds(pl.multiple_of(tensor * share, share), share)],
        state_hbm,
        state_sem,
    )
    state_copy.start()

    blocks = range(0, items_axis * imps, step_rows)
    totals = {row: jnp.zeros((8, step_rows), jnp.float32) for row in blocks}
    targets = dict(totals)
    for d in range(dps):
        if d > 0:
            fetches[d - 1].wait()
        item_base = ((item * dps + (dp ^ rounds(dps)[d])) * tensors + tensor) * items
        ids = {row: wanted[0:1, row : row + step_rows] - item_base for row in blocks}
        for first in steps:
            for row in blocks:
                logits = lax.dot_general(
                    catalogue[d][first : first + step_items, :],
                    hidden[row : row + step_rows, :],
                    NT,
                    preferred_element_type=jnp.float32,
                )
                item_ids = lax.broadcasted_iota(jnp.int32, logits.shape, 0)
                found = jnp.where(item_ids == ids[row] - first, logits, 0.0)
                totals[row] += jnp.sum(jnp.exp(logits).reshape(-1, 8, step_rows), axis=0)
                targets[row] += jnp.sum(found.reshape(-1, 8, step_rows), axis=0)
    for row in blocks:
        total = jnp.sum(totals[row], axis=0, keepdims=True)
        target = jnp.sum(targets[row], axis=0, keepdims=True)
        for part in range(step_rows // imps):
            owner = item ^ slot_rounds[row // imps + part]
            both = jnp.concatenate(
                [v[:, part * imps : (part + 1) * imps] for v in (total, target)], axis=1
            )
            for t in range(tensors):
                sums[rank(owner, t, items_axis, items_axis - 1)] = both
    state_copy.wait()


def in_hbm(x):
    return pltpu.with_memory_space_constraint(x, pltpu.HBM)


def rank(item, tensor, items_axis, first):
    return tensor * items_axis + (item + items_axis - first) % items_axis


def exchange(x, items_axis, tensors, first):
    group = [0] * (items_axis * tensors)
    for tensor in range(tensors):
        for item in range(items_axis):
            group[rank(item, tensor, items_axis, first)] = tensor * items_axis + item
    return lax.all_to_all(
        x, COLUMN, split_axis=0, concat_axis=0, tiled=True, axis_index_groups=[group]
    )


def send(x, axes, count, r):
    return lax.ppermute(x, axes, [(i, i ^ r) for i in range(count)])


def from_others(x, axes, count):
    pieces = {}
    for r in rounds(count)[1:]:
        if r & 3 == 3:
            held, pieces[r - 2] = lax.optimization_barrier((pieces[r - 1], pieces[r - 2]))
            pieces[r] = send(held, axes, count, 1)
        else:
            pieces[r] = send(x, axes, count, r)
    return list(pieces.values())


def local(events, lengths, packing, positions, logged, w_uvqk, w_out, catalogue):
    rows, width = events.shape
    imps = positions.shape[1]
    hists = packing.shape[0]
    items = catalogue.shape[0]
    local_width = w_out.shape[0]
    items_axis, dps, tensors = (lax.axis_size(a) for a in ("item", "dp", "tensor"))
    receivers = items_axis * tensors
    params = pltpu.CompilerParams(vmem_limit_bytes=(12 + 2 * items_axis) * MIB)
    vmem, hbm = spec(pltpu.VMEM), spec(pltpu.HBM)

    other_catalogues = from_others(catalogue, "dp", dps)
    other_w_out = from_others(w_out, "tensor", tensors)
    chosen, limits, wanted, events, done = pl.pallas_call(
        functools.partial(pick_kernel, (items_axis, dps)),
        out_shape=(
            jax.ShapeDtypeStruct((imps, width), jnp.bfloat16),
            jax.ShapeDtypeStruct((imps, 128), jnp.int32),
            jax.ShapeDtypeStruct((1, items_axis * imps), jnp.int32),
            jax.ShapeDtypeStruct(events.shape, events.dtype),
            jax.ShapeDtypeStruct((imps, local_width), jnp.bfloat16),
        ),
        in_specs=[hbm] * 6,
        out_specs=(vmem,) * 5,
        scratch_shapes=[
            pltpu.VMEM(w_uvqk.shape, w_uvqk.dtype),
            pltpu.SMEM((hists,), jnp.int32),
            pltpu.SMEM((hists,), jnp.int32),
            pltpu.VMEM((hists, imps), jnp.int32),
            pltpu.VMEM((hists, imps), jnp.int32),
            pltpu.SemaphoreType.DMA((5 + EVENT_PARTS,)),
        ],
        compiler_params=params,
        cost_estimate=pl.CostEstimate(
            flops=2 * imps * rows * width, bytes_accessed=2 * rows * width, transcendentals=0
        ),
        name="pick",
    )(*(in_hbm(x) for x in (packing, lengths, positions, logged, events, w_uvqk)))
    other_chosen = from_others(chosen, "item", items_axis)

    gated = pl.pallas_call(
        functools.partial(attend_kernel, items_axis),
        out_shape=pltpu.HBM((receivers, imps, local_width), jnp.bfloat16),
        in_specs=[vmem] * 5,
        out_specs=hbm,
        scratch_shapes=[
            pltpu.VMEM((imps, local_width), jnp.bfloat16),
            pltpu.SemaphoreType.DMA((receivers,)),
        ],
        compiler_params=params,
        cost_estimate=pl.CostEstimate(flops=0, bytes_accessed=0, transcendentals=0),
        name="attend",
    )(limits, events, chosen, w_uvqk, done)
    all_gated = exchange(gated, items_axis, tensors, items_axis // 2)

    state, sums = pl.pallas_call(
        functools.partial(score_kernel, (items_axis, dps, tensors)),
        out_shape=(
            jax.ShapeDtypeStruct((imps, width // tensors), jnp.bfloat16),
            jax.ShapeDtypeStruct((receivers, 1, 2 * imps), jnp.float32),
        ),
        in_specs=[vmem] * (3 + items_axis + tensors) + [hbm] * (dps - 1),
        out_specs=(hbm, vmem),
        scratch_shapes=[
            pltpu.VMEM((items_axis * imps, width), jnp.bfloat16),
            pltpu.VMEM((items_axis * imps, local_width * tensors), jnp.bfloat16),
            pltpu.VMEM((dps - 1, items, width), jnp.bfloat16),
            pltpu.SemaphoreType.DMA((dps - 1,)),
            pltpu.SemaphoreType.DMA,
        ],
        compiler_params=params,
        cost_estimate=pl.CostEstimate(
            flops=2 * items_axis * imps * width * (dps * items + local_width * tensors),
            bytes_accessed=2 * dps * items * width,
            transcendentals=items_axis * imps * dps * items,
        ),
        name="score",
    )(
        wanted,
        all_gated,
        chosen,
        *other_chosen,
        w_out,
        *other_w_out,
        catalogue,
        *(in_hbm(x) for x in other_catalogues),
    )
    sums = exchange(sums, items_axis, tensors, items_axis - 1)
    sums = jnp.sum(sums, axis=(0, 1))
    return (state, sums[imps:] - jnp.log(sums[:imps]))


def solution(mesh):
    placed = (
        P(("groups", "item", "dp"), None),
        P("groups"),
        P("groups"),
        P("groups", None),
        P("groups", None),
        P(None, "tensor"),
        P("tensor", None),
        P(("item", "dp", "tensor"), None),
    )
    return jax.shard_map(
        local,
        mesh=mesh,
        in_specs=placed,
        out_specs=(P(("groups", "item", "dp"), "tensor"), P(("groups", "item", "dp"))),
        check_vma=False,
    )
```

```python
import functools
import math

import jax
import jax.numpy as jnp
from jax import lax
from jax.experimental import pallas as pl
from jax.experimental.pallas import tpu as pltpu
from jax.sharding import PartitionSpec as P

DH = 128
SLOTS = ("item", "dp")
COLUMN = ("tensor", "item")
NT = (((1,), (1,)), ((), ()))
MIB = 1024 * 1024
EVENT_PARTS = 3


def rounds(count):
    return [0] + sorted(range(1, count), key=lambda r: (r & 3 == 3, -(r & -2)))


def spec(space):
    return pl.BlockSpec(memory_space=space)


def pick_kernel(
    shards,
    packing,
    lengths,
    positions,
    logged,
    events,
    w_uvqk,
    chosen,
    limits,
    wanted,
    events_v,
    w_uvqk_v,
    done,
    packing_s,
    lengths_s,
    positions_v,
    logged_v,
    sems,
):
    rows = events.shape[0]
    items_axis, dps = shards
    imps = positions.shape[1]
    part_rows = rows // EVENT_PARTS
    parts = [pl.ds(k * part_rows, part_rows) for k in range(EVENT_PARTS)]
    copies = [
        pltpu.make_async_copy(source, target, sems.at[k])
        for k, (source, target) in enumerate(
            [
                (packing, packing_s),
                (positions, positions_v),
                (lengths, lengths_s),
                (logged, logged_v),
            ]
            + [(events.at[part], events_v.at[part]) for part in parts]
            + [(w_uvqk, w_uvqk_v)]
        )
    ]
    for copy in copies:
        copy.start()
    for copy in copies[:4]:
        copy.wait()
    item, dp = lax.axis_index("item"), lax.axis_index("dp")
    history = packing_s[item * dps + dp]
    row = positions_v[pl.ds(history, 1), :].astype(jnp.float32)
    diagonal = lax.broadcasted_iota(jnp.int32, (imps, imps), 0) == lax.broadcasted_iota(
        jnp.int32, (imps, imps), 1
    )
    spots = jnp.sum(jnp.where(diagonal, row, 0.0), axis=1, keepdims=True).astype(jnp.int32)
    limits[...] = jnp.broadcast_to(jnp.minimum(spots, lengths_s[history] - 1), limits.shape)
    for k, r in enumerate(rounds(items_axis)):
        other = packing_s[(item ^ r) * dps + dp]
        wanted[0:1, k * imps : (k + 1) * imps] = logged_v[pl.ds(other, 1), :]
    total = jnp.zeros((imps, events.shape[1]), jnp.float32)
    for k in range(EVENT_PARTS):
        copies[4 + k].wait()
        lanes = k * part_rows + lax.broadcasted_iota(jnp.int32, (imps, part_rows), 1)
        one_hot = jnp.where(lanes == spots, 1.0, 0.0).astype(jnp.bfloat16)
        total += jnp.dot(
            one_hot,
            events_v[k * part_rows : (k + 1) * part_rows, :],
            preferred_element_type=jnp.float32,
        )
    chosen[...] = total.astype(jnp.bfloat16)
    copies[-1].wait()

    @pl.when(is_early(item, items_axis))
    def _():
        attention(limits, events_v, chosen, w_uvqk_v, done)


def attention(limits, events, own, w_uvqk, store):
    lanes = lax.broadcasted_iota(jnp.int32, (own.shape[0], events.shape[0]), 1)
    valid = lanes <= limits[:, 0:1]
    for head in range(w_uvqk.shape[1] // (4 * DH)):
        first = head * 4 * DH
        w_part = [w_uvqk[:, first + k * DH : first + (k + 1) * DH] for k in range(4)]
        w_gate_query = jnp.concatenate([w_part[0], w_part[2]], axis=1)
        w_value_key = jnp.concatenate([w_part[1], w_part[3]], axis=1)
        gate_query = jnp.dot(own[...], w_gate_query, preferred_element_type=jnp.float32)
        gate_query = jax.nn.silu(gate_query).astype(jnp.bfloat16)
        value_key = jnp.dot(events[...], w_value_key, preferred_element_type=jnp.float32)
        value_key = jax.nn.silu(value_key).astype(jnp.bfloat16)
        scores = lax.dot_general(
            gate_query[:, DH:], value_key[:, DH:], NT, preferred_element_type=jnp.float32
        ) / math.sqrt(DH)
        weights = jnp.where(valid, jax.nn.silu(scores), 0.0).astype(jnp.bfloat16)
        attended = jnp.dot(weights, value_key[:, :DH], preferred_element_type=jnp.float32)
        inverse = lax.rsqrt(jnp.mean(attended * attended, axis=-1, keepdims=True) + 1e-06)
        store[:, head * DH : (head + 1) * DH] = (
            attended * inverse * gate_query[:, :DH].astype(jnp.float32)
        ).astype(jnp.bfloat16)


def is_early(item, items_axis):
    return item * 4 < items_axis


def attend_kernel(items_axis, limits, events, chosen, w_uvqk, done, gated, rows, sems):
    early = is_early(lax.axis_index("item"), items_axis)

    @pl.when(early)
    def _():
        rows[...] = done[...]

    @pl.when(jnp.logical_not(early))
    def _():
        attention(limits, events, chosen, w_uvqk, rows)

    copies = [pltpu.make_async_copy(rows, gated.at[k], sems.at[k]) for k in range(gated.shape[0])]
    for copy in copies:
        copy.start()
    for copy in copies:
        copy.wait()


def score_kernel(sizes, wanted, gated, *refs):
    items_axis, dps, tensors = sizes
    chosen, refs = refs[:items_axis], refs[items_axis:]
    w_out, refs = refs[:tensors], refs[tensors:]
    catalogue, refs = list(refs[:dps]), refs[dps:]
    state_hbm, sums, hidden, gates, others, sems, state_sem = refs
    fetches = [
        pltpu.make_async_copy(catalogue[d], others.at[d - 1], sems.at[d - 1]) for d in range(1, dps)
    ]
    for fetch in fetches:
        fetch.start()
    catalogue[1:] = [others.at[d - 1] for d in range(1, dps)]
    item, dp, tensor = (lax.axis_index(a) for a in ("item", "dp", "tensor"))
    imps = chosen[0].shape[0]
    items = catalogue[0].shape[0]
    step_rows = min(256, items_axis * imps)
    step_items = min(256, items)
    steps = range(0, items, step_items)
    slot_rounds, tensor_rounds = rounds(items_axis), rounds(tensors)
    local_width = w_out[0].shape[0]
    for k in range(items_axis):
        for t in range(tensors):
            other, head = item ^ slot_rounds[k], tensor ^ tensor_rounds[t]
            sender = rank(other, head, items_axis, items_axis // 2)
            gates[k * imps : (k + 1) * imps, t * local_width : (t + 1) * local_width] = gated[sender]
    w_whole = jnp.concatenate([w[...] for w in w_out], axis=0)
    mixed = jnp.dot(gates[...], w_whole, preferred_element_type=jnp.float32)
    for k in range(items_axis):
        rows = slice(k * imps, (k + 1) * imps)
        hidden[rows, :] = (mixed[rows] + chosen[k][...].astype(jnp.float32)).astype(jnp.bfloat16)
    share = state_hbm.shape[1]
    state_copy = pltpu.make_async_copy(
        hidden.at[pl.ds(0, imps), pl.ds(pl.multiple_of(tensor * share, share), share)],
        state_hbm,
        state_sem,
    )
    state_copy.start()

    blocks = range(0, items_axis * imps, step_rows)
    totals = {row: jnp.zeros((8, step_rows), jnp.float32) for row in blocks}
    targets = dict(totals)
    for d in range(dps):
        if d > 0:
            fetches[d - 1].wait()
        item_base = ((item * dps + (dp ^ rounds(dps)[d])) * tensors + tensor) * items
        ids = {row: wanted[0:1, row : row + step_rows] - item_base for row in blocks}
        for first in steps:
            for row in blocks:
                logits = lax.dot_general(
                    catalogue[d][first : first + step_items, :],
                    hidden[row : row + step_rows, :],
                    NT,
                    preferred_element_type=jnp.float32,
                )
                item_ids = lax.broadcasted_iota(jnp.int32, logits.shape, 0)
                found = jnp.where(item_ids == ids[row] - first, logits, 0.0)
                totals[row] += jnp.sum(jnp.exp(logits).reshape(-1, 8, step_rows), axis=0)
                targets[row] += jnp.sum(found.reshape(-1, 8, step_rows), axis=0)
    for row in blocks:
        total = jnp.sum(totals[row], axis=0, keepdims=True)
        target = jnp.sum(targets[row], axis=0, keepdims=True)
        for part in range(step_rows // imps):
            owner = item ^ slot_rounds[row // imps + part]
            both = jnp.concatenate(
                [v[:, part * imps : (part + 1) * imps] for v in (total, target)], axis=1
            )
            for t in range(tensors):
                sums[rank(owner, t, items_axis, items_axis - 1)] = both
    state_copy.wait()


def in_hbm(x):
    return pltpu.with_memory_space_constraint(x, pltpu.HBM)


def rank(item, tensor, items_axis, first):
    tensor = lax.axis_size("tensor") - 1 - tensor
    return tensor * items_axis + (item + items_axis - first) % items_axis


def exchange(x, items_axis, tensors, first):
    group = [0] * (items_axis * tensors)
    for tensor in range(tensors):
        for item in range(items_axis):
            group[rank(item, tensor, items_axis, first)] = tensor * items_axis + item
    return lax.all_to_all(
        x, COLUMN, split_axis=0, concat_axis=0, tiled=True, axis_index_groups=[group]
    )


def send(x, axes, count, r):
    return lax.ppermute(x, axes, [(i, i ^ r) for i in range(count)])


def from_others(x, axes, count):
    pieces = {}
    for r in rounds(count)[1:]:
        if r & 3 == 3:
            held, pieces[r - 2] = lax.optimization_barrier((pieces[r - 1], pieces[r - 2]))
            pieces[r] = send(held, axes, count, 1)
        else:
            pieces[r] = send(x, axes, count, r)
    return list(pieces.values())


def local(events, lengths, packing, positions, logged, w_uvqk, w_out, catalogue):
    rows, width = events.shape
    imps = positions.shape[1]
    hists = packing.shape[0]
    items = catalogue.shape[0]
    local_width = w_out.shape[0]
    items_axis, dps, tensors = (lax.axis_size(a) for a in ("item", "dp", "tensor"))
    receivers = items_axis * tensors
    params = pltpu.CompilerParams(vmem_limit_bytes=(12 + 2 * items_axis) * MIB)
    vmem, hbm = spec(pltpu.VMEM), spec(pltpu.HBM)

    other_catalogues = from_others(catalogue, "dp", dps)
    other_w_out = from_others(w_out, "tensor", tensors)
    chosen, limits, wanted, events, w_uvqk, done = pl.pallas_call(
        functools.partial(pick_kernel, (items_axis, dps)),
        out_shape=(
            jax.ShapeDtypeStruct((imps, width), jnp.bfloat16),
            jax.ShapeDtypeStruct((imps, 128), jnp.int32),
            jax.ShapeDtypeStruct((1, items_axis * imps), jnp.int32),
            jax.ShapeDtypeStruct(events.shape, events.dtype),
            jax.ShapeDtypeStruct(w_uvqk.shape, w_uvqk.dtype),
            jax.ShapeDtypeStruct((imps, local_width), jnp.bfloat16),
        ),
        in_specs=[hbm] * 6,
        out_specs=(vmem,) * 6,
        scratch_shapes=[
            pltpu.SMEM((hists,), jnp.int32),
            pltpu.SMEM((hists,), jnp.int32),
            pltpu.VMEM((hists, imps), jnp.int32),
            pltpu.VMEM((hists, imps), jnp.int32),
            pltpu.SemaphoreType.DMA((5 + EVENT_PARTS,)),
        ],
        compiler_params=params,
        cost_estimate=pl.CostEstimate(
            flops=2 * imps * rows * width, bytes_accessed=2 * rows * width, transcendentals=0
        ),
        name="pick",
    )(*(in_hbm(x) for x in (packing, lengths, positions, logged, events, w_uvqk)))
    other_chosen = from_others(chosen, "item", items_axis)

    gated = pl.pallas_call(
        functools.partial(attend_kernel, items_axis),
        out_shape=pltpu.HBM((receivers, imps, local_width), jnp.bfloat16),
        in_specs=[vmem] * 5,
        out_specs=hbm,
        scratch_shapes=[
            pltpu.VMEM((imps, local_width), jnp.bfloat16),
            pltpu.SemaphoreType.DMA((receivers,)),
        ],
        compiler_params=params,
        cost_estimate=pl.CostEstimate(flops=0, bytes_accessed=0, transcendentals=0),
        name="attend",
    )(limits, events, chosen, w_uvqk, done)
    all_gated = exchange(gated, items_axis, tensors, items_axis // 2)

    state, sums = pl.pallas_call(
        functools.partial(score_kernel, (items_axis, dps, tensors)),
        out_shape=(
            jax.ShapeDtypeStruct((imps, width // tensors), jnp.bfloat16),
            jax.ShapeDtypeStruct((receivers, 1, 2 * imps), jnp.float32),
        ),
        in_specs=[vmem] * (3 + items_axis + tensors) + [hbm] * (dps - 1),
        out_specs=(hbm, vmem),
        scratch_shapes=[
            pltpu.VMEM((items_axis * imps, width), jnp.bfloat16),
            pltpu.VMEM((items_axis * imps, local_width * tensors), jnp.bfloat16),
            pltpu.VMEM((dps - 1, items, width), jnp.bfloat16),
            pltpu.SemaphoreType.DMA((dps - 1,)),
            pltpu.SemaphoreType.DMA,
        ],
        compiler_params=params,
        cost_estimate=pl.CostEstimate(
            flops=2 * items_axis * imps * width * (dps * items + local_width * tensors),
            bytes_accessed=2 * dps * items * width,
            transcendentals=items_axis * imps * dps * items,
        ),
        name="score",
    )(
        wanted,
        all_gated,
        chosen,
        *other_chosen,
        w_out,
        *other_w_out,
        catalogue,
        *(in_hbm(x) for x in other_catalogues),
    )
    sums = exchange(sums, items_axis, tensors, items_axis - 1)
    sums = jnp.sum(sums, axis=(0, 1))
    return (state, sums[imps:] - jnp.log(sums[:imps]))


def solution(mesh):
    placed = (
        P(("groups", "item", "dp"), None),
        P("groups"),
        P("groups"),
        P("groups", None),
        P("groups", None),
        P(None, "tensor"),
        P("tensor", None),
        P(("item", "dp", "tensor"), None),
    )
    return jax.shard_map(
        local,
        mesh=mesh,
        in_specs=placed,
        out_specs=(P(("groups", "item", "dp"), "tensor"), P(("groups", "item", "dp"))),
        check_vma=False,
    )
```

```python
import functools
import math

import jax
import jax.numpy as jnp
from jax import lax
from jax.experimental import pallas as pl
from jax.experimental.pallas import tpu as pltpu
from jax.sharding import PartitionSpec as P

DH = 128
SLOTS = ("item", "dp")
COLUMN = ("tensor", "item")
NT = (((1,), (1,)), ((), ()))
MIB = 1024 * 1024
EVENT_PARTS = 3


def rounds(count):
    return [0] + sorted(range(1, count), key=lambda r: (r & 3 == 3, -(r & -2)))


def spec(space):
    return pl.BlockSpec(memory_space=space)


def pick_kernel(
    shards,
    packing,
    lengths,
    positions,
    logged,
    events,
    w_uvqk,
    chosen,
    limits,
    wanted,
    events_v,
    w_uvqk_v,
    done,
    packing_s,
    lengths_s,
    positions_v,
    logged_v,
    sems,
):
    rows = events.shape[0]
    items_axis, dps = shards
    imps = positions.shape[1]
    part_rows = rows // EVENT_PARTS
    parts = [pl.ds(k * part_rows, part_rows) for k in range(EVENT_PARTS)]
    copies = [
        pltpu.make_async_copy(source, target, sems.at[k])
        for k, (source, target) in enumerate(
            [
                (packing, packing_s),
                (positions, positions_v),
                (lengths, lengths_s),
                (logged, logged_v),
            ]
            + [(events.at[part], events_v.at[part]) for part in parts]
            + [(w_uvqk, w_uvqk_v)]
        )
    ]
    for copy in copies:
        copy.start()
    for copy in copies[:4]:
        copy.wait()
    item, dp = lax.axis_index("item"), lax.axis_index("dp")
    history = packing_s[item * dps + dp]
    row = positions_v[pl.ds(history, 1), :].astype(jnp.float32)
    diagonal = lax.broadcasted_iota(jnp.int32, (imps, imps), 0) == lax.broadcasted_iota(
        jnp.int32, (imps, imps), 1
    )
    spots = jnp.sum(jnp.where(diagonal, row, 0.0), axis=1, keepdims=True).astype(jnp.int32)
    limits[...] = jnp.broadcast_to(jnp.minimum(spots, lengths_s[history] - 1), limits.shape)
    for k, r in enumerate(rounds(items_axis)):
        other = packing_s[(item ^ r) * dps + dp]
        wanted[0:1, k * imps : (k + 1) * imps] = logged_v[pl.ds(other, 1), :]
    total = jnp.zeros((imps, events.shape[1]), jnp.float32)
    for k in range(EVENT_PARTS):
        copies[4 + k].wait()
        lanes = k * part_rows + lax.broadcasted_iota(jnp.int32, (imps, part_rows), 1)
        one_hot = jnp.where(lanes == spots, 1.0, 0.0).astype(jnp.bfloat16)
        total += jnp.dot(
            one_hot,
            events_v[k * part_rows : (k + 1) * part_rows, :],
            preferred_element_type=jnp.float32,
        )
    chosen[...] = total.astype(jnp.bfloat16)
    copies[-1].wait()

    @pl.when(is_early(item, items_axis))
    def _():
        attention(limits, events_v, chosen, w_uvqk_v, done)


def attention(limits, events, own, w_uvqk, store):
    lanes = lax.broadcasted_iota(jnp.int32, (own.shape[0], events.shape[0]), 1)
    valid = lanes <= limits[:, 0:1]
    for head in range(w_uvqk.shape[1] // (4 * DH)):
        first = head * 4 * DH
        w_part = [w_uvqk[:, first + k * DH : first + (k + 1) * DH] for k in range(4)]
        w_gate_query = jnp.concatenate([w_part[0], w_part[2]], axis=1)
        w_value_key = jnp.concatenate([w_part[1], w_part[3]], axis=1)
        gate_query = jnp.dot(own[...], w_gate_query, preferred_element_type=jnp.float32)
        gate_query = jax.nn.silu(gate_query).astype(jnp.bfloat16)
        value_key = jnp.dot(events[...], w_value_key, preferred_element_type=jnp.float32)
        value_key = jax.nn.silu(value_key).astype(jnp.bfloat16)
        scores = lax.dot_general(
            gate_query[:, DH:], value_key[:, DH:], NT, preferred_element_type=jnp.float32
        ) / math.sqrt(DH)
        weights = jnp.where(valid, jax.nn.silu(scores), 0.0).astype(jnp.bfloat16)
        attended = jnp.dot(weights, value_key[:, :DH], preferred_element_type=jnp.float32)
        inverse = lax.rsqrt(jnp.mean(attended * attended, axis=-1, keepdims=True) + 1e-06)
        store[:, head * DH : (head + 1) * DH] = (
            attended * inverse * gate_query[:, :DH].astype(jnp.float32)
        ).astype(jnp.bfloat16)


def is_early(item, items_axis):
    return item * 4 < items_axis


def attend_kernel(items_axis, limits, events, chosen, w_uvqk, done, gated, rows, sems):
    early = is_early(lax.axis_index("item"), items_axis)

    @pl.when(early)
    def _():
        rows[...] = done[...]

    @pl.when(jnp.logical_not(early))
    def _():
        attention(limits, events, chosen, w_uvqk, rows)

    copies = [pltpu.make_async_copy(rows, gated.at[k], sems.at[k]) for k in range(gated.shape[0])]
    for copy in copies:
        copy.start()
    for copy in copies:
        copy.wait()


def score_kernel(sizes, wanted, gated, *refs):
    items_axis, dps, tensors = sizes
    chosen, refs = refs[:items_axis], refs[items_axis:]
    w_out, refs = refs[:tensors], refs[tensors:]
    catalogue, refs = list(refs[:dps]), refs[dps:]
    state_hbm, sums, hidden, gates, others, sems, state_sem = refs
    fetches = [
        pltpu.make_async_copy(catalogue[d], others.at[d - 1], sems.at[d - 1]) for d in range(1, dps)
    ]
    for fetch in fetches:
        fetch.start()
    catalogue[1:] = [others.at[d - 1] for d in range(1, dps)]
    item, dp, tensor = (lax.axis_index(a) for a in ("item", "dp", "tensor"))
    imps = chosen[0].shape[0]
    items = catalogue[0].shape[0]
    step_rows = min(256, items_axis * imps)
    step_items = min(256, items)
    steps = range(0, items, step_items)
    slot_rounds, tensor_rounds = rounds(items_axis), rounds(tensors)
    local_width = w_out[0].shape[0]
    for k in range(items_axis):
        for t in range(tensors):
            other, head = item ^ slot_rounds[k], tensor ^ tensor_rounds[t]
            sender = rank(other, head, items_axis, (items_axis - 1) // 2)
            gates[k * imps : (k + 1) * imps, t * local_width : (t + 1) * local_width] = gated[sender]
    w_whole = jnp.concatenate([w[...] for w in w_out], axis=0)
    mixed = jnp.dot(gates[...], w_whole, preferred_element_type=jnp.float32)
    for k in range(items_axis):
        rows = slice(k * imps, (k + 1) * imps)
        hidden[rows, :] = (mixed[rows] + chosen[k][...].astype(jnp.float32)).astype(jnp.bfloat16)
    share = state_hbm.shape[1]
    state_copy = pltpu.make_async_copy(
        hidden.at[pl.ds(0, imps), pl.ds(pl.multiple_of(tensor * share, share), share)],
        state_hbm,
        state_sem,
    )
    state_copy.start()

    blocks = range(0, items_axis * imps, step_rows)
    totals = {row: jnp.zeros((8, step_rows), jnp.float32) for row in blocks}
    targets = dict(totals)
    for d in range(dps):
        if d > 0:
            fetches[d - 1].wait()
        item_base = ((item * dps + (dp ^ rounds(dps)[d])) * tensors + tensor) * items
        ids = {row: wanted[0:1, row : row + step_rows] - item_base for row in blocks}
        for first in steps:
            for row in blocks:
                logits = lax.dot_general(
                    catalogue[d][first : first + step_items, :],
                    hidden[row : row + step_rows, :],
                    NT,
                    preferred_element_type=jnp.float32,
                )
                item_ids = lax.broadcasted_iota(jnp.int32, logits.shape, 0)
                found = jnp.where(item_ids == ids[row] - first, logits, 0.0)
                totals[row] += jnp.sum(jnp.exp(logits).reshape(-1, 8, step_rows), axis=0)
                targets[row] += jnp.sum(found.reshape(-1, 8, step_rows), axis=0)
    for row in blocks:
        total = jnp.sum(totals[row], axis=0, keepdims=True)
        target = jnp.sum(targets[row], axis=0, keepdims=True)
        for part in range(step_rows // imps):
            owner = item ^ slot_rounds[row // imps + part]
            both = jnp.concatenate(
                [v[:, part * imps : (part + 1) * imps] for v in (total, target)], axis=1
            )
            for t in range(tensors):
                sums[rank(owner, t, items_axis, items_axis - 1)] = both
    state_copy.wait()


def in_hbm(x):
    return pltpu.with_memory_space_constraint(x, pltpu.HBM)


def rank(item, tensor, items_axis, first):
    tensor = lax.axis_size("tensor") - 1 - tensor
    return tensor * items_axis + (item + items_axis - first) % items_axis


def exchange(x, items_axis, tensors, first):
    group = [0] * (items_axis * tensors)
    for tensor in range(tensors):
        for item in range(items_axis):
            group[rank(item, tensor, items_axis, first)] = tensor * items_axis + item
    return lax.all_to_all(
        x, COLUMN, split_axis=0, concat_axis=0, tiled=True, axis_index_groups=[group]
    )


def send(x, axes, count, r):
    return lax.ppermute(x, axes, [(i, i ^ r) for i in range(count)])


def from_others(x, axes, count):
    pieces = {}
    for r in rounds(count)[1:]:
        if r & 3 == 3:
            held, pieces[r - 2] = lax.optimization_barrier((pieces[r - 1], pieces[r - 2]))
            pieces[r] = send(held, axes, count, 1)
        else:
            pieces[r] = send(x, axes, count, r)
    return list(pieces.values())


def local(events, lengths, packing, positions, logged, w_uvqk, w_out, catalogue):
    rows, width = events.shape
    imps = positions.shape[1]
    hists = packing.shape[0]
    items = catalogue.shape[0]
    local_width = w_out.shape[0]
    items_axis, dps, tensors = (lax.axis_size(a) for a in ("item", "dp", "tensor"))
    receivers = items_axis * tensors
    params = pltpu.CompilerParams(vmem_limit_bytes=(12 + 2 * items_axis) * MIB)
    vmem, hbm = spec(pltpu.VMEM), spec(pltpu.HBM)

    other_catalogues = from_others(catalogue, "dp", dps)
    other_w_out = from_others(w_out, "tensor", tensors)
    chosen, limits, wanted, events, w_uvqk, done = pl.pallas_call(
        functools.partial(pick_kernel, (items_axis, dps)),
        out_shape=(
            jax.ShapeDtypeStruct((imps, width), jnp.bfloat16),
            jax.ShapeDtypeStruct((imps, 128), jnp.int32),
            jax.ShapeDtypeStruct((1, items_axis * imps), jnp.int32),
            jax.ShapeDtypeStruct(events.shape, events.dtype),
            jax.ShapeDtypeStruct(w_uvqk.shape, w_uvqk.dtype),
            jax.ShapeDtypeStruct((imps, local_width), jnp.bfloat16),
        ),
        in_specs=[hbm] * 6,
        out_specs=(vmem,) * 6,
        scratch_shapes=[
            pltpu.SMEM((hists,), jnp.int32),
            pltpu.SMEM((hists,), jnp.int32),
            pltpu.VMEM((hists, imps), jnp.int32),
            pltpu.VMEM((hists, imps), jnp.int32),
            pltpu.SemaphoreType.DMA((5 + EVENT_PARTS,)),
        ],
        compiler_params=params,
        cost_estimate=pl.CostEstimate(
            flops=2 * imps * rows * width, bytes_accessed=2 * rows * width, transcendentals=0
        ),
        name="pick",
    )(*(in_hbm(x) for x in (packing, lengths, positions, logged, events, w_uvqk)))
    other_chosen = from_others(chosen, "item", items_axis)

    gated = pl.pallas_call(
        functools.partial(attend_kernel, items_axis),
        out_shape=pltpu.HBM((receivers, imps, local_width), jnp.bfloat16),
        in_specs=[vmem] * 5,
        out_specs=hbm,
        scratch_shapes=[
            pltpu.VMEM((imps, local_width), jnp.bfloat16),
            pltpu.SemaphoreType.DMA((receivers,)),
        ],
        compiler_params=params,
        cost_estimate=pl.CostEstimate(flops=0, bytes_accessed=0, transcendentals=0),
        name="attend",
    )(limits, events, chosen, w_uvqk, done)
    all_gated = exchange(gated, items_axis, tensors, (items_axis - 1) // 2)

    state, sums = pl.pallas_call(
        functools.partial(score_kernel, (items_axis, dps, tensors)),
        out_shape=(
            jax.ShapeDtypeStruct((imps, width // tensors), jnp.bfloat16),
            jax.ShapeDtypeStruct((receivers, 1, 2 * imps), jnp.float32),
        ),
        in_specs=[vmem] * (3 + items_axis + tensors) + [hbm] * (dps - 1),
        out_specs=(hbm, vmem),
        scratch_shapes=[
            pltpu.VMEM((items_axis * imps, width), jnp.bfloat16),
            pltpu.VMEM((items_axis * imps, local_width * tensors), jnp.bfloat16),
            pltpu.VMEM((dps - 1, items, width), jnp.bfloat16),
            pltpu.SemaphoreType.DMA((dps - 1,)),
            pltpu.SemaphoreType.DMA,
        ],
        compiler_params=params,
        cost_estimate=pl.CostEstimate(
            flops=2 * items_axis * imps * width * (dps * items + local_width * tensors),
            bytes_accessed=2 * dps * items * width,
            transcendentals=items_axis * imps * dps * items,
        ),
        name="score",
    )(
        wanted,
        all_gated,
        chosen,
        *other_chosen,
        w_out,
        *other_w_out,
        catalogue,
        *(in_hbm(x) for x in other_catalogues),
    )
    sums = exchange(sums, items_axis, tensors, items_axis - 1)
    sums = jnp.sum(sums, axis=(0, 1))
    return (state, sums[imps:] - jnp.log(sums[:imps]))


def solution(mesh):
    placed = (
        P(("groups", "item", "dp"), None),
        P("groups"),
        P("groups"),
        P("groups", None),
        P("groups", None),
        P(None, "tensor"),
        P("tensor", None),
        P(("item", "dp", "tensor"), None),
    )
    return jax.shard_map(
        local,
        mesh=mesh,
        in_specs=placed,
        out_specs=(P(("groups", "item", "dp"), "tensor"), P(("groups", "item", "dp"))),
        check_vma=False,
    )
```

```python
import functools
import math

import jax
import jax.numpy as jnp
from jax import lax
from jax.experimental import pallas as pl
from jax.experimental.pallas import tpu as pltpu
from jax.sharding import PartitionSpec as P

DH = 128
SLOTS = ("item", "dp")
COLUMN = ("tensor", "item")
NT = (((1,), (1,)), ((), ()))
MIB = 1024 * 1024
EVENT_PARTS = 6


def rounds(count):
    return [0] + sorted(range(1, count), key=lambda r: (r & 3 == 3, -(r & -2)))


def spec(space):
    return pl.BlockSpec(memory_space=space)


def pick_kernel(
    shards,
    packing,
    lengths,
    positions,
    logged,
    events,
    w_uvqk,
    chosen,
    limits,
    wanted,
    events_v,
    w_uvqk_v,
    done,
    packing_s,
    lengths_s,
    positions_v,
    logged_v,
    sems,
):
    rows = events.shape[0]
    items_axis, dps = shards
    imps = positions.shape[1]
    part_rows = rows // EVENT_PARTS
    parts = [pl.ds(k * part_rows, part_rows) for k in range(EVENT_PARTS)]
    copies = [
        pltpu.make_async_copy(source, target, sems.at[k])
        for k, (source, target) in enumerate(
            [
                (packing, packing_s),
                (positions, positions_v),
                (lengths, lengths_s),
                (logged, logged_v),
            ]
            + [(events.at[part], events_v.at[part]) for part in parts]
            + [(w_uvqk, w_uvqk_v)]
        )
    ]
    for copy in copies:
        copy.start()
    for copy in copies[:4]:
        copy.wait()
    item, dp = lax.axis_index("item"), lax.axis_index("dp")
    history = packing_s[item * dps + dp]
    row = positions_v[pl.ds(history, 1), :].astype(jnp.float32)
    diagonal = lax.broadcasted_iota(jnp.int32, (imps, imps), 0) == lax.broadcasted_iota(
        jnp.int32, (imps, imps), 1
    )
    spots = jnp.sum(jnp.where(diagonal, row, 0.0), axis=1, keepdims=True).astype(jnp.int32)
    limits[...] = jnp.broadcast_to(jnp.minimum(spots, lengths_s[history] - 1), limits.shape)
    for k, r in enumerate(rounds(items_axis)):
        other = packing_s[(item ^ r) * dps + dp]
        wanted[0:1, k * imps : (k + 1) * imps] = logged_v[pl.ds(other, 1), :]
    total = jnp.zeros((imps, events.shape[1]), jnp.float32)
    for k in range(EVENT_PARTS):
        copies[4 + k].wait()
        lanes = k * part_rows + lax.broadcasted_iota(jnp.int32, (imps, part_rows), 1)
        one_hot = jnp.where(lanes == spots, 1.0, 0.0).astype(jnp.bfloat16)
        total += jnp.dot(
            one_hot,
            events_v[k * part_rows : (k + 1) * part_rows, :],
            preferred_element_type=jnp.float32,
        )
    chosen[...] = total.astype(jnp.bfloat16)
    copies[-1].wait()

    @pl.when(is_early(item, items_axis))
    def _():
        attention(limits, events_v, chosen, w_uvqk_v, done)


def attention(limits, events, own, w_uvqk, store):
    lanes = lax.broadcasted_iota(jnp.int32, (own.shape[0], events.shape[0]), 1)
    valid = lanes <= limits[:, 0:1]
    for head in range(w_uvqk.shape[1] // (4 * DH)):
        first = head * 4 * DH
        w_part = [w_uvqk[:, first + k * DH : first + (k + 1) * DH] for k in range(4)]
        w_gate_query = jnp.concatenate([w_part[0], w_part[2]], axis=1)
        w_value_key = jnp.concatenate([w_part[1], w_part[3]], axis=1)
        gate_query = jnp.dot(own[...], w_gate_query, preferred_element_type=jnp.float32)
        gate_query = jax.nn.silu(gate_query).astype(jnp.bfloat16)
        value_key = jnp.dot(events[...], w_value_key, preferred_element_type=jnp.float32)
        value_key = jax.nn.silu(value_key).astype(jnp.bfloat16)
        scores = lax.dot_general(
            gate_query[:, DH:], value_key[:, DH:], NT, preferred_element_type=jnp.float32
        ) / math.sqrt(DH)
        weights = jnp.where(valid, jax.nn.silu(scores), 0.0).astype(jnp.bfloat16)
        attended = jnp.dot(weights, value_key[:, :DH], preferred_element_type=jnp.float32)
        inverse = lax.rsqrt(jnp.mean(attended * attended, axis=-1, keepdims=True) + 1e-06)
        store[:, head * DH : (head + 1) * DH] = (
            attended * inverse * gate_query[:, :DH].astype(jnp.float32)
        ).astype(jnp.bfloat16)


def is_early(item, items_axis):
    return item * 4 < items_axis


def attend_kernel(items_axis, limits, events, chosen, w_uvqk, done, gated, rows, sems):
    early = is_early(lax.axis_index("item"), items_axis)

    @pl.when(early)
    def _():
        rows[...] = done[...]

    @pl.when(jnp.logical_not(early))
    def _():
        attention(limits, events, chosen, w_uvqk, rows)

    copies = [pltpu.make_async_copy(rows, gated.at[k], sems.at[k]) for k in range(gated.shape[0])]
    for copy in copies:
        copy.start()
    for copy in copies:
        copy.wait()


def score_kernel(sizes, wanted, gated, *refs):
    items_axis, dps, tensors = sizes
    chosen, refs = refs[:items_axis], refs[items_axis:]
    w_out, refs = refs[:tensors], refs[tensors:]
    catalogue, refs = list(refs[:dps]), refs[dps:]
    state_hbm, sums, hidden, gates, others, sems, state_sem = refs
    fetches = [
        pltpu.make_async_copy(catalogue[d], others.at[d - 1], sems.at[d - 1]) for d in range(1, dps)
    ]
    for fetch in fetches:
        fetch.start()
    catalogue[1:] = [others.at[d - 1] for d in range(1, dps)]
    item, dp, tensor = (lax.axis_index(a) for a in ("item", "dp", "tensor"))
    imps = chosen[0].shape[0]
    items = catalogue[0].shape[0]
    step_rows = min(256, items_axis * imps)
    step_items = min(256, items)
    steps = range(0, items, step_items)
    slot_rounds, tensor_rounds = rounds(items_axis), rounds(tensors)
    local_width = w_out[0].shape[0]
    for k in range(items_axis):
        for t in range(tensors):
            other, head = item ^ slot_rounds[k], tensor ^ tensor_rounds[t]
            sender = rank(other, head, items_axis, items_axis // 2)
            gates[k * imps : (k + 1) * imps, t * local_width : (t + 1) * local_width] = gated[sender]
    w_whole = jnp.concatenate([w[...] for w in w_out], axis=0)
    mixed = jnp.dot(gates[...], w_whole, preferred_element_type=jnp.float32)
    for k in range(items_axis):
        rows = slice(k * imps, (k + 1) * imps)
        hidden[rows, :] = (mixed[rows] + chosen[k][...].astype(jnp.float32)).astype(jnp.bfloat16)
    share = state_hbm.shape[1]
    state_copy = pltpu.make_async_copy(
        hidden.at[pl.ds(0, imps), pl.ds(pl.multiple_of(tensor * share, share), share)],
        state_hbm,
        state_sem,
    )
    state_copy.start()

    blocks = range(0, items_axis * imps, step_rows)
    totals = {row: jnp.zeros((8, step_rows), jnp.float32) for row in blocks}
    targets = dict(totals)
    for d in range(dps):
        if d > 0:
            fetches[d - 1].wait()
        item_base = ((item * dps + (dp ^ rounds(dps)[d])) * tensors + tensor) * items
        ids = {row: wanted[0:1, row : row + step_rows] - item_base for row in blocks}
        for first in steps:
            for row in blocks:
                logits = lax.dot_general(
                    catalogue[d][first : first + step_items, :],
                    hidden[row : row + step_rows, :],
                    NT,
                    preferred_element_type=jnp.float32,
                )
                item_ids = lax.broadcasted_iota(jnp.int32, logits.shape, 0)
                found = jnp.where(item_ids == ids[row] - first, logits, 0.0)
                totals[row] += jnp.sum(jnp.exp(logits).reshape(-1, 8, step_rows), axis=0)
                targets[row] += jnp.sum(found.reshape(-1, 8, step_rows), axis=0)
    for row in blocks:
        total = jnp.sum(totals[row], axis=0, keepdims=True)
        target = jnp.sum(targets[row], axis=0, keepdims=True)
        for part in range(step_rows // imps):
            owner = item ^ slot_rounds[row // imps + part]
            both = jnp.concatenate(
                [v[:, part * imps : (part + 1) * imps] for v in (total, target)], axis=1
            )
            for t in range(tensors):
                sums[rank(owner, t, items_axis, items_axis - 1)] = both
    state_copy.wait()


def in_hbm(x):
    return pltpu.with_memory_space_constraint(x, pltpu.HBM)


def rank(item, tensor, items_axis, first):
    tensor = lax.axis_size("tensor") - 1 - tensor
    return tensor * items_axis + ((item + items_axis - first) & (items_axis - 1))


def exchange(x, items_axis, tensors, first):
    group = [0] * (items_axis * tensors)
    for tensor in range(tensors):
        for item in range(items_axis):
            group[rank(item, tensor, items_axis, first)] = tensor * items_axis + item
    return lax.all_to_all(
        x, COLUMN, split_axis=0, concat_axis=0, tiled=True, axis_index_groups=[group]
    )


def send(x, axes, count, r):
    return lax.ppermute(x, axes, [(i, i ^ r) for i in range(count)])


def from_others(x, axes, count):
    pieces = {}
    for r in rounds(count)[1:]:
        if r & 3 == 3:
            held, pieces[r - 2] = lax.optimization_barrier((pieces[r - 1], pieces[r - 2]))
            pieces[r] = send(held, axes, count, 1)
        else:
            pieces[r] = send(x, axes, count, r)
    return list(pieces.values())


def local(events, lengths, packing, positions, logged, w_uvqk, w_out, catalogue):
    rows, width = events.shape
    imps = positions.shape[1]
    hists = packing.shape[0]
    items = catalogue.shape[0]
    local_width = w_out.shape[0]
    items_axis, dps, tensors = (lax.axis_size(a) for a in ("item", "dp", "tensor"))
    receivers = items_axis * tensors
    params = pltpu.CompilerParams(vmem_limit_bytes=(12 + 2 * items_axis) * MIB)
    vmem, hbm = spec(pltpu.VMEM), spec(pltpu.HBM)

    other_catalogues = from_others(catalogue, "dp", dps)
    other_w_out = from_others(w_out, "tensor", tensors)
    chosen, limits, wanted, events, w_uvqk, done = pl.pallas_call(
        functools.partial(pick_kernel, (items_axis, dps)),
        out_shape=(
            jax.ShapeDtypeStruct((imps, width), jnp.bfloat16),
            jax.ShapeDtypeStruct((imps, 128), jnp.int32),
            jax.ShapeDtypeStruct((1, items_axis * imps), jnp.int32),
            jax.ShapeDtypeStruct(events.shape, events.dtype),
            jax.ShapeDtypeStruct(w_uvqk.shape, w_uvqk.dtype),
            jax.ShapeDtypeStruct((imps, local_width), jnp.bfloat16),
        ),
        in_specs=[hbm] * 6,
        out_specs=(vmem,) * 6,
        scratch_shapes=[
            pltpu.SMEM((hists,), jnp.int32),
            pltpu.SMEM((hists,), jnp.int32),
            pltpu.VMEM((hists, imps), jnp.int32),
            pltpu.VMEM((hists, imps), jnp.int32),
            pltpu.SemaphoreType.DMA((5 + EVENT_PARTS,)),
        ],
        compiler_params=params,
        cost_estimate=pl.CostEstimate(
            flops=2 * imps * rows * width, bytes_accessed=2 * rows * width, transcendentals=0
        ),
        name="pick",
    )(*(in_hbm(x) for x in (packing, lengths, positions, logged, events, w_uvqk)))
    other_chosen = from_others(chosen, "item", items_axis)

    gated = pl.pallas_call(
        functools.partial(attend_kernel, items_axis),
        out_shape=pltpu.HBM((receivers, imps, local_width), jnp.bfloat16),
        in_specs=[vmem] * 5,
        out_specs=hbm,
        scratch_shapes=[
            pltpu.VMEM((imps, local_width), jnp.bfloat16),
            pltpu.SemaphoreType.DMA((receivers,)),
        ],
        compiler_params=params,
        cost_estimate=pl.CostEstimate(flops=0, bytes_accessed=0, transcendentals=0),
        name="attend",
    )(limits, events, chosen, w_uvqk, done)
    all_gated = exchange(gated, items_axis, tensors, items_axis // 2)

    state, sums = pl.pallas_call(
        functools.partial(score_kernel, (items_axis, dps, tensors)),
        out_shape=(
            jax.ShapeDtypeStruct((imps, width // tensors), jnp.bfloat16),
            jax.ShapeDtypeStruct((receivers, 1, 2 * imps), jnp.float32),
        ),
        in_specs=[vmem] * (3 + items_axis + tensors) + [hbm] * (dps - 1),
        out_specs=(hbm, vmem),
        scratch_shapes=[
            pltpu.VMEM((items_axis * imps, width), jnp.bfloat16),
            pltpu.VMEM((items_axis * imps, local_width * tensors), jnp.bfloat16),
            pltpu.VMEM((dps - 1, items, width), jnp.bfloat16),
            pltpu.SemaphoreType.DMA((dps - 1,)),
            pltpu.SemaphoreType.DMA,
        ],
        compiler_params=params,
        cost_estimate=pl.CostEstimate(
            flops=2 * items_axis * imps * width * (dps * items + local_width * tensors),
            bytes_accessed=2 * dps * items * width,
            transcendentals=items_axis * imps * dps * items,
        ),
        name="score",
    )(
        wanted,
        all_gated,
        chosen,
        *other_chosen,
        w_out,
        *other_w_out,
        catalogue,
        *(in_hbm(x) for x in other_catalogues),
    )
    sums = exchange(sums, items_axis, tensors, items_axis - 1)
    sums = jnp.sum(sums, axis=(0, 1))
    return (state, sums[imps:] - jnp.log(sums[:imps]))


def solution(mesh):
    placed = (
        P(("groups", "item", "dp"), None),
        P("groups"),
        P("groups"),
        P("groups", None),
        P("groups", None),
        P(None, "tensor"),
        P("tensor", None),
        P(("item", "dp", "tensor"), None),
    )
    return jax.shard_map(
        local,
        mesh=mesh,
        in_specs=placed,
        out_specs=(P(("groups", "item", "dp"), "tensor"), P(("groups", "item", "dp"))),
        check_vma=False,
    )
```

```python
import functools
import math

import jax
import jax.numpy as jnp
from jax import lax
from jax.experimental import pallas as pl
from jax.experimental.pallas import tpu as pltpu
from jax.sharding import PartitionSpec as P

DH = 128
SLOTS = ("item", "dp")
COLUMN = ("tensor", "item")
NT = (((1,), (1,)), ((), ()))
MIB = 1024 * 1024
EVENT_PARTS = 3


def rounds(count):
    return [0] + sorted(range(1, count), key=lambda r: (r & 3 == 3, -(r & -2)))


def spec(space):
    return pl.BlockSpec(memory_space=space)


def pick_kernel(
    shards,
    packing,
    lengths,
    positions,
    logged,
    events,
    w_uvqk,
    chosen,
    limits,
    wanted,
    events_v,
    w_uvqk_v,
    done,
    packing_s,
    lengths_s,
    positions_v,
    logged_v,
    sems,
):
    rows = events.shape[0]
    items_axis, dps = shards
    imps = positions.shape[1]
    part_rows = rows // EVENT_PARTS
    parts = [pl.ds(k * part_rows, part_rows) for k in range(EVENT_PARTS)]
    copies = [
        pltpu.make_async_copy(source, target, sems.at[k])
        for k, (source, target) in enumerate(
            [
                (packing, packing_s),
                (positions, positions_v),
                (lengths, lengths_s),
                (logged, logged_v),
            ]
            + [(events.at[part], events_v.at[part]) for part in parts]
            + [(w_uvqk, w_uvqk_v)]
        )
    ]
    for copy in copies:
        copy.start()
    for copy in copies[:4]:
        copy.wait()
    item, dp = lax.axis_index("item"), lax.axis_index("dp")
    history = packing_s[item * dps + dp]
    row = positions_v[pl.ds(history, 1), :].astype(jnp.float32)
    diagonal = lax.broadcasted_iota(jnp.int32, (imps, imps), 0) == lax.broadcasted_iota(
        jnp.int32, (imps, imps), 1
    )
    spots = jnp.sum(jnp.where(diagonal, row, 0.0), axis=1, keepdims=True).astype(jnp.int32)
    limits[...] = jnp.broadcast_to(jnp.minimum(spots, lengths_s[history] - 1), limits.shape)
    for k, r in enumerate(rounds(items_axis)):
        other = packing_s[(item ^ r) * dps + dp]
        wanted[0:1, k * imps : (k + 1) * imps] = logged_v[pl.ds(other, 1), :]
    total = jnp.zeros((imps, events.shape[1]), jnp.float32)
    for k in range(EVENT_PARTS):
        copies[4 + k].wait()
        lanes = k * part_rows + lax.broadcasted_iota(jnp.int32, (imps, part_rows), 1)
        one_hot = jnp.where(lanes == spots, 1.0, 0.0).astype(jnp.bfloat16)
        total += jnp.dot(
            one_hot,
            events_v[k * part_rows : (k + 1) * part_rows, :],
            preferred_element_type=jnp.float32,
        )
    chosen[...] = total.astype(jnp.bfloat16)
    copies[-1].wait()

    @pl.when(is_early(item, items_axis))
    def _():
        attention(limits, events_v, chosen, w_uvqk_v, done)


def attention(limits, events, own, w_uvqk, store):
    lanes = lax.broadcasted_iota(jnp.int32, (own.shape[0], events.shape[0]), 1)
    valid = lanes <= limits[:, 0:1]
    for head in range(w_uvqk.shape[1] // (4 * DH)):
        first = head * 4 * DH
        w_part = [w_uvqk[:, first + k * DH : first + (k + 1) * DH] for k in range(4)]
        w_gate_query = jnp.concatenate([w_part[0], w_part[2]], axis=1)
        w_value_key = jnp.concatenate([w_part[1], w_part[3]], axis=1)
        gate_query = jnp.dot(own[...], w_gate_query, preferred_element_type=jnp.float32)
        gate_query = jax.nn.silu(gate_query).astype(jnp.bfloat16)
        value_key = jnp.dot(events[...], w_value_key, preferred_element_type=jnp.float32)
        value_key = jax.nn.silu(value_key).astype(jnp.bfloat16)
        scores = lax.dot_general(
            gate_query[:, DH:], value_key[:, DH:], NT, preferred_element_type=jnp.float32
        ) / math.sqrt(DH)
        weights = jnp.where(valid, jax.nn.silu(scores), 0.0).astype(jnp.bfloat16)
        attended = jnp.dot(weights, value_key[:, :DH], preferred_element_type=jnp.float32)
        inverse = lax.rsqrt(jnp.mean(attended * attended, axis=-1, keepdims=True) + 1e-06)
        store[:, head * DH : (head + 1) * DH] = (
            attended * inverse * gate_query[:, :DH].astype(jnp.float32)
        ).astype(jnp.bfloat16)


def is_early(item, items_axis):
    return item * 4 < items_axis


def attend_kernel(items_axis, limits, events, chosen, w_uvqk, done, gated, rows, sems):
    early = is_early(lax.axis_index("item"), items_axis)

    @pl.when(early)
    def _():
        rows[...] = done[...]

    @pl.when(jnp.logical_not(early))
    def _():
        attention(limits, events, chosen, w_uvqk, rows)

    copies = [pltpu.make_async_copy(rows, gated.at[k], sems.at[k]) for k in range(gated.shape[0])]
    for copy in copies:
        copy.start()
    for copy in copies:
        copy.wait()


def score_kernel(sizes, wanted, gated, *refs):
    items_axis, dps, tensors = sizes
    chosen, refs = refs[:items_axis], refs[items_axis:]
    w_out, refs = refs[:tensors], refs[tensors:]
    catalogue, refs = list(refs[:dps]), refs[dps:]
    state_hbm, sums, hidden, gates, others, sems, state_sem = refs
    fetches = [
        pltpu.make_async_copy(catalogue[d], others.at[d - 1], sems.at[d - 1]) for d in range(1, dps)
    ]
    for fetch in fetches:
        fetch.start()
    catalogue[1:] = [others.at[d - 1] for d in range(1, dps)]
    item, dp, tensor = (lax.axis_index(a) for a in ("item", "dp", "tensor"))
    imps = chosen[0].shape[0]
    items = catalogue[0].shape[0]
    step_rows = min(256, items_axis * imps)
    step_items = min(256, items)
    steps = range(0, items, step_items)
    slot_rounds, tensor_rounds = rounds(items_axis), rounds(tensors)
    local_width = w_out[0].shape[0]
    for k in range(items_axis):
        for t in range(tensors):
            other, head = item ^ slot_rounds[k], tensor ^ tensor_rounds[t]
            sender = rank(other, head, items_axis, items_axis // 2)
            gates[k * imps : (k + 1) * imps, t * local_width : (t + 1) * local_width] = gated[sender]
    w_whole = jnp.concatenate([w[...] for w in w_out], axis=0)
    mixed = jnp.dot(gates[...], w_whole, preferred_element_type=jnp.float32)
    for k in range(items_axis):
        rows = slice(k * imps, (k + 1) * imps)
        hidden[rows, :] = (mixed[rows] + chosen[k][...].astype(jnp.float32)).astype(jnp.bfloat16)
    share = state_hbm.shape[1]
    state_copy = pltpu.make_async_copy(
        hidden.at[pl.ds(0, imps), pl.ds(pl.multiple_of(tensor * share, share), share)],
        state_hbm,
        state_sem,
    )
    state_copy.start()

    blocks = range(0, items_axis * imps, step_rows)
    totals = {row: jnp.zeros((8, step_rows), jnp.float32) for row in blocks}
    targets = dict(totals)
    for d in range(dps):
        if d > 0:
            fetches[d - 1].wait()
        item_base = ((item * dps + (dp ^ rounds(dps)[d])) * tensors + tensor) * items
        ids = {row: wanted[0:1, row : row + step_rows] - item_base for row in blocks}
        for first in steps:
            for row in blocks:
                logits = lax.dot_general(
                    catalogue[d][first : first + step_items, :],
                    hidden[row : row + step_rows, :],
                    NT,
                    preferred_element_type=jnp.float32,
                )
                item_ids = lax.broadcasted_iota(jnp.int32, logits.shape, 0)
                found = jnp.where(item_ids == ids[row] - first, logits, 0.0)
                totals[row] += jnp.sum(jnp.exp(logits).reshape(-1, 8, step_rows), axis=0)
                targets[row] += jnp.sum(found.reshape(-1, 8, step_rows), axis=0)
    for row in blocks:
        total = jnp.sum(totals[row], axis=0, keepdims=True)
        target = jnp.sum(targets[row], axis=0, keepdims=True)
        for part in range(step_rows // imps):
            owner = item ^ slot_rounds[row // imps + part]
            both = jnp.concatenate(
                [v[:, part * imps : (part + 1) * imps] for v in (total, target)], axis=1
            )
            for t in range(tensors):
                sums[rank(owner, tensors - 1 - t, items_axis, items_axis - 1)] = both
    state_copy.wait()


def in_hbm(x):
    return pltpu.with_memory_space_constraint(x, pltpu.HBM)


def rank(item, tensor, items_axis, first):
    return tensor * items_axis + (item + items_axis - first) % items_axis


def exchange(x, items_axis, tensors, first, last_tensor_leads):
    group = [0] * (items_axis * tensors)
    for tensor in range(tensors):
        for item in range(items_axis):
            place = tensors - 1 - tensor if last_tensor_leads else tensor
            group[rank(item, place, items_axis, first)] = tensor * items_axis + item
    return lax.all_to_all(
        x, COLUMN, split_axis=0, concat_axis=0, tiled=True, axis_index_groups=[group]
    )


def send(x, axes, count, r):
    return lax.ppermute(x, axes, [(i, i ^ r) for i in range(count)])


def from_others(x, axes, count):
    pieces = {}
    for r in rounds(count)[1:]:
        if r & 3 == 3:
            held, pieces[r - 2] = lax.optimization_barrier((pieces[r - 1], pieces[r - 2]))
            pieces[r] = send(held, axes, count, 1)
        else:
            pieces[r] = send(x, axes, count, r)
    return list(pieces.values())


def local(events, lengths, packing, positions, logged, w_uvqk, w_out, catalogue):
    rows, width = events.shape
    imps = positions.shape[1]
    hists = packing.shape[0]
    items = catalogue.shape[0]
    local_width = w_out.shape[0]
    items_axis, dps, tensors = (lax.axis_size(a) for a in ("item", "dp", "tensor"))
    receivers = items_axis * tensors
    params = pltpu.CompilerParams(vmem_limit_bytes=(12 + 2 * items_axis) * MIB)
    vmem, hbm = spec(pltpu.VMEM), spec(pltpu.HBM)

    other_catalogues = from_others(catalogue, "dp", dps)
    other_w_out = from_others(w_out, "tensor", tensors)
    chosen, limits, wanted, events, w_uvqk, done = pl.pallas_call(
        functools.partial(pick_kernel, (items_axis, dps)),
        out_shape=(
            jax.ShapeDtypeStruct((imps, width), jnp.bfloat16),
            jax.ShapeDtypeStruct((imps, 128), jnp.int32),
            jax.ShapeDtypeStruct((1, items_axis * imps), jnp.int32),
            jax.ShapeDtypeStruct(events.shape, events.dtype),
            jax.ShapeDtypeStruct(w_uvqk.shape, w_uvqk.dtype),
            jax.ShapeDtypeStruct((imps, local_width), jnp.bfloat16),
        ),
        in_specs=[hbm] * 6,
        out_specs=(vmem,) * 6,
        scratch_shapes=[
            pltpu.SMEM((hists,), jnp.int32),
            pltpu.SMEM((hists,), jnp.int32),
            pltpu.VMEM((hists, imps), jnp.int32),
            pltpu.VMEM((hists, imps), jnp.int32),
            pltpu.SemaphoreType.DMA((5 + EVENT_PARTS,)),
        ],
        compiler_params=params,
        cost_estimate=pl.CostEstimate(
            flops=2 * imps * rows * width, bytes_accessed=2 * rows * width, transcendentals=0
        ),
        name="pick",
    )(*(in_hbm(x) for x in (packing, lengths, positions, logged, events, w_uvqk)))
    other_chosen = from_others(chosen, "item", items_axis)

    gated = pl.pallas_call(
        functools.partial(attend_kernel, items_axis),
        out_shape=pltpu.HBM((receivers, imps, local_width), jnp.bfloat16),
        in_specs=[vmem] * 5,
        out_specs=hbm,
        scratch_shapes=[
            pltpu.VMEM((imps, local_width), jnp.bfloat16),
            pltpu.SemaphoreType.DMA((receivers,)),
        ],
        compiler_params=params,
        cost_estimate=pl.CostEstimate(flops=0, bytes_accessed=0, transcendentals=0),
        name="attend",
    )(limits, events, chosen, w_uvqk, done)
    all_gated = exchange(gated, items_axis, tensors, items_axis // 2, False)

    state, sums = pl.pallas_call(
        functools.partial(score_kernel, (items_axis, dps, tensors)),
        out_shape=(
            jax.ShapeDtypeStruct((imps, width // tensors), jnp.bfloat16),
            jax.ShapeDtypeStruct((receivers, 1, 2 * imps), jnp.float32),
        ),
        in_specs=[vmem] * (3 + items_axis + tensors) + [hbm] * (dps - 1),
        out_specs=(hbm, vmem),
        scratch_shapes=[
            pltpu.VMEM((items_axis * imps, width), jnp.bfloat16),
            pltpu.VMEM((items_axis * imps, local_width * tensors), jnp.bfloat16),
            pltpu.VMEM((dps - 1, items, width), jnp.bfloat16),
            pltpu.SemaphoreType.DMA((dps - 1,)),
            pltpu.SemaphoreType.DMA,
        ],
        compiler_params=params,
        cost_estimate=pl.CostEstimate(
            flops=2 * items_axis * imps * width * (dps * items + local_width * tensors),
            bytes_accessed=2 * dps * items * width,
            transcendentals=items_axis * imps * dps * items,
        ),
        name="score",
    )(
        wanted,
        all_gated,
        chosen,
        *other_chosen,
        w_out,
        *other_w_out,
        catalogue,
        *(in_hbm(x) for x in other_catalogues),
    )
    sums = exchange(sums, items_axis, tensors, items_axis - 1, True)
    sums = jnp.sum(sums, axis=(0, 1))
    return (state, sums[imps:] - jnp.log(sums[:imps]))


def solution(mesh):
    placed = (
        P(("groups", "item", "dp"), None),
        P("groups"),
        P("groups"),
        P("groups", None),
        P("groups", None),
        P(None, "tensor"),
        P("tensor", None),
        P(("item", "dp", "tensor"), None),
    )
    return jax.shard_map(
        local,
        mesh=mesh,
        in_specs=placed,
        out_specs=(P(("groups", "item", "dp"), "tensor"), P(("groups", "item", "dp"))),
        check_vma=False,
    )
```
